32 devices in a mesh: gz: 8 (over z, x), gx: 4 (over y, core).
Axes of the slice: x: 2, y: 2, z: 4, core: 2. Of those that a mesh axis runs over, the one named last changes fastest.
Arguments:
- velocity: float32 [64, 512, 512], P('gz', 'gx'), may hold values from -8 to 8
Outputs:
- detail_one: float32 [7, 32, 256, 256], P(None, 'gz', 'gx')
- detail_two: float32 [7, 16, 128, 128], P(None, 'gz', 'gx')
- detail_three: float32 [7, 8, 64, 64], P(None, 'gz', 'gx')
- coarse: float32 [8, 64, 64], P('gz', 'gx')
The draws below stay inside these ranges and needn't reach their ends.
All inputs are finite; a program needn't handle non-finite values.
Results may differ from the reference program's by a relative error of at most 0.00002.
Values sent between devices are 32-bit elements; how exact they have to be, the bound alone decides.
No kernel may reach another device: no remote copies, remote signals or barrier semaphores. Data moves between devices by JAX's collectives and lax.ppermute only.
A program may use at most 64 MiB of HBM per device.

```python
import jax
import jax.numpy as jnp
from jax import lax

NX = 512
NY = 512
LEVELS = 3
NZ = 64


def block_scale(key, dims, pieces, low, top_value):
    level = 1.0
    for position, blocks in pieces:
        heights = jax.random.uniform(jax.random.fold_in(jax.random.fold_in(key, 6), position), (blocks,), jnp.float32, low / len(pieces), top_value / len(pieces))
        level = level * jnp.repeat(jnp.exp(heights), dims[position] // blocks).reshape((-1,) + (1,) * (len(dims) - 1 - position))
    return level


def scatter_about(rng, extent, deviation, limit, cuts=(), held_as=jnp.bfloat16):
    result = jax.random.normal(rng, extent, jnp.float32) * deviation
    if len(cuts) > 0:
        result = block_scale(rng, extent, cuts, -0.22, 0.18) * result
    return jnp.clip(result, min=-limit, max=limit).astype(held_as)


def setup_inputs(seed: int = 0) -> dict:
    seeds = jax.random.split(jax.random.key(seed), 2)
    return {
        "velocity": scatter_about(seeds[0], (NZ, NX, NY), 1.0, 8.0, ((0, 8), (1, 4)), jnp.float32),
    }


LOW_TAPS = (0.026748757411, -0.016864118443, -0.078223266529, 0.266864118443, 0.602949018236, 0.266864118443, -0.078223266529, -0.016864118443, 0.026748757411)
HIGH_TAPS = (0.091271763114, -0.057543526229, -0.591271763114, 1.115087052457, -0.591271763114, -0.057543526229, 0.091271763114)


def wrap_extend(field, along):
    count = field.shape[along]
    return jnp.concatenate([lax.slice_in_dim(field, count - 4, count, axis=along), field, lax.slice_in_dim(field, 0, 3, axis=along)], along)


def split_bands(extended, along, length):
    widths = [(0, 0)] * extended.ndim
    widths[along] = (0, 1)
    padded = jnp.pad(extended, widths)
    half = length // 2
    shape = padded.shape[:along] + (half + 4, 2) + padded.shape[along + 1:]
    phases = padded.reshape(shape)
    even_part = lax.index_in_dim(phases, 0, along + 1, keepdims=False)
    odd_part = lax.index_in_dim(phases, 1, along + 1, keepdims=False)
    low_band = jnp.zeros_like(lax.slice_in_dim(even_part, 0, half, axis=along))
    high_band = jnp.zeros_like(low_band)
    for offset in range(9):
        source = even_part if offset % 2 == 0 else odd_part
        start = offset // 2
        taken = lax.slice_in_dim(source, start, start + half, axis=along)
        low_band = low_band + LOW_TAPS[offset] * taken
        if offset >= 2:
            high_band = high_band + HIGH_TAPS[offset - 2] * taken
    return jnp.stack([low_band, high_band], 0)


def one_level(field):
    zbands = split_bands(wrap_extend(field, 0), 0, field.shape[0])
    xbands = split_bands(wrap_extend(zbands, 2), 2, field.shape[1])
    ybands = split_bands(wrap_extend(xbands, 4), 4, field.shape[2])
    return ybands.reshape((8,) + ybands.shape[3:])


def reference(velocity):
    approx = velocity.astype(jnp.float32)
    details = []
    for level_number in range(LEVELS):
        bands = one_level(approx)
        details.append(bands[1:])
        approx = bands[0]
    return details[0], details[1], details[2], approx
```

```python
import functools

import jax
import jax.numpy as jnp
import numpy as np
from jax import lax
from jax.experimental import pallas as pl
from jax.experimental.pallas import tpu as pltpu
from jax.sharding import PartitionSpec as P

LEVELS = 3
LANES = 128

LOW_TAPS = (
    0.026748757411,
    -0.016864118443,
    -0.078223266529,
    0.266864118443,
    0.602949018236,
    0.266864118443,
    -0.078223266529,
    -0.016864118443,
    0.026748757411,
)
HIGH_TAPS = (
    0.091271763114,
    -0.057543526229,
    -0.591271763114,
    1.115087052457,
    -0.591271763114,
    -0.057543526229,
    0.091271763114,
)

ALPHA = -1.586134342059924
BETA = -0.052980118572961
GAMMA = 0.882911075530934
DELTA = 0.443506852043971
LOW_SCALE = 0.812893066115961
HIGH_SCALE = 1.230174104914001


def shifted(value, axis, steps):
    count = lax.axis_size(axis)
    pairs = [(source, (source + steps) % count) for source in range(count)]
    return lax.ppermute(value, axis, pairs)


def band_matrix(length):
    half = length // 2
    matrix = np.zeros((length, length), np.float64)
    for j in range(half):
        for k in range(-4, 5):
            matrix[(2 * j + k) % length, j] += LOW_TAPS[k + 4]
        for k in range(-3, 4):
            matrix[(2 * j + 1 + k) % length, half + j] += HIGH_TAPS[k + 3]
    return matrix


def three_parts(matrix):
    parts = []
    rest = matrix
    for _ in range(3):
        part = rest.astype(np.float32).astype(jnp.bfloat16)
        parts.append(part)
        rest = rest - part.astype(np.float64)
    return np.stack(parts)


def exact_dot(value, parts):
    first = value.astype(jnp.bfloat16)
    rest = value - first.astype(jnp.float32)
    second = rest.astype(jnp.bfloat16)
    third = (rest - second.astype(jnp.float32)).astype(jnp.bfloat16)

    def dot(a, b):
        return jnp.dot(a, b, preferred_element_type=jnp.float32)

    small = dot(third, parts[0]) + dot(second, parts[1]) + dot(first, parts[2])
    middle = dot(second, parts[0]) + dot(first, parts[1])
    return dot(first, parts[0]) + (middle + small)


def lift_rows(even, odd):
    count = even.shape[0]

    def after(a):
        return pltpu.roll(a, count - 1, 0)

    def before(a):
        return pltpu.roll(a, 1, 0)

    odd = odd + ALPHA * (even + after(even))
    even = even + BETA * (before(odd) + odd)
    odd = odd + GAMMA * (even + after(even))
    even = even + DELTA * (before(odd) + odd)
    return even * LOW_SCALE, odd * HIGH_SCALE


def rim_sums(planes):
    even, odd = planes[0::2], planes[1::2]
    up_odd = odd[-1] + ALPHA * even[-1]
    up_even = even[-1] + BETA * (odd[-2] + ALPHA * (even[-2] + even[-1]))
    down_even = even[0] + BETA * (odd[0] + ALPHA * (even[0] + even[1]))
    return (up_odd, up_even), (even[0], down_even)


def lift_planes(planes, below, above):
    even, odd = planes[0::2], planes[1::2]
    count = len(even)
    first_odd = below[0] + ALPHA * even[0]
    odd = [
        odd[i] + ALPHA * (even[i] + (even[i + 1] if i + 1 < count else above[0]))
        for i in range(count)
    ]
    first_even = below[1] + BETA * first_odd
    even = [
        even[i] + BETA * ((odd[i - 1] if i else first_odd) + odd[i])
        for i in range(count)
    ]
    last_even = above[1] + BETA * odd[-1]
    first_odd = first_odd + GAMMA * (first_even + even[0])
    odd = [
        odd[i] + GAMMA * (even[i] + (even[i + 1] if i + 1 < count else last_even))
        for i in range(count)
    ]
    even = [
        even[i] + DELTA * ((odd[i - 1] if i else first_odd) + odd[i])
        for i in range(count)
    ]
    return [e * LOW_SCALE for e in even], [o * HIGH_SCALE for o in odd]


def lift_pair(pair, below, far_below, above, far_above):
    even, odd = pair
    odd_far = far_below + ALPHA * below[0]
    odd_below = below[1] + ALPHA * (below[0] + even)
    odd = odd + ALPHA * (even + above[0])
    odd_above = above[1] + ALPHA * (above[0] + far_above)
    even_below = below[0] + BETA * (odd_far + odd_below)
    even = even + BETA * (odd_below + odd)
    even_above = above[0] + BETA * (odd + odd_above)
    odd_below = odd_below + GAMMA * (even_below + even)
    odd = odd + GAMMA * (even + even_above)
    even = even + DELTA * (odd_below + odd)
    return even * LOW_SCALE, odd * HIGH_SCALE


def chunk_of(rows):
    for size in (16, 8):
        if rows % size == 0:
            return size
    return rows


def over_rows(rows, body):
    size = chunk_of(rows)

    def step(i, carry):
        body(pl.ds(pl.multiple_of(i * size, size), size))
        return carry

    lax.fori_loop(0, rows // size, step, 0)


def spread_rims(source, up_ref, down_ref, rows):
    planes = source.shape[0]

    def body(at):
        up, down = rim_sums([source[z, at, :] for z in range(planes)])
        for k in range(2):
            up_ref[k, at, :] = up[k]
            down_ref[k, at, :] = down[k]

    over_rows(rows, body)


def y_low_kernel(v_ref, w_ref, y_ref, up_ref, down_ref):
    def step(z, carry):
        y_ref[z] = exact_dot(v_ref[z], w_ref)
        return carry

    lax.fori_loop(0, v_ref.shape[0], step, 0)
    spread_rims(y_ref, up_ref, down_ref, y_ref.shape[1])


def y_high_kernel(v_ref, w_ref, y_ref, up_ref, down_ref):
    rows = v_ref.shape[1]

    def step(z, carry):
        y = exact_dot(v_ref[z], w_ref)
        y_ref[z] = y
        up_ref[z] = y[rows - 8 :]
        down_ref[z] = y[:8]
        return carry

    lax.fori_loop(0, v_ref.shape[0], step, 0)


def lift_in_scratch(scratch, pairs):
    even = scratch[pl.ds(0, pairs, stride=2), :]
    odd = scratch[pl.ds(1, pairs, stride=2), :]
    return lift_rows(even, odd)


def lane_tiles(width):
    size = min(width, LANES)
    return [pl.ds(k, size) for k in range(0, width, size)]


def x_high_kernel(y_ref, below_ref, above_ref, x_ref, up_ref, down_ref, scratch):
    planes, rows, width = y_ref.shape
    half = rows // 2

    def step(z, carry):
        for tile, lanes in enumerate(lane_tiles(width)):
            part = scratch.at[tile]
            part[8:16] = below_ref[z, :, lanes]
            part[16 : 16 + rows] = y_ref[z, :, lanes]
            part[16 + rows : 24 + rows] = above_ref[z, :, lanes]
            low, high = lift_in_scratch(part, half + 16)
            x_ref[z, 0:half, lanes] = low[8 : 8 + half]
            x_ref[z, half:rows, lanes] = high[8 : 8 + half]
        return carry

    scratch[:, 0:8] = jnp.zeros_like(scratch[:, 0:8])
    scratch[:, 24 + rows :] = jnp.zeros_like(scratch[:, 24 + rows :])
    lax.fori_loop(0, planes, step, 0)
    spread_rims(x_ref, up_ref, down_ref, rows)


LOW_BELOW, LOW_ABOVE = 32, 24


def z_low_kernel(y_ref, below_ref, above_ref, low_ref, high_ref, up_ref, down_ref):
    planes, rows, _ = y_ref.shape

    def body(at):
        low, high = lift_planes(
            [y_ref[z, at, :] for z in range(planes)],
            [below_ref[k, at, :] for k in range(2)],
            [above_ref[k, at, :] for k in range(2)],
        )
        for z in range(planes // 2):
            low_ref[z, at, :] = low[z]
            high_ref[z, at, :] = high[z]

    over_rows(rows, body)
    up_ref[:, 0:LOW_BELOW, :] = low_ref[:, rows - LOW_BELOW : rows, :]
    up_ref[:, LOW_BELOW : LOW_BELOW + 8, :] = high_ref[:, rows - 8 : rows, :]
    down_ref[:, 0:LOW_ABOVE, :] = low_ref[:, 0:LOW_ABOVE, :]
    down_ref[:, LOW_ABOVE : LOW_ABOVE + 8, :] = high_ref[:, 0:8, :]


def x_low_kernel(
    low_ref, high_ref, below_ref, above_ref, w_ref,
    detail_ref, bands_ref, up_ref, down_ref,
    scratch, approx, split, held, sem,
):
    planes, rows, width = low_ref.shape
    half = rows // 2
    deep = (rows + 64) // 2
    quarter = half // 2

    def step(z, carry):
        for tile, lanes in enumerate(lane_tiles(width)):
            part = scratch.at[tile]
            part[0:LOW_BELOW] = below_ref[z, 0:LOW_BELOW, lanes]
            part[LOW_BELOW : LOW_BELOW + rows] = low_ref[z, :, lanes]
            top = LOW_BELOW + rows
            part[top : top + LOW_ABOVE] = above_ref[z, 0:LOW_ABOVE, lanes]
            low, high = lift_in_scratch(part, deep)
            approx[:, lanes] = low
            held[1, z, :, lanes] = high[16 : 16 + half]
        whole = exact_dot(approx[...], w_ref)
        for tile, lanes in enumerate(lane_tiles(width)):
            split[z, tile] = whole[:, tile * LANES : (tile + 1) * LANES]
            part = scratch.at[tile]
            part[8:16] = below_ref[z, LOW_BELOW : LOW_BELOW + 8, lanes]
            part[16 : 16 + rows] = high_ref[z, :, lanes]
            part[16 + rows : 24 + rows] = above_ref[z, LOW_ABOVE : LOW_ABOVE + 8, lanes]
            low, high = lift_in_scratch(part, half + 16)
            held[0, z, :, lanes] = low[8 : 8 + half]
            held[2, z, :, lanes] = high[8 : 8 + half]
        return carry

    scratch[:, rows + 32 :] = jnp.zeros_like(scratch[:, rows + 32 :])
    lax.fori_loop(0, planes, step, 0)
    copy = pltpu.make_async_copy(held, detail_ref.at[0:3], sem)
    copy.start()
    span = deep // 2
    for z in range(planes):
        for y in range(2):
            low, high = lift_in_scratch(split.at[z, y], span)
            if y == 0:
                bands_ref[z, 0:span, :] = low
            else:
                bands_ref[z, span : span + quarter, :] = low[8 : 8 + quarter]
            start = span + quarter * (1 + y)
            bands_ref[z, start : start + quarter, :] = high[8 : 8 + quarter]
    spread_rims(bands_ref, up_ref, down_ref, bands_ref.shape[1])
    copy.wait()


def z_high_kernel(x_ref, below_ref, above_ref, whole_ref, detail_ref, held, sem):
    del whole_ref
    planes, rows, _ = x_ref.shape
    half = rows // 2
    for xb in range(2):

        def body(at):
            here = pl.ds(at.start + xb * half, at.size)
            low, high = lift_planes(
                [x_ref[z, here, :] for z in range(planes)],
                [below_ref[k, here, :] for k in range(2)],
                [above_ref[k, here, :] for k in range(2)],
            )
            for z in range(planes // 2):
                held[2 * xb, z, at, :] = low[z]
                held[2 * xb + 1, z, at, :] = high[z]

        over_rows(half, body)
    copy = pltpu.make_async_copy(held, detail_ref.at[3:7], sem)
    copy.start()
    copy.wait()


def z_middle_kernel(
    bands_ref, below_ref, above_ref, w_ref,
    detail_ref, planes_ref, far_ref,
    low_ref, high_ref, split,
):
    planes, rows, width = bands_ref.shape
    kept = planes // 2
    quarter = detail_ref.shape[2]
    span = rows - 3 * quarter

    def body(at):
        low, high = lift_planes(
            [bands_ref[z, at, :] for z in range(planes)],
            [below_ref[k, at, :] for k in range(2)],
            [above_ref[k, at, :] for k in range(2)],
        )
        for z in range(kept):
            low_ref[z, at, :] = low[z]
            high_ref[z, at, :] = high[z]

    over_rows(rows, body)
    for z in range(kept):
        split[z] = exact_dot(low_ref[z, 0:span, :], w_ref)
        detail_ref[0, z] = high_ref[z, 8 : 8 + quarter, :]
        for place, band in enumerate((4, 2, 6)):
            start = span + quarter * place
            detail_ref[band - 1, z] = low_ref[z, start : start + quarter, :]
            detail_ref[band, z] = high_ref[z, start : start + quarter, :]
    eighth = quarter // 2
    for z in range(kept):
        low, high = lift_in_scratch(split.at[z], span // 2)
        planes_ref[z, 0:eighth, :] = low[4 : 4 + eighth]
        planes_ref[z, eighth:, :] = high[4 : 4 + eighth]
    far_ref[0] = planes_ref[1] + ALPHA * planes_ref[0]


def z_last_kernel(
    planes_ref, below_ref, far_below_ref, above_ref, far_above_ref, detail_ref, coarse_ref
):
    low, high = lift_pair(
        (planes_ref[0], planes_ref[1]),
        (below_ref[0], below_ref[1]),
        far_below_ref[0],
        (above_ref[0], above_ref[1]),
        far_above_ref[0],
    )
    rows, width = coarse_ref.shape[1:]
    coarse_ref[0] = low[0:rows, 0:width]
    for band in range(1, 8):
        value = high if band % 2 else low
        xb, yb = (band // 2) % 2, band // 4
        detail_ref[band - 1, 0] = value[
            xb * rows : (xb + 1) * rows, yb * width : (yb + 1) * width
        ]


def call(kernel, out_shapes, inputs, scratch=(), anywhere=(), aliases=None, open_inputs=()):
    whole = pl.BlockSpec(memory_space=pltpu.VMEM)
    unplaced = pl.BlockSpec(memory_space=pl.ANY)
    return pl.pallas_call(
        kernel,
        out_shape=[jax.ShapeDtypeStruct(s, jnp.float32) for s in out_shapes],
        in_specs=[unplaced if i in open_inputs else whole for i in range(len(inputs))],
        out_specs=[unplaced if i in anywhere else whole for i in range(len(out_shapes))],
        scratch_shapes=list(scratch),
        input_output_aliases=aliases or {},
        compiler_params=pltpu.CompilerParams(vmem_limit_bytes=24 * 2**20),
        name=kernel.__name__,
    )(*inputs)


def on_device(velocity):
    planes, rows, width = velocity.shape
    half_width = width // 2
    half = rows // 2
    quarter = half // 2
    tiles = half_width // LANES
    f32 = jnp.float32
    matrix = band_matrix(width)
    w_low = jnp.asarray(three_parts(matrix[:, :half_width]))
    w_high = jnp.asarray(three_parts(matrix[:, half_width:]))
    w_two = jnp.asarray(three_parts(band_matrix(half_width)))
    w_three = jnp.asarray(three_parts(band_matrix(half_width // 2)))

    whole = (planes, rows, half_width)
    rims = (2, rows, half_width)
    y_low, up, down = call(y_low_kernel, [whole, rims, rims], [velocity, w_low])
    low_below, low_above = shifted(up, "gz", 1), shifted(down, "gz", -1)

    edge = (planes, 8, half_width)
    y_high, up, down = call(y_high_kernel, [whole, edge, edge], [velocity, w_high])
    below, above = shifted(up, "gx", 1), shifted(down, "gx", -1)
    x_high, up, down = call(
        x_high_kernel,
        [whole, rims, rims],
        [y_high, below, above],
        [pltpu.VMEM((tiles, rows + 32, LANES), f32)],
    )
    high_below, high_above = shifted(up, "gz", 1), shifted(down, "gz", -1)

    kept = (planes // 2, rows, half_width)
    z_low, z_high, up, down = call(
        z_low_kernel,
        [
            kept,
            kept,
            (planes // 2, LOW_BELOW + 8, half_width),
            (planes // 2, LOW_ABOVE + 8, half_width),
        ],
        [y_low, low_below, low_above],
    )
    below, above = shifted(up, "gx", 1), shifted(down, "gx", -1)
    deep = (rows + 64) // 2
    packed = deep // 2 + 3 * quarter
    detail_shape = (7, planes // 2, half, half_width)
    middle = (2, packed, half_width // 2)
    detail_one, bands, up, down = call(
        x_low_kernel,
        [detail_shape, (planes // 2, packed, half_width // 2), middle, middle],
        [z_low, z_high, below, above, w_two],
        [
            pltpu.VMEM((tiles, rows + 64, LANES), f32),
            pltpu.VMEM((deep, half_width), f32),
            pltpu.VMEM((planes // 2, tiles, deep, LANES), f32),
            pltpu.VMEM((3,) + detail_shape[1:], f32),
            pltpu.SemaphoreType.DMA,
        ],
        anywhere=(0,),
    )
    below, above = shifted(up, "gz", 1), shifted(down, "gz", -1)
    (detail_one,) = call(
        z_high_kernel,
        [detail_shape],
        [x_high, high_below, high_above, detail_one],
        [pltpu.VMEM((4,) + detail_shape[1:], f32), pltpu.SemaphoreType.DMA],
        anywhere=(0,),
        aliases={3: 0},
        open_inputs=(3,),
    )
    lanes = half_width // 2
    last = planes // 4
    detail_two, level, far = call(
        z_middle_kernel,
        [(7, last, quarter, lanes), (last, quarter, lanes), (1, quarter, lanes)],
        [bands, below, above, w_three],
        [
            pltpu.VMEM((last, packed, lanes), f32),
            pltpu.VMEM((last, packed, lanes), f32),
            pltpu.VMEM((last, deep // 2, lanes), f32),
        ],
    )
    below, above = shifted(level, "gz", 1), shifted(level, "gz", -1)
    far_below, far_above = shifted(far, "gz", 2), shifted(level[0:1], "gz", -2)
    detail_three, coarse = call(
        z_last_kernel,
        [(7, 1, quarter // 2, lanes // 2), (1, quarter // 2, lanes // 2)],
        [level, below, far_below, above, far_above],
    )
    return detail_one, detail_two, detail_three, coarse


def solution(mesh):
    placed = (P("gz", "gx", None),)
    return jax.shard_map(
        on_device,
        mesh=mesh,
        in_specs=placed,
        out_specs=(
            P(None, "gz", "gx", None),
            P(None, "gz", "gx", None),
            P(None, "gz", "gx", None),
            P("gz", "gx", None),
        ),
        check_vma=False,
    )
```

```python
import functools

import jax
import jax.numpy as jnp
import numpy as np
from jax import lax
from jax.experimental import pallas as pl
from jax.experimental.pallas import tpu as pltpu
from jax.sharding import PartitionSpec as P

LEVELS = 3
LANES = 128

LOW_TAPS = (
    0.026748757411,
    -0.016864118443,
    -0.078223266529,
    0.266864118443,
    0.602949018236,
    0.266864118443,
    -0.078223266529,
    -0.016864118443,
    0.026748757411,
)
HIGH_TAPS = (
    0.091271763114,
    -0.057543526229,
    -0.591271763114,
    1.115087052457,
    -0.591271763114,
    -0.057543526229,
    0.091271763114,
)

ALPHA = -1.586134342059924
BETA = -0.052980118572961
GAMMA = 0.882911075530934
DELTA = 0.443506852043971
LOW_SCALE = 0.812893066115961
HIGH_SCALE = 1.230174104914001


def shifted(value, axis, steps):
    count = lax.axis_size(axis)
    pairs = [(source, (source + steps) % count) for source in range(count)]
    return lax.ppermute(value, axis, pairs)


def band_matrix(length):
    half = length // 2
    matrix = np.zeros((length, length), np.float64)
    for j in range(half):
        for k in range(-4, 5):
            matrix[(2 * j + k) % length, j] += LOW_TAPS[k + 4]
        for k in range(-3, 4):
            matrix[(2 * j + 1 + k) % length, half + j] += HIGH_TAPS[k + 3]
    return matrix


def three_parts(matrix):
    parts = []
    rest = matrix
    for _ in range(3):
        part = rest.astype(np.float32).astype(jnp.bfloat16)
        parts.append(part)
        rest = rest - part.astype(np.float64)
    return np.stack(parts)


def exact_dot(value, parts):
    first = value.astype(jnp.bfloat16)
    rest = value - first.astype(jnp.float32)
    second = rest.astype(jnp.bfloat16)
    third = (rest - second.astype(jnp.float32)).astype(jnp.bfloat16)

    def dot(a, b):
        return jnp.dot(a, b, preferred_element_type=jnp.float32)

    small = dot(third, parts[0]) + dot(second, parts[1]) + dot(first, parts[2])
    middle = dot(second, parts[0]) + dot(first, parts[1])
    return dot(first, parts[0]) + (middle + small)


def lift_rows(even, odd):
    count = even.shape[0]

    def after(a):
        return pltpu.roll(a, count - 1, 0)

    def before(a):
        return pltpu.roll(a, 1, 0)

    odd = odd + ALPHA * (even + after(even))
    even = even + BETA * (before(odd) + odd)
    odd = odd + GAMMA * (even + after(even))
    even = even + DELTA * (before(odd) + odd)
    return even * LOW_SCALE, odd * HIGH_SCALE


def rim_sums(planes):
    even, odd = planes[0::2], planes[1::2]
    up_odd = odd[-1] + ALPHA * even[-1]
    up_even = even[-1] + BETA * (odd[-2] + ALPHA * (even[-2] + even[-1]))
    down_even = even[0] + BETA * (odd[0] + ALPHA * (even[0] + even[1]))
    return (up_odd, up_even), (even[0], down_even)


def lift_planes(planes, below, above):
    even, odd = planes[0::2], planes[1::2]
    count = len(even)
    first_odd = below[0] + ALPHA * even[0]
    odd = [
        odd[i] + ALPHA * (even[i] + (even[i + 1] if i + 1 < count else above[0]))
        for i in range(count)
    ]
    first_even = below[1] + BETA * first_odd
    even = [
        even[i] + BETA * ((odd[i - 1] if i else first_odd) + odd[i])
        for i in range(count)
    ]
    last_even = above[1] + BETA * odd[-1]
    first_odd = first_odd + GAMMA * (first_even + even[0])
    odd = [
        odd[i] + GAMMA * (even[i] + (even[i + 1] if i + 1 < count else last_even))
        for i in range(count)
    ]
    even = [
        even[i] + DELTA * ((odd[i - 1] if i else first_odd) + odd[i])
        for i in range(count)
    ]
    return [e * LOW_SCALE for e in even], [o * HIGH_SCALE for o in odd]


def double_taps():
    low, high = {}, {}
    for k in range(-4, 5):
        for m in range(-4, 5):
            at = 2 * k + m
            low[at] = low.get(at, 0.0) + LOW_TAPS[k + 4] * LOW_TAPS[m + 4]
    for k in range(-3, 4):
        for m in range(-4, 5):
            at = 2 * (k + 1) + m
            high[at] = high.get(at, 0.0) + HIGH_TAPS[k + 3] * LOW_TAPS[m + 4]
    return low, high


def ring_distances(planes):
    reach = -(-max(double_taps()[0]) // planes)
    return [0] + [sign * step for step in range(1, reach + 1) for sign in (1, -1)]


def deep_share(planes, distance):
    count = len(planes)
    shares = []
    for taps in double_taps():
        terms = [
            planes[z] * taps[z - count * distance]
            for z in range(count)
            if z - count * distance in taps
        ]
        shares.append(functools.reduce(jnp.add, terms) if terms else jnp.zeros_like(planes[0]))
    return shares


def chunk_of(rows):
    for size in (16, 8):
        if rows % size == 0:
            return size
    return rows


def over_rows(rows, body):
    size = chunk_of(rows)

    def step(i, carry):
        body(pl.ds(pl.multiple_of(i * size, size), size))
        return carry

    lax.fori_loop(0, rows // size, step, 0)


def spread_rims(source, up_ref, down_ref, rows):
    planes = source.shape[0]

    def body(at):
        up, down = rim_sums([source[z, at, :] for z in range(planes)])
        for k in range(2):
            up_ref[k, at, :] = up[k]
            down_ref[k, at, :] = down[k]

    over_rows(rows, body)


def y_low_kernel(v_ref, w_ref, y_ref, up_ref, down_ref):
    def step(z, carry):
        y_ref[z] = exact_dot(v_ref[z], w_ref)
        return carry

    lax.fori_loop(0, v_ref.shape[0], step, 0)
    spread_rims(y_ref, up_ref, down_ref, y_ref.shape[1])


def y_high_kernel(v_ref, w_ref, y_ref, up_ref, down_ref):
    rows = v_ref.shape[1]

    def step(z, carry):
        y = exact_dot(v_ref[z], w_ref)
        y_ref[z] = y
        up_ref[z] = y[rows - 8 :]
        down_ref[z] = y[:8]
        return carry

    lax.fori_loop(0, v_ref.shape[0], step, 0)


def lift_in_scratch(scratch, pairs):
    even = scratch[pl.ds(0, pairs, stride=2), :]
    odd = scratch[pl.ds(1, pairs, stride=2), :]
    return lift_rows(even, odd)


def lane_tiles(width):
    size = min(width, LANES)
    return [pl.ds(k, size) for k in range(0, width, size)]


def x_high_kernel(y_ref, below_ref, above_ref, x_ref, up_ref, down_ref, scratch):
    planes, rows, width = y_ref.shape
    half = rows // 2

    def step(z, carry):
        for tile, lanes in enumerate(lane_tiles(width)):
            part = scratch.at[tile]
            part[8:16] = below_ref[z, :, lanes]
            part[16 : 16 + rows] = y_ref[z, :, lanes]
            part[16 + rows : 24 + rows] = above_ref[z, :, lanes]
            low, high = lift_in_scratch(part, half + 16)
            x_ref[z, 0:half, lanes] = low[8 : 8 + half]
            x_ref[z, half:rows, lanes] = high[8 : 8 + half]
        return carry

    scratch[:, 0:8] = jnp.zeros_like(scratch[:, 0:8])
    scratch[:, 24 + rows :] = jnp.zeros_like(scratch[:, 24 + rows :])
    lax.fori_loop(0, planes, step, 0)
    spread_rims(x_ref, up_ref, down_ref, rows)


LOW_BELOW, LOW_ABOVE = 32, 24


def z_low_kernel(y_ref, below_ref, above_ref, later_ref, low_ref, high_ref, up_ref, down_ref):
    del later_ref
    planes, rows, _ = y_ref.shape

    def body(at):
        low, high = lift_planes(
            [y_ref[z, at, :] for z in range(planes)],
            [below_ref[k, at, :] for k in range(2)],
            [above_ref[k, at, :] for k in range(2)],
        )
        for z in range(planes // 2):
            low_ref[z, at, :] = low[z]
            high_ref[z, at, :] = high[z]

    over_rows(rows, body)
    up_ref[:, 0:LOW_BELOW, :] = low_ref[:, rows - LOW_BELOW : rows, :]
    up_ref[:, LOW_BELOW : LOW_BELOW + 8, :] = high_ref[:, rows - 8 : rows, :]
    down_ref[:, 0:LOW_ABOVE, :] = low_ref[:, 0:LOW_ABOVE, :]
    down_ref[:, LOW_ABOVE : LOW_ABOVE + 8, :] = high_ref[:, 0:8, :]


def x_low_kernel(
    low_ref, high_ref, below_ref, above_ref, w_two_ref, w_three_ref,
    detail_ref, bands_ref, up_ref, down_ref, own_ref, *rest,
):
    *far_refs, scratch, approx, split, deep_split, deep_planes, held, sem = rest
    planes, rows, width = low_ref.shape
    half = rows // 2
    deep = (rows + 64) // 2
    quarter = half // 2
    eighth = quarter // 2

    def step(z, carry):
        for tile, lanes in enumerate(lane_tiles(width)):
            part = scratch.at[tile]
            part[0:LOW_BELOW] = below_ref[z, 0:LOW_BELOW, lanes]
            part[LOW_BELOW : LOW_BELOW + rows] = low_ref[z, :, lanes]
            top = LOW_BELOW + rows
            part[top : top + LOW_ABOVE] = above_ref[z, 0:LOW_ABOVE, lanes]
            low, high = lift_in_scratch(part, deep)
            approx[:, lanes] = low
            held[1, z, :, lanes] = high[16 : 16 + half]
        whole = exact_dot(approx[...], w_two_ref)
        for tile, lanes in enumerate(lane_tiles(width)):
            split[z, tile] = whole[:, tile * LANES : (tile + 1) * LANES]
            part = scratch.at[tile]
            part[8:16] = below_ref[z, LOW_BELOW : LOW_BELOW + 8, lanes]
            part[16 : 16 + rows] = high_ref[z, :, lanes]
            part[16 + rows : 24 + rows] = above_ref[z, LOW_ABOVE : LOW_ABOVE + 8, lanes]
            low, high = lift_in_scratch(part, half + 16)
            held[0, z, :, lanes] = low[8 : 8 + half]
            held[2, z, :, lanes] = high[8 : 8 + half]
        return carry

    scratch[:, rows + 32 :] = jnp.zeros_like(scratch[:, rows + 32 :])
    lax.fori_loop(0, planes, step, 0)
    copy = pltpu.make_async_copy(held, detail_ref.at[0:3], sem)
    copy.start()
    span = deep // 2
    for z in range(planes):
        for y in range(2):
            low, high = lift_in_scratch(split.at[z, y], span)
            start = 2 * y * quarter
            bands_ref[z, start : start + quarter, :] = low[8 : 8 + quarter]
            bands_ref[z, start + quarter : start + 2 * quarter, :] = high[8 : 8 + quarter]
            if y == 0:
                deep_split[z] = exact_dot(low, w_three_ref)
    for z in range(planes):
        low, high = lift_in_scratch(deep_split.at[z], span // 2)
        deep_planes[z, 0:eighth, :] = low[4 : 4 + eighth]
        deep_planes[z, eighth:, :] = high[4 : 4 + eighth]
    packed = bands_ref.shape[1]
    spread_rims(bands_ref, up_ref, down_ref, packed)
    near = (own_ref, up_ref.at[:, packed:, :], down_ref.at[:, packed:, :])
    for distance, ref in zip(ring_distances(planes), near + tuple(far_refs), strict=True):
        share = deep_share([deep_planes[z] for z in range(planes)], distance)
        ref[0] = share[0]
        ref[1] = share[1]
    copy.wait()


def z_high_kernel(x_ref, below_ref, above_ref, whole_ref, detail_ref, held, sem):
    del whole_ref
    planes, rows, _ = x_ref.shape
    half = rows // 2
    for xb in range(2):

        def body(at):
            here = pl.ds(at.start + xb * half, at.size)
            low, high = lift_planes(
                [x_ref[z, here, :] for z in range(planes)],
                [below_ref[k, here, :] for k in range(2)],
                [above_ref[k, here, :] for k in range(2)],
            )
            for z in range(planes // 2):
                held[2 * xb, z, at, :] = low[z]
                held[2 * xb + 1, z, at, :] = high[z]

        over_rows(half, body)
    copy = pltpu.make_async_copy(held, detail_ref.at[3:7], sem)
    copy.start()
    copy.wait()


def z_middle_kernel(bands_ref, below_ref, above_ref, own_ref, *rest):
    *far_refs, detail_ref, deep_ref, coarse_ref, low_ref, high_ref = rest
    planes, rows, _ = bands_ref.shape
    kept = planes // 2
    quarter = detail_ref.shape[2]

    def body(at):
        low, high = lift_planes(
            [bands_ref[z, at, :] for z in range(planes)],
            [below_ref[k, at, :] for k in range(2)],
            [above_ref[k, at, :] for k in range(2)],
        )
        for z in range(kept):
            low_ref[z, at, :] = low[z]
            high_ref[z, at, :] = high[z]

    over_rows(rows, body)
    for z in range(kept):
        for band in range(1, 8):
            source = high_ref if band % 2 else low_ref
            start = quarter * (band // 2)
            detail_ref[band - 1, z] = source[z, start : start + quarter, :]
    height, width = coarse_ref.shape[1:]
    near = (own_ref, below_ref.at[:, rows:, :], above_ref.at[:, rows:, :])
    low, high = (
        functools.reduce(jnp.add, [ref[k] for ref in near + tuple(far_refs)])
        for k in range(2)
    )
    coarse_ref[0] = low[0:height, 0:width]
    for band in range(1, 8):
        value = high if band % 2 else low
        xb, yb = (band // 2) % 2, band // 4
        deep_ref[band - 1, 0] = value[
            xb * height : (xb + 1) * height, yb * width : (yb + 1) * width
        ]


def call(kernel, out_shapes, inputs, scratch=(), anywhere=(), aliases=None, open_inputs=()):
    whole = pl.BlockSpec(memory_space=pltpu.VMEM)
    unplaced = pl.BlockSpec(memory_space=pl.ANY)
    return pl.pallas_call(
        kernel,
        out_shape=[jax.ShapeDtypeStruct(s, jnp.float32) for s in out_shapes],
        in_specs=[unplaced if i in open_inputs else whole for i in range(len(inputs))],
        out_specs=[unplaced if i in anywhere else whole for i in range(len(out_shapes))],
        scratch_shapes=list(scratch),
        input_output_aliases=aliases or {},
        compiler_params=pltpu.CompilerParams(vmem_limit_bytes=24 * 2**20),
        name=kernel.__name__,
    )(*inputs)


def on_device(velocity):
    planes, rows, width = velocity.shape
    half_width = width // 2
    half = rows // 2
    quarter = half // 2
    tiles = half_width // LANES
    f32 = jnp.float32
    matrix = band_matrix(width)
    w_low = jnp.asarray(three_parts(matrix[:, :half_width]))
    w_high = jnp.asarray(three_parts(matrix[:, half_width:]))
    w_two = jnp.asarray(three_parts(band_matrix(half_width)))
    w_three = jnp.asarray(three_parts(band_matrix(half_width // 2)))

    whole = (planes, rows, half_width)
    rims = (2, rows, half_width)
    y_low, up, down = call(y_low_kernel, [whole, rims, rims], [velocity, w_low])
    low_below, low_above = shifted(up, "gz", 1), shifted(down, "gz", -1)

    edge = (planes, 8, half_width)
    y_high, up, down = call(y_high_kernel, [whole, edge, edge], [velocity, w_high])
    below, above = shifted(up, "gx", 1), shifted(down, "gx", -1)
    x_high, up_high, down_high = call(
        x_high_kernel,
        [whole, rims, rims],
        [y_high, below, above],
        [pltpu.VMEM((tiles, rows + 32, LANES), f32)],
    )
    high_below, high_above = shifted(up_high, "gz", 1), shifted(down_high, "gz", -1)

    kept = (planes // 2, rows, half_width)
    z_low, z_high, up, down = call(
        z_low_kernel,
        [
            kept,
            kept,
            (planes // 2, LOW_BELOW + 8, half_width),
            (planes // 2, LOW_ABOVE + 8, half_width),
        ],
        [y_low, low_below, low_above, up_high],
        open_inputs=(3,),
    )
    below, above = shifted(up, "gx", 1), shifted(down, "gx", -1)
    deep = (rows + 64) // 2
    packed = 4 * quarter
    eighth = quarter // 2
    lanes = half_width // 2
    detail_shape = (7, planes // 2, half, half_width)
    middle = (2, packed + 2 * eighth, lanes)
    share = (2, 2 * eighth, lanes)
    distances = ring_distances(planes // 2)
    detail_one, bands, up, down, own, *far = call(
        x_low_kernel,
        [detail_shape, (planes // 2, packed, lanes), middle, middle]
        + [share] * (len(distances) - 2),
        [z_low, z_high, below, above, w_two, w_three],
        [
            pltpu.VMEM((tiles, rows + 64, LANES), f32),
            pltpu.VMEM((deep, half_width), f32),
            pltpu.VMEM((planes // 2, tiles, deep, LANES), f32),
            pltpu.VMEM((planes // 2, deep // 2, lanes), f32),
            pltpu.VMEM((planes // 2, 2 * eighth, lanes), f32),
            pltpu.VMEM((3,) + detail_shape[1:], f32),
            pltpu.SemaphoreType.DMA,
        ],
        anywhere=(0,),
    )
    below, above = shifted(up, "gz", 1), shifted(down, "gz", -1)
    far = [shifted(part, "gz", step) for part, step in zip(far, distances[3:], strict=True)]
    (detail_one,) = call(
        z_high_kernel,
        [detail_shape],
        [x_high, high_below, high_above, detail_one],
        [pltpu.VMEM((4,) + detail_shape[1:], f32), pltpu.SemaphoreType.DMA],
        anywhere=(0,),
        aliases={3: 0},
        open_inputs=(3,),
    )
    last = planes // 4
    detail_two, detail_three, coarse = call(
        z_middle_kernel,
        [
            (7, last, quarter, lanes),
            (7, 1, eighth, lanes // 2),
            (1, eighth, lanes // 2),
        ],
        [bands, below, above, own, *far],
        [pltpu.VMEM((last, packed, lanes), f32)] * 2,
    )
    return detail_one, detail_two, detail_three, coarse


def solution(mesh):
    placed = (P("gz", "gx", None),)
    return jax.shard_map(
        on_device,
        mesh=mesh,
        in_specs=placed,
        out_specs=(
            P(None, "gz", "gx", None),
            P(None, "gz", "gx", None),
            P(None, "gz", "gx", None),
            P("gz", "gx", None),
        ),
        check_vma=False,
    )
```

```python
import functools

import jax
import jax.numpy as jnp
import numpy as np
from jax import lax
from jax.experimental import pallas as pl
from jax.experimental.pallas import tpu as pltpu
from jax.sharding import PartitionSpec as P

LEVELS = 3
GAP = 1
PLANES = 4
PARTS = 1
MARK = (8, 128)
LANES = 128

LOW_TAPS = (
    0.026748757411,
    -0.016864118443,
    -0.078223266529,
    0.266864118443,
    0.602949018236,
    0.266864118443,
    -0.078223266529,
    -0.016864118443,
    0.026748757411,
)
HIGH_TAPS = (
    0.091271763114,
    -0.057543526229,
    -0.591271763114,
    1.115087052457,
    -0.591271763114,
    -0.057543526229,
    0.091271763114,
)

ALPHA = -1.586134342059924
BETA = -0.052980118572961
GAMMA = 0.882911075530934
DELTA = 0.443506852043971
LOW_SCALE = 0.812893066115961
HIGH_SCALE = 1.230174104914001


def shifted(value, axis, steps):
    count = lax.axis_size(axis)
    pairs = [(source, (source + steps) % count) for source in range(count)]
    return lax.ppermute(value, axis, pairs)


def band_matrix(length):
    half = length // 2
    matrix = np.zeros((length, length), np.float64)
    for j in range(half):
        for k in range(-4, 5):
            matrix[(2 * j + k) % length, j] += LOW_TAPS[k + 4]
        for k in range(-3, 4):
            matrix[(2 * j + 1 + k) % length, half + j] += HIGH_TAPS[k + 3]
    return matrix


def three_parts(matrix):
    parts = []
    rest = matrix
    for _ in range(3):
        part = rest.astype(np.float32).astype(jnp.bfloat16)
        parts.append(part)
        rest = rest - part.astype(np.float64)
    return np.stack(parts)


def exact_dot(value, parts):
    first = value.astype(jnp.bfloat16)
    rest = value - first.astype(jnp.float32)
    second = rest.astype(jnp.bfloat16)
    third = (rest - second.astype(jnp.float32)).astype(jnp.bfloat16)

    count = value.shape[0]

    def dot(parts_of_value, part):
        rows = jnp.concatenate(parts_of_value, 0)
        result = jnp.dot(rows, part, preferred_element_type=jnp.float32)
        return [result[k * count : (k + 1) * count] for k in range(len(parts_of_value))]

    large, middle, small = dot([first, second, third], parts[0])
    middle_too, small_too = dot([first, second], parts[1])
    (small_last,) = dot([first], parts[2])
    return large + ((middle + middle_too) + (small + small_too + small_last))


def lift_rows(even, odd):
    count = even.shape[0]

    def after(a):
        return pltpu.roll(a, count - 1, 0)

    def before(a):
        return pltpu.roll(a, 1, 0)

    odd = odd + ALPHA * (even + after(even))
    even = even + BETA * (before(odd) + odd)
    odd = odd + GAMMA * (even + after(even))
    even = even + DELTA * (before(odd) + odd)
    return even * LOW_SCALE, odd * HIGH_SCALE


def rim_sums(planes):
    even, odd = planes[0::2], planes[1::2]
    up_odd = odd[-1] + ALPHA * even[-1]
    up_even = even[-1] + BETA * (odd[-2] + ALPHA * (even[-2] + even[-1]))
    down_even = even[0] + BETA * (odd[0] + ALPHA * (even[0] + even[1]))
    return (up_odd, up_even), (even[0], down_even)


def lift_planes(planes, below, above):
    even, odd = planes[0::2], planes[1::2]
    count = len(even)
    first_odd = below[0] + ALPHA * even[0]
    odd = [
        odd[i] + ALPHA * (even[i] + (even[i + 1] if i + 1 < count else above[0]))
        for i in range(count)
    ]
    first_even = below[1] + BETA * first_odd
    even = [
        even[i] + BETA * ((odd[i - 1] if i else first_odd) + odd[i])
        for i in range(count)
    ]
    last_even = above[1] + BETA * odd[-1]
    first_odd = first_odd + GAMMA * (first_even + even[0])
    odd = [
        odd[i] + GAMMA * (even[i] + (even[i + 1] if i + 1 < count else last_even))
        for i in range(count)
    ]
    even = [
        even[i] + DELTA * ((odd[i - 1] if i else first_odd) + odd[i])
        for i in range(count)
    ]
    return [e * LOW_SCALE for e in even], [o * HIGH_SCALE for o in odd]


def double_taps():
    low, high = {}, {}
    for k in range(-4, 5):
        for m in range(-4, 5):
            at = 2 * k + m
            low[at] = low.get(at, 0.0) + LOW_TAPS[k + 4] * LOW_TAPS[m + 4]
    for k in range(-3, 4):
        for m in range(-4, 5):
            at = 2 * (k + 1) + m
            high[at] = high.get(at, 0.0) + HIGH_TAPS[k + 3] * LOW_TAPS[m + 4]
    return low, high


def ring_distances(planes):
    reach = -(-max(double_taps()[0]) // planes)
    return [0] + [sign * step for step in range(1, reach + 1) for sign in (1, -1)]


def deep_share(planes, distance):
    count = len(planes)
    shares = []
    for taps in double_taps():
        terms = [
            planes[z] * taps[z - count * distance]
            for z in range(count)
            if z - count * distance in taps
        ]
        shares.append(functools.reduce(jnp.add, terms) if terms else jnp.zeros_like(planes[0]))
    return shares


def chunk_of(rows):
    for size in (16, 8):
        if rows % size == 0:
            return size
    return rows


def over_rows(rows, body):
    size = chunk_of(rows)

    def step(i, carry):
        body(pl.ds(pl.multiple_of(i * size, size), size))
        return carry

    lax.fori_loop(0, rows // size, step, 0)


def spread_rims(source, up_ref, down_ref, rows):
    planes = source.shape[0]

    def body(at):
        up, down = rim_sums([source[z, at, :] for z in range(planes)])
        for k in range(2):
            up_ref[k, at, :] = up[k]
            down_ref[k, at, :] = down[k]

    over_rows(rows, body)


def mark(ref):
    ref[...] = jnp.zeros_like(ref)


def rim_kernel(v_ref, w_ref, up_ref, down_ref, held, weights, raw, sems):
    planes, rows, _ = held.shape
    parts = sems.shape[0] - 1
    size = rows // parts
    copies = []
    for part in range(parts):
        at = pl.ds(part * size, size)
        copies.append(pltpu.make_async_copy(v_ref.at[:, at, :], held.at[:, at, :], sems.at[part]))
        copies[-1].start()
    weight_copy = pltpu.make_async_copy(w_ref, weights, sems.at[parts])
    weight_copy.start()
    for part in range(parts):
        copies[part].wait()

        def step(i, carry):
            at = pl.ds(pl.multiple_of(part * size + i * 8, 8), 8)
            up, down = rim_sums([held[z, at, :] for z in range(planes)])
            for k, value in enumerate(up + down):
                raw[k, at, :] = value
            return carry

        lax.fori_loop(0, size // 8, step, 0)
        if part == 0:
            weight_copy.wait()
        at = pl.ds(part * size, size)
        low = exact_dot(raw[:, at, :].reshape(4 * size, -1), weights)
        for k, ref in enumerate((up_ref, up_ref, down_ref, down_ref)):
            ref[k % 2, at, :] = low[k * size : (k + 1) * size]


def y_kernel(v_ref, w_low_ref, w_high_ref, low_ref, high_ref, up_ref, down_ref):
    planes, rows, width = v_ref.shape
    block = PLANES if planes % PLANES == 0 else 1

    def step(i, carry):
        at = pl.ds(i * block, block)
        flat = v_ref[at].reshape(block * rows, width)
        low_ref[at] = exact_dot(flat, w_low_ref).reshape(block, rows, width // 2)
        high = exact_dot(flat, w_high_ref).reshape(block, rows, width // 2)
        high_ref[at] = high
        up_ref[at] = high[:, rows - 8 :]
        down_ref[at] = high[:, :8]
        return carry

    lax.fori_loop(0, planes // block, step, 0)


def lift_in_scratch(scratch, pairs):
    even = scratch[pl.ds(0, pairs, stride=2), :]
    odd = scratch[pl.ds(1, pairs, stride=2), :]
    return lift_rows(even, odd)


def lane_tiles(width):
    size = min(width, LANES)
    return [pl.ds(k, size) for k in range(0, width, size)]


def x_high_kernel(
    y_ref, below_ref, above_ref, x_ref, up_ref, down_ref, mark_ref, scratch
):
    planes, rows, width = y_ref.shape
    half = rows // 2

    def step(z, carry):
        for tile, lanes in enumerate(lane_tiles(width)):
            part = scratch.at[tile]
            part[8:16] = below_ref[z, :, lanes]
            part[16 : 16 + rows] = y_ref[z, :, lanes]
            part[16 + rows : 24 + rows] = above_ref[z, :, lanes]
            low, high = lift_in_scratch(part, half + 16)
            x_ref[z, 0:half, lanes] = low[8 : 8 + half]
            x_ref[z, half:rows, lanes] = high[8 : 8 + half]
        return carry

    scratch[:, 0:8] = jnp.zeros_like(scratch[:, 0:8])
    scratch[:, 24 + rows :] = jnp.zeros_like(scratch[:, 24 + rows :])
    lax.fori_loop(0, planes, step, 0)
    spread_rims(x_ref, up_ref, down_ref, rows)
    mark(mark_ref)


LOW_BELOW, LOW_ABOVE = 32, 24


def lift_rows_of(y_ref, below_ref, above_ref, at):
    return lift_planes(
        [y_ref[z, at, :] for z in range(y_ref.shape[0])],
        [below_ref[k, at, :] for k in range(2)],
        [above_ref[k, at, :] for k in range(2)],
    )


def z_edge_kernel(y_ref, below_ref, above_ref, after_ref, up_ref, down_ref, mark_ref):
    del after_ref
    planes, rows, _ = y_ref.shape
    size = 8
    for start in range(0, LOW_ABOVE, size):
        low, high = lift_rows_of(y_ref, below_ref, above_ref, slice(start, start + size))
        for z in range(planes // 2):
            down_ref[z, start : start + size] = low[z]
            if start == 0:
                down_ref[z, LOW_ABOVE : LOW_ABOVE + size] = high[z]
    for start in range(0, LOW_BELOW, size):
        at = rows - LOW_BELOW + start
        low, high = lift_rows_of(y_ref, below_ref, above_ref, slice(at, at + size))
        for z in range(planes // 2):
            up_ref[z, start : start + size] = low[z]
            if start == LOW_BELOW - size:
                up_ref[z, LOW_BELOW : LOW_BELOW + size] = high[z]
    mark(mark_ref)


def z_lift_kernel(y_ref, below_ref, above_ref, after_ref, low_ref, high_ref):
    del after_ref
    planes, rows, _ = y_ref.shape

    def body(at):
        low, high = lift_rows_of(y_ref, below_ref, above_ref, at)
        for z in range(planes // 2):
            low_ref[z, at, :] = low[z]
            high_ref[z, at, :] = high[z]

    over_rows(rows, body)


def x_low_kernel(
    low_ref, below_ref, above_ref, w_two_ref, w_three_ref,
    part_ref, bands_ref, up_ref, down_ref, own_ref, *rest,
):
    *far_refs, mark_ref, scratch, approx, split, deep_split, deep_planes = rest
    planes, rows, width = low_ref.shape
    half = rows // 2
    deep = (rows + 64) // 2
    quarter = half // 2
    eighth = quarter // 2

    def step(z, carry):
        for tile, lanes in enumerate(lane_tiles(width)):
            part = scratch.at[tile]
            part[0:LOW_BELOW] = below_ref[z, 0:LOW_BELOW, lanes]
            part[LOW_BELOW : LOW_BELOW + rows] = low_ref[z, :, lanes]
            top = LOW_BELOW + rows
            part[top : top + LOW_ABOVE] = above_ref[z, 0:LOW_ABOVE, lanes]
            low, high = lift_in_scratch(part, deep)
            approx[:, lanes] = low
            part_ref[0, z, :, lanes] = high[16 : 16 + half]
        whole = exact_dot(approx[...], w_two_ref)
        for tile in range(split.shape[1]):
            split[z, tile] = whole[:, tile * LANES : (tile + 1) * LANES]
        return carry

    scratch[:, rows + 32 :] = jnp.zeros_like(scratch[:, rows + 32 :])
    lax.fori_loop(0, planes, step, 0)
    span = deep // 2
    for z in range(planes):
        for y in range(2):
            low, high = lift_in_scratch(split.at[z, y], span)
            start = 2 * y * quarter
            bands_ref[z, start : start + quarter, :] = low[8 : 8 + quarter]
            bands_ref[z, start + quarter : start + 2 * quarter, :] = high[8 : 8 + quarter]
            if y == 0:
                deep_split[z] = exact_dot(low, w_three_ref)
    for z in range(planes):
        low, high = lift_in_scratch(deep_split.at[z], span // 2)
        deep_planes[z, 0:eighth, :] = low[4 : 4 + eighth]
        deep_planes[z, eighth:, :] = high[4 : 4 + eighth]
    packed = bands_ref.shape[1]
    spread_rims(bands_ref, up_ref, down_ref, packed)
    near = (own_ref, up_ref.at[:, packed:, :], down_ref.at[:, packed:, :])
    for distance, ref in zip(ring_distances(planes), near + tuple(far_refs), strict=True):
        share = deep_share([deep_planes[z] for z in range(planes)], distance)
        ref[0] = share[0]
        ref[1] = share[1]
    mark(mark_ref)


def x_detail_kernel(part_ref, high_ref, below_ref, above_ref, detail_ref, scratch, held, sems):
    planes, rows, width = high_ref.shape
    half = rows // 2
    copies = [pltpu.make_async_copy(part_ref, detail_ref.at[1:2], sems.at[0])]
    copies[0].start()
    scratch[:, 0:8] = jnp.zeros_like(scratch[:, 0:8])
    scratch[:, rows + 24 :] = jnp.zeros_like(scratch[:, rows + 24 :])

    def step(z, carry):
        for tile, lanes in enumerate(lane_tiles(width)):
            part = scratch.at[tile]
            part[8:16] = below_ref[z, LOW_BELOW : LOW_BELOW + 8, lanes]
            part[16 : 16 + rows] = high_ref[z, :, lanes]
            part[16 + rows : 24 + rows] = above_ref[z, LOW_ABOVE : LOW_ABOVE + 8, lanes]
            low, high = lift_in_scratch(part, half + 16)
            held[0, z, :, lanes] = low[8 : 8 + half]
            held[1, z, :, lanes] = high[8 : 8 + half]
        return carry

    lax.fori_loop(0, planes, step, 0)
    for k in range(2):
        copies.append(
            pltpu.make_async_copy(
                held.at[k : k + 1], detail_ref.at[2 * k : 2 * k + 1], sems.at[1 + k]
            )
        )
        copies[-1].start()
    for copy in copies:
        copy.wait()


def z_high_kernel(x_ref, below_ref, above_ref, whole_ref, after_ref, detail_ref, held, sems):
    del whole_ref, after_ref
    planes, rows, _ = x_ref.shape
    half = rows // 2
    copies = []
    for xb in range(2):

        def body(at):
            here = pl.ds(at.start + xb * half, at.size)
            low, high = lift_rows_of(x_ref, below_ref, above_ref, here)
            for z in range(planes // 2):
                held[2 * xb, z, at, :] = low[z]
                held[2 * xb + 1, z, at, :] = high[z]

        over_rows(half, body)
        copies.append(
            pltpu.make_async_copy(
                held.at[pl.ds(2 * xb, 2)], detail_ref.at[pl.ds(3 + 2 * xb, 2)], sems.at[xb]
            )
        )
        copies[-1].start()
    for copy in copies:
        copy.wait()


def z_middle_kernel(bands_ref, below_ref, above_ref, own_ref, *rest):
    *far_refs, detail_ref, deep_ref, coarse_ref, low_ref, high_ref = rest
    planes, rows, _ = bands_ref.shape
    kept = planes // 2
    quarter = detail_ref.shape[2]

    def body(at):
        low, high = lift_planes(
            [bands_ref[z, at, :] for z in range(planes)],
            [below_ref[k, at, :] for k in range(2)],
            [above_ref[k, at, :] for k in range(2)],
        )
        for z in range(kept):
            low_ref[z, at, :] = low[z]
            high_ref[z, at, :] = high[z]

    over_rows(rows, body)
    for z in range(kept):
        for band in range(1, 8):
            source = high_ref if band % 2 else low_ref
            start = quarter * (band // 2)
            detail_ref[band - 1, z] = source[z, start : start + quarter, :]
    height, width = coarse_ref.shape[1:]
    near = (own_ref, below_ref.at[:, rows:, :], above_ref.at[:, rows:, :])
    low, high = (
        functools.reduce(jnp.add, [ref[k] for ref in near + tuple(far_refs)])
        for k in range(2)
    )
    coarse_ref[0] = low[0:height, 0:width]
    for band in range(1, 8):
        value = high if band % 2 else low
        xb, yb = (band // 2) % 2, band // 4
        deep_ref[band - 1, 0] = value[
            xb * height : (xb + 1) * height, yb * width : (yb + 1) * width
        ]


def call(
    kernel, out_shapes, inputs, scratch=(), anywhere=(), aliases=None, open_inputs=(), cost=1
):
    whole = pl.BlockSpec(memory_space=pltpu.VMEM)
    unplaced = pl.BlockSpec(memory_space=pl.ANY)
    return pl.pallas_call(
        kernel,
        out_shape=[
            jax.ShapeDtypeStruct(s, jnp.float32)
            if isinstance(s, tuple)
            else jax.ShapeDtypeStruct(s.shape, s.dtype)
            for s in out_shapes
        ],
        in_specs=[unplaced if i in open_inputs else whole for i in range(len(inputs))],
        out_specs=[unplaced if i in anywhere else whole for i in range(len(out_shapes))],
        scratch_shapes=list(scratch),
        input_output_aliases=aliases or {},
        cost_estimate=pl.CostEstimate(flops=cost, bytes_accessed=cost, transcendentals=0),
        compiler_params=pltpu.CompilerParams(vmem_limit_bytes=24 * 2**20),
        name=kernel.__name__,
    )(*inputs)


def on_device(velocity):
    planes, rows, width = velocity.shape
    half_width = width // 2
    half = rows // 2
    quarter = half // 2
    tiles = half_width // LANES
    f32 = jnp.float32
    matrix = band_matrix(width)
    w_low = jnp.asarray(three_parts(matrix[:, :half_width]))
    w_high = jnp.asarray(three_parts(matrix[:, half_width:]))
    w_two = jnp.asarray(three_parts(band_matrix(half_width)))
    w_three = jnp.asarray(three_parts(band_matrix(half_width // 2)))

    whole = (planes, rows, half_width)
    rims = (2, rows, half_width)
    up, down, held, weights = call(
        rim_kernel,
        [rims, rims, velocity.shape, w_low],
        [
            pltpu.with_memory_space_constraint(velocity, pltpu.HBM),
            pltpu.with_memory_space_constraint(w_low, pltpu.HBM),
        ],
        [
            pltpu.VMEM((4, rows, width), f32),
            pltpu.SemaphoreType.DMA((PARTS + 1,)),
        ],
        open_inputs=(0, 1),
    )
    low_below, low_above = shifted(up, "gz", 1), shifted(down, "gz", -1)

    edge = (planes, 8, half_width)
    y_low, y_high, up, down = call(
        y_kernel, [whole, whole, edge, edge], [held, weights, w_high]
    )
    below, above = shifted(up, "gx", 1), shifted(down, "gx", -1)
    x_high, up, down, mark_high = call(
        x_high_kernel,
        [whole, rims, rims, MARK],
        [y_high, below, above],
        [pltpu.VMEM((tiles, rows + 32, LANES), f32)],
    )
    high_below, high_above = shifted(up, "gz", 1), shifted(down, "gz", -1)

    kept = (planes // 2, rows, half_width)
    up, down, mark_edge = call(
        z_edge_kernel,
        [
            (planes // 2, LOW_BELOW + 8, half_width),
            (planes // 2, LOW_ABOVE + 8, half_width),
            MARK,
        ],
        [y_low, low_below, low_above, mark_high],
    )
    edge_below, edge_above = shifted(up, "gx", 1), shifted(down, "gx", -1)
    z_low, z_high = call(
        z_lift_kernel, [kept, kept], [y_low, low_below, low_above, mark_edge], cost=GAP
    )
    deep = (rows + 64) // 2
    packed = 4 * quarter
    eighth = quarter // 2
    lanes = half_width // 2
    detail_shape = (7, planes // 2, half, half_width)
    middle = (2, packed + 2 * eighth, lanes)
    share = (2, 2 * eighth, lanes)
    distances = ring_distances(planes // 2)
    part, bands, up, down, own, *far, mark_low = call(
        x_low_kernel,
        [(1,) + detail_shape[1:], (planes // 2, packed, lanes), middle, middle]
        + [share] * (len(distances) - 2)
        + [MARK],
        [z_low, edge_below, edge_above, w_two, w_three],
        [
            pltpu.VMEM((tiles, rows + 64, LANES), f32),
            pltpu.VMEM((deep, half_width), f32),
            pltpu.VMEM((planes // 2, tiles, deep, LANES), f32),
            pltpu.VMEM((planes // 2, deep // 2, lanes), f32),
            pltpu.VMEM((planes // 2, 2 * eighth, lanes), f32),
        ],
    )
    (detail_one,) = call(
        x_detail_kernel,
        [detail_shape],
        [part, z_high, edge_below, edge_above],
        [
            pltpu.VMEM((tiles, rows + 32, LANES), f32),
            pltpu.VMEM((2,) + detail_shape[1:], f32),
            pltpu.SemaphoreType.DMA((3,)),
        ],
        anywhere=(0,),
    )
    below, above = shifted(up, "gz", 1), shifted(down, "gz", -1)
    far = [shifted(part, "gz", step) for part, step in zip(far, distances[3:], strict=True)]
    (detail_one,) = call(
        z_high_kernel,
        [detail_shape],
        [x_high, high_below, high_above, detail_one, mark_low],
        [pltpu.VMEM((4,) + detail_shape[1:], f32), pltpu.SemaphoreType.DMA((2,))],
        anywhere=(0,),
        aliases={3: 0},
        open_inputs=(3,),
    )
    last = planes // 4
    detail_two, detail_three, coarse = call(
        z_middle_kernel,
        [
            (7, last, quarter, lanes),
            (7, 1, eighth, lanes // 2),
            (1, eighth, lanes // 2),
        ],
        [bands, below, above, own, *far],
        [pltpu.VMEM((last, packed, lanes), f32)] * 2,
    )
    return detail_one, detail_two, detail_three, coarse


def solution(mesh):
    placed = (P("gz", "gx", None),)
    return jax.shard_map(
        on_device,
        mesh=mesh,
        in_specs=placed,
        out_specs=(
            P(None, "gz", "gx", None),
            P(None, "gz", "gx", None),
            P(None, "gz", "gx", None),
            P("gz", "gx", None),
        ),
        check_vma=False,
    )
```

```python
import functools

import jax
import jax.numpy as jnp
import numpy as np
from jax import lax
from jax.experimental import pallas as pl
from jax.experimental.pallas import tpu as pltpu
from jax.sharding import PartitionSpec as P

LEVELS = 3
GAP = 1
GAP_OWN = 10**11
GAP_DETAIL = 1
PLANES = 4
PARTS = 1
MARK = (8, 128)
LANES = 128

LOW_TAPS = (
    0.026748757411,
    -0.016864118443,
    -0.078223266529,
    0.266864118443,
    0.602949018236,
    0.266864118443,
    -0.078223266529,
    -0.016864118443,
    0.026748757411,
)
HIGH_TAPS = (
    0.091271763114,
    -0.057543526229,
    -0.591271763114,
    1.115087052457,
    -0.591271763114,
    -0.057543526229,
    0.091271763114,
)

ALPHA = -1.586134342059924
BETA = -0.052980118572961
GAMMA = 0.882911075530934
DELTA = 0.443506852043971
LOW_SCALE = 0.812893066115961
HIGH_SCALE = 1.230174104914001


def shifted(value, axis, steps):
    count = lax.axis_size(axis)
    pairs = [(source, (source + steps) % count) for source in range(count)]
    return lax.ppermute(value, axis, pairs)


def other_core(value):
    count = lax.axis_size("gx")
    return lax.ppermute(value, "gx", [(source, source ^ 1) for source in range(count)])


def shifted_by_core(value, steps):
    high, wide = lax.axis_size("gz"), lax.axis_size("gx")
    pairs = [
        (z * wide + x, ((z + (-steps if x % 2 else steps)) % high) * wide + x)
        for z in range(high)
        for x in range(wide)
    ]
    return lax.ppermute(value, ("gz", "gx"), pairs)


def band_matrix(length):
    half = length // 2
    matrix = np.zeros((length, length), np.float64)
    for j in range(half):
        for k in range(-4, 5):
            matrix[(2 * j + k) % length, j] += LOW_TAPS[k + 4]
        for k in range(-3, 4):
            matrix[(2 * j + 1 + k) % length, half + j] += HIGH_TAPS[k + 3]
    return matrix


def three_parts(matrix):
    parts = []
    rest = matrix
    for _ in range(3):
        part = rest.astype(np.float32).astype(jnp.bfloat16)
        parts.append(part)
        rest = rest - part.astype(np.float64)
    return np.stack(parts)


def exact_dot(value, parts):
    first = value.astype(jnp.bfloat16)
    rest = value - first.astype(jnp.float32)
    second = rest.astype(jnp.bfloat16)
    third = (rest - second.astype(jnp.float32)).astype(jnp.bfloat16)

    count = value.shape[0]

    def dot(parts_of_value, part):
        rows = jnp.concatenate(parts_of_value, 0)
        result = jnp.dot(rows, part, preferred_element_type=jnp.float32)
        return [result[k * count : (k + 1) * count] for k in range(len(parts_of_value))]

    large, middle, small = dot([first, second, third], parts[0])
    middle_too, small_too = dot([first, second], parts[1])
    (small_last,) = dot([first], parts[2])
    return large + ((middle + middle_too) + (small + small_too + small_last))


def lift_rows(even, odd):
    count = even.shape[0]

    def after(a):
        return pltpu.roll(a, count - 1, 0)

    def before(a):
        return pltpu.roll(a, 1, 0)

    odd = odd + ALPHA * (even + after(even))
    even = even + BETA * (before(odd) + odd)
    odd = odd + GAMMA * (even + after(even))
    even = even + DELTA * (before(odd) + odd)
    return even * LOW_SCALE, odd * HIGH_SCALE


def rim_sums(planes):
    even, odd = planes[0::2], planes[1::2]
    up_odd = odd[-1] + ALPHA * even[-1]
    up_even = even[-1] + BETA * (odd[-2] + ALPHA * (even[-2] + even[-1]))
    down_even = even[0] + BETA * (odd[0] + ALPHA * (even[0] + even[1]))
    return (up_odd, up_even), (even[0], down_even)


def lift_planes(planes, below, above):
    even, odd = planes[0::2], planes[1::2]
    count = len(even)
    first_odd = below[0] + ALPHA * even[0]
    odd = [
        odd[i] + ALPHA * (even[i] + (even[i + 1] if i + 1 < count else above[0]))
        for i in range(count)
    ]
    first_even = below[1] + BETA * first_odd
    even = [
        even[i] + BETA * ((odd[i - 1] if i else first_odd) + odd[i])
        for i in range(count)
    ]
    last_even = above[1] + BETA * odd[-1]
    first_odd = first_odd + GAMMA * (first_even + even[0])
    odd = [
        odd[i] + GAMMA * (even[i] + (even[i + 1] if i + 1 < count else last_even))
        for i in range(count)
    ]
    even = [
        even[i] + DELTA * ((odd[i - 1] if i else first_odd) + odd[i])
        for i in range(count)
    ]
    return [e * LOW_SCALE for e in even], [o * HIGH_SCALE for o in odd]


def double_taps():
    low, high = {}, {}
    for k in range(-4, 5):
        for m in range(-4, 5):
            at = 2 * k + m
            low[at] = low.get(at, 0.0) + LOW_TAPS[k + 4] * LOW_TAPS[m + 4]
    for k in range(-3, 4):
        for m in range(-4, 5):
            at = 2 * (k + 1) + m
            high[at] = high.get(at, 0.0) + HIGH_TAPS[k + 3] * LOW_TAPS[m + 4]
    return low, high


def ring_distances(planes):
    reach = -(-max(double_taps()[0]) // planes)
    return [0] + [sign * step for step in range(1, reach + 1) for sign in (1, -1)]


def deep_share(planes, distance):
    count = len(planes)
    shares = []
    for taps in double_taps():
        terms = [
            planes[z] * taps[z - count * distance]
            for z in range(count)
            if z - count * distance in taps
        ]
        shares.append(functools.reduce(jnp.add, terms) if terms else jnp.zeros_like(planes[0]))
    return shares


def chunk_of(rows):
    for size in (16, 8):
        if rows % size == 0:
            return size
    return rows


def over_rows(rows, body):
    size = chunk_of(rows)

    def step(i, carry):
        body(pl.ds(pl.multiple_of(i * size, size), size))
        return carry

    lax.fori_loop(0, rows // size, step, 0)


def spread_rims(source, up_ref, down_ref, rows):
    planes = source.shape[0]

    def body(at):
        up, down = rim_sums([source[z, at, :] for z in range(planes)])
        for k in range(2):
            up_ref[k, at, :] = up[k]
            down_ref[k, at, :] = down[k]

    over_rows(rows, body)


def mark(ref):
    ref[...] = jnp.zeros_like(ref)


def rim_kernel(v_ref, w_ref, up_ref, down_ref, held, weights, raw, sems):
    planes, rows, _ = held.shape
    parts = sems.shape[0] - 1
    size = rows // parts
    copies = []
    for part in range(parts):
        at = pl.ds(part * size, size)
        copies.append(pltpu.make_async_copy(v_ref.at[:, at, :], held.at[:, at, :], sems.at[part]))
        copies[-1].start()
    weight_copy = pltpu.make_async_copy(w_ref, weights, sems.at[parts])
    weight_copy.start()
    for part in range(parts):
        copies[part].wait()

        def step(i, carry):
            at = pl.ds(pl.multiple_of(part * size + i * 8, 8), 8)
            up, down = rim_sums([held[z, at, :] for z in range(planes)])
            for k, value in enumerate(up + down):
                raw[k, at, :] = value
            return carry

        lax.fori_loop(0, size // 8, step, 0)
        if part == 0:
            weight_copy.wait()
        at = pl.ds(part * size, size)
        low = exact_dot(raw[:, at, :].reshape(4 * size, -1), weights)
        for k, ref in enumerate((up_ref, up_ref, down_ref, down_ref)):
            ref[k % 2, at, :] = low[k * size : (k + 1) * size]


def y_kernel(v_ref, w_low_ref, w_high_ref, low_ref, high_ref, up_ref, down_ref):
    planes, rows, width = v_ref.shape
    block = PLANES if planes % PLANES == 0 else 1

    def step(i, carry):
        at = pl.ds(i * block, block)
        flat = v_ref[at].reshape(block * rows, width)
        low_ref[at] = exact_dot(flat, w_low_ref).reshape(block, rows, width // 2)
        high = exact_dot(flat, w_high_ref).reshape(block, rows, width // 2)
        high_ref[at] = high
        up_ref[at] = high[:, rows - 8 :]
        down_ref[at] = high[:, :8]
        return carry

    lax.fori_loop(0, planes // block, step, 0)


def lift_in_scratch(scratch, pairs):
    even = scratch[pl.ds(0, pairs, stride=2), :]
    odd = scratch[pl.ds(1, pairs, stride=2), :]
    return lift_rows(even, odd)


def lane_tiles(width):
    size = min(width, LANES)
    return [pl.ds(k, size) for k in range(0, width, size)]


def x_high_kernel(
    y_ref, below_ref, above_ref, x_ref, up_ref, down_ref, mark_ref, scratch
):
    planes, rows, width = y_ref.shape
    half = rows // 2

    def step(z, carry):
        for tile, lanes in enumerate(lane_tiles(width)):
            part = scratch.at[tile]
            part[8:16] = below_ref[z, :, lanes]
            part[16 : 16 + rows] = y_ref[z, :, lanes]
            part[16 + rows : 24 + rows] = above_ref[z, :, lanes]
            low, high = lift_in_scratch(part, half + 16)
            x_ref[z, 0:half, lanes] = low[8 : 8 + half]
            x_ref[z, half:rows, lanes] = high[8 : 8 + half]
        return carry

    scratch[:, 0:8] = jnp.zeros_like(scratch[:, 0:8])
    scratch[:, 24 + rows :] = jnp.zeros_like(scratch[:, 24 + rows :])
    lax.fori_loop(0, planes, step, 0)
    spread_rims(x_ref, up_ref, down_ref, rows)
    mark(mark_ref)


LOW_BELOW, LOW_ABOVE = 32, 24


def lift_rows_of(y_ref, below_ref, above_ref, at):
    return lift_planes(
        [y_ref[z, at, :] for z in range(y_ref.shape[0])],
        [below_ref[k, at, :] for k in range(2)],
        [above_ref[k, at, :] for k in range(2)],
    )


def z_edge_kernel(y_ref, below_ref, above_ref, after_ref, up_ref, down_ref, mark_ref):
    del after_ref
    planes, rows, _ = y_ref.shape
    size = 8
    for start in range(0, LOW_ABOVE, size):
        low, high = lift_rows_of(y_ref, below_ref, above_ref, slice(start, start + size))
        for z in range(planes // 2):
            down_ref[z, start : start + size] = low[z]
            if start == 0:
                down_ref[z, LOW_ABOVE : LOW_ABOVE + size] = high[z]
    for start in range(0, LOW_BELOW, size):
        at = rows - LOW_BELOW + start
        low, high = lift_rows_of(y_ref, below_ref, above_ref, slice(at, at + size))
        for z in range(planes // 2):
            up_ref[z, start : start + size] = low[z]
            if start == LOW_BELOW - size:
                up_ref[z, LOW_BELOW : LOW_BELOW + size] = high[z]
    mark(mark_ref)


def z_lift_kernel(y_ref, below_ref, above_ref, after_ref, low_ref, high_ref):
    del after_ref
    planes, rows, _ = y_ref.shape

    def body(at):
        low, high = lift_rows_of(y_ref, below_ref, above_ref, at)
        for z in range(planes // 2):
            low_ref[z, at, :] = low[z]
            high_ref[z, at, :] = high[z]

    over_rows(rows, body)


def x_low_kernel(
    low_ref, below_ref, above_ref, w_two_ref, w_three_ref,
    part_ref, bands_ref, up_ref, down_ref, deep_planes, mark_ref,
    scratch, approx, split, deep_split,
):
    planes, rows, width = low_ref.shape
    half = rows // 2
    deep = (rows + 64) // 2
    quarter = half // 2
    eighth = quarter // 2

    def step(z, carry):
        for tile, lanes in enumerate(lane_tiles(width)):
            part = scratch.at[tile]
            part[0:LOW_BELOW] = below_ref[z, 0:LOW_BELOW, lanes]
            part[LOW_BELOW : LOW_BELOW + rows] = low_ref[z, :, lanes]
            top = LOW_BELOW + rows
            part[top : top + LOW_ABOVE] = above_ref[z, 0:LOW_ABOVE, lanes]
            low, high = lift_in_scratch(part, deep)
            approx[:, lanes] = low
            part_ref[0, z, :, lanes] = high[16 : 16 + half]
        whole = exact_dot(approx[...], w_two_ref)
        for tile in range(split.shape[1]):
            split[z, tile] = whole[:, tile * LANES : (tile + 1) * LANES]
        return carry

    scratch[:, rows + 32 :] = jnp.zeros_like(scratch[:, rows + 32 :])
    lax.fori_loop(0, planes, step, 0)
    span = deep // 2
    for z in range(planes):
        for y in range(2):
            low, high = lift_in_scratch(split.at[z, y], span)
            start = 2 * y * quarter
            bands_ref[z, start : start + quarter, :] = low[8 : 8 + quarter]
            bands_ref[z, start + quarter : start + 2 * quarter, :] = high[8 : 8 + quarter]
            if y == 0:
                deep_split[z] = exact_dot(low, w_three_ref)
    for z in range(planes):
        low, high = lift_in_scratch(deep_split.at[z], span // 2)
        deep_planes[z, 0:eighth, :] = low[4 : 4 + eighth]
        deep_planes[z, eighth:, :] = high[4 : 4 + eighth]
    packed = bands_ref.shape[1]
    spread_rims(bands_ref, up_ref, down_ref, packed)
    for distance, ref in ((1, up_ref), (-1, down_ref)):
        share = deep_share([deep_planes[z] for z in range(planes)], distance)
        for k in range(2):
            ref[k, packed:, :] = share[k]
    mark(mark_ref)


def own_kernel(deep_ref, own_ref, mark_ref):
    share = deep_share([deep_ref[z] for z in range(deep_ref.shape[0])], 0)
    for k in range(2):
        own_ref[k] = share[k]
    mark(mark_ref)


def far_kernel(deep_ref, keep_ref, give_ref, held):
    planes = [deep_ref[z] for z in range(deep_ref.shape[0])]
    core = lax.rem(lax.axis_index("gx"), 2)
    for step in range(keep_ref.shape[0]):
        for sign, slot in ((1, core), (-1, 1 - core)):
            share = deep_share(planes, sign * (step + 2))
            for k in range(2):
                held[slot, step, k] = share[k]
    keep_ref[...] = held[0]
    give_ref[...] = held[1]


def pack_kernel(keep_ref, got_ref, after_ref, *out_refs):
    del after_ref
    for step, ref in enumerate(out_refs):
        ref[0] = keep_ref[step]
        ref[1] = got_ref[step]


def sum_kernel(*refs):
    *far_refs, after_ref, mine_ref, other_ref = refs
    del after_ref
    total = functools.reduce(jnp.add, [ref[...] for ref in far_refs])
    mine_ref[...] = total[0]
    other_ref[...] = total[1]


def x_detail_kernel(
    part_ref, high_ref, below_ref, above_ref, detail_ref, mark_ref, scratch, held, sems
):
    planes, rows, width = high_ref.shape
    half = rows // 2
    copies = [pltpu.make_async_copy(part_ref, detail_ref.at[1:2], sems.at[0])]
    copies[0].start()
    scratch[:, 0:8] = jnp.zeros_like(scratch[:, 0:8])
    scratch[:, rows + 24 :] = jnp.zeros_like(scratch[:, rows + 24 :])

    def step(z, carry):
        for tile, lanes in enumerate(lane_tiles(width)):
            part = scratch.at[tile]
            part[8:16] = below_ref[z, LOW_BELOW : LOW_BELOW + 8, lanes]
            part[16 : 16 + rows] = high_ref[z, :, lanes]
            part[16 + rows : 24 + rows] = above_ref[z, LOW_ABOVE : LOW_ABOVE + 8, lanes]
            low, high = lift_in_scratch(part, half + 16)
            held[0, z, :, lanes] = low[8 : 8 + half]
            held[1, z, :, lanes] = high[8 : 8 + half]
        return carry

    lax.fori_loop(0, planes, step, 0)
    for k in range(2):
        copies.append(
            pltpu.make_async_copy(
                held.at[k : k + 1], detail_ref.at[2 * k : 2 * k + 1], sems.at[1 + k]
            )
        )
        copies[-1].start()
    for copy in copies:
        copy.wait()
    mark(mark_ref)


def z_high_kernel(x_ref, below_ref, above_ref, whole_ref, after_ref, detail_ref, held, sems):
    del whole_ref, after_ref
    planes, rows, _ = x_ref.shape
    half = rows // 2
    copies = []
    for xb in range(2):

        def body(at):
            here = pl.ds(at.start + xb * half, at.size)
            low, high = lift_rows_of(x_ref, below_ref, above_ref, here)
            for z in range(planes // 2):
                held[2 * xb, z, at, :] = low[z]
                held[2 * xb + 1, z, at, :] = high[z]

        over_rows(half, body)
        copies.append(
            pltpu.make_async_copy(
                held.at[pl.ds(2 * xb, 2)], detail_ref.at[pl.ds(3 + 2 * xb, 2)], sems.at[xb]
            )
        )
        copies[-1].start()
    for copy in copies:
        copy.wait()


def z_middle_kernel(
    bands_ref, below_ref, above_ref, own_ref, far_ref, back_ref,
    detail_ref, deep_ref, coarse_ref, low_ref, high_ref,
):
    planes, rows, _ = bands_ref.shape
    kept = planes // 2
    quarter = detail_ref.shape[2]

    def body(at):
        low, high = lift_planes(
            [bands_ref[z, at, :] for z in range(planes)],
            [below_ref[k, at, :] for k in range(2)],
            [above_ref[k, at, :] for k in range(2)],
        )
        for z in range(kept):
            low_ref[z, at, :] = low[z]
            high_ref[z, at, :] = high[z]

    over_rows(rows, body)
    for z in range(kept):
        for band in range(1, 8):
            source = high_ref if band % 2 else low_ref
            start = quarter * (band // 2)
            detail_ref[band - 1, z] = source[z, start : start + quarter, :]
    height, width = coarse_ref.shape[1:]
    shares = (
        own_ref, below_ref.at[:, rows:, :], above_ref.at[:, rows:, :], far_ref, back_ref
    )
    low, high = (
        functools.reduce(jnp.add, [ref[k] for ref in shares])
        for k in range(2)
    )
    coarse_ref[0] = low[0:height, 0:width]
    for band in range(1, 8):
        value = high if band % 2 else low
        xb, yb = (band // 2) % 2, band // 4
        deep_ref[band - 1, 0] = value[
            xb * height : (xb + 1) * height, yb * width : (yb + 1) * width
        ]


def call(
    kernel, out_shapes, inputs, scratch=(), anywhere=(), aliases=None, open_inputs=(), scalars=(), cost=1
):
    whole = pl.BlockSpec(memory_space=pltpu.VMEM)
    unplaced = pl.BlockSpec(memory_space=pl.ANY)
    small = pl.BlockSpec(memory_space=pltpu.SMEM)
    return pl.pallas_call(
        kernel,
        out_shape=[
            jax.ShapeDtypeStruct(s, jnp.float32)
            if isinstance(s, tuple)
            else jax.ShapeDtypeStruct(s.shape, s.dtype)
            for s in out_shapes
        ],
        in_specs=[
            unplaced if i in open_inputs else small if i in scalars else whole
            for i in range(len(inputs))
        ],
        out_specs=[unplaced if i in anywhere else whole for i in range(len(out_shapes))],
        scratch_shapes=list(scratch),
        input_output_aliases=aliases or {},
        cost_estimate=pl.CostEstimate(flops=cost, bytes_accessed=cost, transcendentals=0),
        compiler_params=pltpu.CompilerParams(vmem_limit_bytes=24 * 2**20),
        name=kernel.__name__,
    )(*inputs)


def on_device(velocity):
    planes, rows, width = velocity.shape
    half_width = width // 2
    half = rows // 2
    quarter = half // 2
    tiles = half_width // LANES
    f32 = jnp.float32
    matrix = band_matrix(width)
    w_low = jnp.asarray(three_parts(matrix[:, :half_width]))
    w_high = jnp.asarray(three_parts(matrix[:, half_width:]))
    w_two = jnp.asarray(three_parts(band_matrix(half_width)))
    w_three = jnp.asarray(three_parts(band_matrix(half_width // 2)))

    whole = (planes, rows, half_width)
    rims = (2, rows, half_width)
    up, down, held, weights = call(
        rim_kernel,
        [rims, rims, velocity.shape, w_low],
        [
            pltpu.with_memory_space_constraint(velocity, pltpu.HBM),
            pltpu.with_memory_space_constraint(w_low, pltpu.HBM),
        ],
        [
            pltpu.VMEM((4, rows, width), f32),
            pltpu.SemaphoreType.DMA((PARTS + 1,)),
        ],
        open_inputs=(0, 1),
    )
    low_below, low_above = shifted(up, "gz", 1), shifted(down, "gz", -1)

    edge = (planes, 8, half_width)
    y_low, y_high, up, down = call(
        y_kernel, [whole, whole, edge, edge], [held, weights, w_high]
    )
    below, above = shifted(up, "gx", 1), shifted(down, "gx", -1)
    x_high, up, down, mark_high = call(
        x_high_kernel,
        [whole, rims, rims, MARK],
        [y_high, below, above],
        [pltpu.VMEM((tiles, rows + 32, LANES), f32)],
    )
    high_below, high_above = shifted(up, "gz", 1), shifted(down, "gz", -1)

    kept = (planes // 2, rows, half_width)
    up, down, mark_edge = call(
        z_edge_kernel,
        [
            (planes // 2, LOW_BELOW + 8, half_width),
            (planes // 2, LOW_ABOVE + 8, half_width),
            MARK,
        ],
        [y_low, low_below, low_above, mark_high],
    )
    edge_below, edge_above = shifted(up, "gx", 1), shifted(down, "gx", -1)
    z_low, z_high = call(
        z_lift_kernel, [kept, kept], [y_low, low_below, low_above, mark_edge], cost=GAP
    )
    deep = (rows + 64) // 2
    packed = 4 * quarter
    eighth = quarter // 2
    lanes = half_width // 2
    detail_shape = (7, planes // 2, half, half_width)
    middle = (2, packed + 2 * eighth, lanes)
    share = (2, 2 * eighth, lanes)
    steps = max(ring_distances(planes // 2)) - 1
    part, bands, up, down, deep_planes, mark_low = call(
        x_low_kernel,
        [
            (1,) + detail_shape[1:],
            (planes // 2, packed, lanes),
            middle,
            middle,
            (planes // 2, 2 * eighth, lanes),
            MARK,
        ],
        [z_low, edge_below, edge_above, w_two, w_three],
        [
            pltpu.VMEM((tiles, rows + 64, LANES), f32),
            pltpu.VMEM((deep, half_width), f32),
            pltpu.VMEM((planes // 2, tiles, deep, LANES), f32),
            pltpu.VMEM((planes // 2, deep // 2, lanes), f32),
        ],
    )
    detail_one, mark_detail = call(
        x_detail_kernel,
        [detail_shape, MARK],
        [part, z_high, edge_below, edge_above],
        [
            pltpu.VMEM((tiles, rows + 32, LANES), f32),
            pltpu.VMEM((2,) + detail_shape[1:], f32),
            pltpu.SemaphoreType.DMA((3,)),
        ],
        anywhere=(0,),
        cost=GAP_DETAIL,
    )
    below, above = shifted(up, "gz", 1), shifted(down, "gz", -1)
    keep, give = call(
        far_kernel,
        [(steps,) + share] * 2,
        [deep_planes],
        [pltpu.VMEM((2, steps) + share, f32)],
    )
    own, mark_own = call(own_kernel, [share, MARK], [deep_planes], cost=GAP_OWN)
    both = call(pack_kernel, [(2,) + share] * steps, [keep, other_core(give), mark_own])
    both = [shifted_by_core(part, k + 2) for k, part in enumerate(both)]
    far, back = call(sum_kernel, [share] * 2, [*both, mark_detail])
    back = other_core(back)
    (detail_one,) = call(
        z_high_kernel,
        [detail_shape],
        [x_high, high_below, high_above, detail_one, mark_low],
        [pltpu.VMEM((4,) + detail_shape[1:], f32), pltpu.SemaphoreType.DMA((2,))],
        anywhere=(0,),
        aliases={3: 0},
        open_inputs=(3,),
    )
    last = planes // 4
    detail_two, detail_three, coarse = call(
        z_middle_kernel,
        [
            (7, last, quarter, lanes),
            (7, 1, eighth, lanes // 2),
            (1, eighth, lanes // 2),
        ],
        [bands, below, above, own, far, back],
        [pltpu.VMEM((last, packed, lanes), f32)] * 2,
    )
    return detail_one, detail_two, detail_three, coarse


def solution(mesh):
    placed = (P("gz", "gx", None),)
    return jax.shard_map(
        on_device,
        mesh=mesh,
        in_specs=placed,
        out_specs=(
            P(None, "gz", "gx", None),
            P(None, "gz", "gx", None),
            P(None, "gz", "gx", None),
            P("gz", "gx", None),
        ),
        check_vma=False,
    )
```

```python
import functools

import jax
import jax.numpy as jnp
import numpy as np
from jax import lax
from jax.experimental import pallas as pl
from jax.experimental.pallas import tpu as pltpu
from jax.sharding import PartitionSpec as P

LEVELS = 3
GAP = 1
GAP_OWN = 1
GAP_DETAIL = 1
PLANES = 4
PARTS = 1
MARK = (8, 128)
LANES = 128

LOW_TAPS = (
    0.026748757411,
    -0.016864118443,
    -0.078223266529,
    0.266864118443,
    0.602949018236,
    0.266864118443,
    -0.078223266529,
    -0.016864118443,
    0.026748757411,
)
HIGH_TAPS = (
    0.091271763114,
    -0.057543526229,
    -0.591271763114,
    1.115087052457,
    -0.591271763114,
    -0.057543526229,
    0.091271763114,
)

ALPHA = -1.586134342059924
BETA = -0.052980118572961
GAMMA = 0.882911075530934
DELTA = 0.443506852043971
LOW_SCALE = 0.812893066115961
HIGH_SCALE = 1.230174104914001


def shifted(value, axis, steps):
    count = lax.axis_size(axis)
    pairs = [(source, (source + steps) % count) for source in range(count)]
    return lax.ppermute(value, axis, pairs)


def other_core(value):
    count = lax.axis_size("gx")
    return lax.ppermute(value, "gx", [(source, source ^ 1) for source in range(count)])


def shifted_by_core(value, steps):
    high, wide = lax.axis_size("gz"), lax.axis_size("gx")
    pairs = [
        (z * wide + x, ((z + (-steps if x % 2 else steps)) % high) * wide + x)
        for z in range(high)
        for x in range(wide)
    ]
    return lax.ppermute(value, ("gz", "gx"), pairs)


def band_matrix(length):
    half = length // 2
    matrix = np.zeros((length, length), np.float64)
    for j in range(half):
        for k in range(-4, 5):
            matrix[(2 * j + k) % length, j] += LOW_TAPS[k + 4]
        for k in range(-3, 4):
            matrix[(2 * j + 1 + k) % length, half + j] += HIGH_TAPS[k + 3]
    return matrix


def three_parts(matrix):
    parts = []
    rest = matrix
    for _ in range(3):
        part = rest.astype(np.float32).astype(jnp.bfloat16)
        parts.append(part)
        rest = rest - part.astype(np.float64)
    return np.stack(parts)


def exact_dot(value, parts):
    first = value.astype(jnp.bfloat16)
    rest = value - first.astype(jnp.float32)
    second = rest.astype(jnp.bfloat16)
    third = (rest - second.astype(jnp.float32)).astype(jnp.bfloat16)

    count = value.shape[0]

    def dot(parts_of_value, part):
        rows = jnp.concatenate(parts_of_value, 0)
        result = jnp.dot(rows, part, preferred_element_type=jnp.float32)
        return [result[k * count : (k + 1) * count] for k in range(len(parts_of_value))]

    large, middle, small = dot([first, second, third], parts[0])
    middle_too, small_too = dot([first, second], parts[1])
    (small_last,) = dot([first], parts[2])
    return large + ((middle + middle_too) + (small + small_too + small_last))


def lift_rows(even, odd):
    count = even.shape[0]

    def after(a):
        return pltpu.roll(a, count - 1, 0)

    def before(a):
        return pltpu.roll(a, 1, 0)

    odd = odd + ALPHA * (even + after(even))
    even = even + BETA * (before(odd) + odd)
    odd = odd + GAMMA * (even + after(even))
    even = even + DELTA * (before(odd) + odd)
    return even * LOW_SCALE, odd * HIGH_SCALE


def rim_sums(planes):
    even, odd = planes[0::2], planes[1::2]
    up_odd = odd[-1] + ALPHA * even[-1]
    up_even = even[-1] + BETA * (odd[-2] + ALPHA * (even[-2] + even[-1]))
    down_even = even[0] + BETA * (odd[0] + ALPHA * (even[0] + even[1]))
    return (up_odd, up_even), (even[0], down_even)


def lift_planes(planes, below, above):
    even, odd = planes[0::2], planes[1::2]
    count = len(even)
    first_odd = below[0] + ALPHA * even[0]
    odd = [
        odd[i] + ALPHA * (even[i] + (even[i + 1] if i + 1 < count else above[0]))
        for i in range(count)
    ]
    first_even = below[1] + BETA * first_odd
    even = [
        even[i] + BETA * ((odd[i - 1] if i else first_odd) + odd[i])
        for i in range(count)
    ]
    last_even = above[1] + BETA * odd[-1]
    first_odd = first_odd + GAMMA * (first_even + even[0])
    odd = [
        odd[i] + GAMMA * (even[i] + (even[i + 1] if i + 1 < count else last_even))
        for i in range(count)
    ]
    even = [
        even[i] + DELTA * ((odd[i - 1] if i else first_odd) + odd[i])
        for i in range(count)
    ]
    return [e * LOW_SCALE for e in even], [o * HIGH_SCALE for o in odd]


def double_taps():
    low, high = {}, {}
    for k in range(-4, 5):
        for m in range(-4, 5):
            at = 2 * k + m
            low[at] = low.get(at, 0.0) + LOW_TAPS[k + 4] * LOW_TAPS[m + 4]
    for k in range(-3, 4):
        for m in range(-4, 5):
            at = 2 * (k + 1) + m
            high[at] = high.get(at, 0.0) + HIGH_TAPS[k + 3] * LOW_TAPS[m + 4]
    return low, high


def ring_distances(planes):
    reach = -(-max(double_taps()[0]) // planes)
    return [0] + [sign * step for step in range(1, reach + 1) for sign in (1, -1)]


def deep_share(planes, distance):
    count = len(planes)
    shares = []
    for taps in double_taps():
        terms = [
            planes[z] * taps[z - count * distance]
            for z in range(count)
            if z - count * distance in taps
        ]
        shares.append(functools.reduce(jnp.add, terms) if terms else jnp.zeros_like(planes[0]))
    return shares


def single_plane(planes, distance):
    low, high = (
        [taps.get(z - planes * distance, 0.0) for z in range(planes)] for taps in double_taps()
    )
    if not any(high):
        return 0.0
    if sum(1 for pair in zip(low, high, strict=True) if any(pair)) == 1 and any(low):
        return sum(high) / sum(low)
    return None


def far_steps(planes):
    steps = []
    for distance in range(2, max(ring_distances(planes)) + 1):
        ratios = [single_plane(planes, sign * distance) for sign in (1, -1)]
        steps.append((distance, 2 if None in ratios else 1, ratios))
    return steps


def chunk_of(rows):
    for size in (16, 8):
        if rows % size == 0:
            return size
    return rows


def over_rows(rows, body):
    size = chunk_of(rows)

    def step(i, carry):
        body(pl.ds(pl.multiple_of(i * size, size), size))
        return carry

    lax.fori_loop(0, rows // size, step, 0)


def spread_rims(source, up_ref, down_ref, rows):
    planes = source.shape[0]

    def body(at):
        up, down = rim_sums([source[z, at, :] for z in range(planes)])
        for k in range(2):
            up_ref[k, at, :] = up[k]
            down_ref[k, at, :] = down[k]

    over_rows(rows, body)


def mark(ref):
    ref[...] = jnp.zeros_like(ref)


def rim_kernel(v_ref, w_ref, up_ref, down_ref, held, weights, raw, sems):
    planes, rows, _ = held.shape
    parts = sems.shape[0] - 1
    size = rows // parts
    copies = []
    for part in range(parts):
        at = pl.ds(part * size, size)
        copies.append(pltpu.make_async_copy(v_ref.at[:, at, :], held.at[:, at, :], sems.at[part]))
        copies[-1].start()
    weight_copy = pltpu.make_async_copy(w_ref, weights, sems.at[parts])
    weight_copy.start()
    for part in range(parts):
        copies[part].wait()

        def step(i, carry):
            at = pl.ds(pl.multiple_of(part * size + i * 8, 8), 8)
            up, down = rim_sums([held[z, at, :] for z in range(planes)])
            for k, value in enumerate(up + down):
                raw[k, at, :] = value
            return carry

        lax.fori_loop(0, size // 8, step, 0)
        if part == 0:
            weight_copy.wait()
        at = pl.ds(part * size, size)
        low = exact_dot(raw[:, at, :].reshape(4 * size, -1), weights)
        for k, ref in enumerate((up_ref, up_ref, down_ref, down_ref)):
            ref[k % 2, at, :] = low[k * size : (k + 1) * size]


def y_kernel(v_ref, w_low_ref, w_high_ref, low_ref, high_ref, up_ref, down_ref):
    planes, rows, width = v_ref.shape
    block = PLANES if planes % PLANES == 0 else 1

    def step(i, carry):
        at = pl.ds(i * block, block)
        flat = v_ref[at].reshape(block * rows, width)
        low_ref[at] = exact_dot(flat, w_low_ref).reshape(block, rows, width // 2)
        high = exact_dot(flat, w_high_ref).reshape(block, rows, width // 2)
        high_ref[at] = high
        up_ref[at] = high[:, rows - 8 :]
        down_ref[at] = high[:, :8]
        return carry

    lax.fori_loop(0, planes // block, step, 0)


def lift_in_scratch(scratch, pairs):
    even = scratch[pl.ds(0, pairs, stride=2), :]
    odd = scratch[pl.ds(1, pairs, stride=2), :]
    return lift_rows(even, odd)


def lane_tiles(width):
    size = min(width, LANES)
    return [pl.ds(k, size) for k in range(0, width, size)]


def x_high_kernel(
    y_ref, below_ref, above_ref, x_ref, up_ref, down_ref, mark_ref, scratch
):
    planes, rows, width = y_ref.shape
    half = rows // 2

    def step(z, carry):
        for tile, lanes in enumerate(lane_tiles(width)):
            part = scratch.at[tile]
            part[8:16] = below_ref[z, :, lanes]
            part[16 : 16 + rows] = y_ref[z, :, lanes]
            part[16 + rows : 24 + rows] = above_ref[z, :, lanes]
            low, high = lift_in_scratch(part, half + 16)
            x_ref[z, 0:half, lanes] = low[8 : 8 + half]
            x_ref[z, half:rows, lanes] = high[8 : 8 + half]
        return carry

    scratch[:, 0:8] = jnp.zeros_like(scratch[:, 0:8])
    scratch[:, 24 + rows :] = jnp.zeros_like(scratch[:, 24 + rows :])
    lax.fori_loop(0, planes, step, 0)
    spread_rims(x_ref, up_ref, down_ref, rows)
    mark(mark_ref)


LOW_BELOW, LOW_ABOVE = 32, 24


def lift_rows_of(y_ref, below_ref, above_ref, at):
    return lift_planes(
        [y_ref[z, at, :] for z in range(y_ref.shape[0])],
        [below_ref[k, at, :] for k in range(2)],
        [above_ref[k, at, :] for k in range(2)],
    )


def z_edge_kernel(y_ref, below_ref, above_ref, after_ref, up_ref, down_ref, mark_ref):
    del after_ref
    planes, rows, _ = y_ref.shape
    size = 8
    for start in range(0, LOW_ABOVE, size):
        low, high = lift_rows_of(y_ref, below_ref, above_ref, slice(start, start + size))
        for z in range(planes // 2):
            down_ref[z, start : start + size] = low[z]
            if start == 0:
                down_ref[z, LOW_ABOVE : LOW_ABOVE + size] = high[z]
    for start in range(0, LOW_BELOW, size):
        at = rows - LOW_BELOW + start
        low, high = lift_rows_of(y_ref, below_ref, above_ref, slice(at, at + size))
        for z in range(planes // 2):
            up_ref[z, start : start + size] = low[z]
            if start == LOW_BELOW - size:
                up_ref[z, LOW_BELOW : LOW_BELOW + size] = high[z]
    mark(mark_ref)


def z_lift_kernel(y_ref, below_ref, above_ref, after_ref, low_ref, high_ref):
    del after_ref
    planes, rows, _ = y_ref.shape

    def body(at):
        low, high = lift_rows_of(y_ref, below_ref, above_ref, at)
        for z in range(planes // 2):
            low_ref[z, at, :] = low[z]
            high_ref[z, at, :] = high[z]

    over_rows(rows, body)


def x_low_kernel(
    low_ref, below_ref, above_ref, w_two_ref, w_three_ref,
    part_ref, bands_ref, up_ref, down_ref, deep_planes, mark_ref,
    scratch, approx, split, deep_split,
):
    planes, rows, width = low_ref.shape
    half = rows // 2
    deep = (rows + 64) // 2
    quarter = half // 2
    eighth = quarter // 2

    def step(z, carry):
        for tile, lanes in enumerate(lane_tiles(width)):
            part = scratch.at[tile]
            part[0:LOW_BELOW] = below_ref[z, 0:LOW_BELOW, lanes]
            part[LOW_BELOW : LOW_BELOW + rows] = low_ref[z, :, lanes]
            top = LOW_BELOW + rows
            part[top : top + LOW_ABOVE] = above_ref[z, 0:LOW_ABOVE, lanes]
            low, high = lift_in_scratch(part, deep)
            approx[:, lanes] = low
            part_ref[0, z, :, lanes] = high[16 : 16 + half]
        whole = exact_dot(approx[...], w_two_ref)
        for tile in range(split.shape[1]):
            split[z, tile] = whole[:, tile * LANES : (tile + 1) * LANES]
        return carry

    scratch[:, rows + 32 :] = jnp.zeros_like(scratch[:, rows + 32 :])
    lax.fori_loop(0, planes, step, 0)
    span = deep // 2
    for z in range(planes):
        for y in range(2):
            low, high = lift_in_scratch(split.at[z, y], span)
            start = 2 * y * quarter
            bands_ref[z, start : start + quarter, :] = low[8 : 8 + quarter]
            bands_ref[z, start + quarter : start + 2 * quarter, :] = high[8 : 8 + quarter]
            if y == 0:
                deep_split[z] = exact_dot(low, w_three_ref)
    for z in range(planes):
        low, high = lift_in_scratch(deep_split.at[z], span // 2)
        deep_planes[z, 0:eighth, :] = low[4 : 4 + eighth]
        deep_planes[z, eighth:, :] = high[4 : 4 + eighth]
    packed = bands_ref.shape[1]
    spread_rims(bands_ref, up_ref, down_ref, packed)
    for distance, ref in ((1, up_ref), (-1, down_ref)):
        share = deep_share([deep_planes[z] for z in range(planes)], distance)
        for k in range(2):
            ref[k, packed:, :] = share[k]
    mark(mark_ref)


def own_kernel(deep_ref, own_ref, mark_ref):
    share = deep_share([deep_ref[z] for z in range(deep_ref.shape[0])], 0)
    for k in range(2):
        own_ref[k] = share[k]
    mark(mark_ref)


def far_kernel(deep_ref, keep_ref, give_ref, held):
    planes = [deep_ref[z] for z in range(deep_ref.shape[0])]
    core = lax.rem(lax.axis_index("gx"), 2)
    at = 0
    for distance, count, _ in far_steps(len(planes)):
        for sign, slot in ((1, core), (-1, 1 - core)):
            share = deep_share(planes, sign * distance)
            for k in range(count):
                held[slot, at + k] = share[k]
        at = at + count
    keep_ref[...] = held[0]
    give_ref[...] = held[1]


def pack_kernel(first, keep_ref, got_ref, after_ref, out_ref):
    del after_ref
    for k in range(out_ref.shape[1]):
        out_ref[0, k] = keep_ref[first + k]
        out_ref[1, k] = got_ref[first + k]


def sum_kernel(planes, *refs):
    *far_refs, after_ref, mine_ref, other_ref = refs
    del after_ref
    core = lax.rem(lax.axis_index("gx"), 2)
    for owner, out_ref in enumerate((mine_ref, other_ref)):
        low = jnp.zeros_like(out_ref[0])
        high = jnp.zeros_like(low)
        for ref, (_, count, ratios) in zip(far_refs, far_steps(planes), strict=True):
            part = ref[owner, 0]
            low = low + part
            if count == 1:
                high = high + part * jnp.where(core == 0, *map(jnp.float32, ratios))
            else:
                high = high + ref[owner, 1]
        out_ref[0] = low
        out_ref[1] = high


def x_detail_kernel(
    part_ref, high_ref, below_ref, above_ref, detail_ref, mark_ref, scratch, held, sems
):
    planes, rows, width = high_ref.shape
    half = rows // 2
    copies = [pltpu.make_async_copy(part_ref, detail_ref.at[1:2], sems.at[0])]
    copies[0].start()
    scratch[:, 0:8] = jnp.zeros_like(scratch[:, 0:8])
    scratch[:, rows + 24 :] = jnp.zeros_like(scratch[:, rows + 24 :])

    def step(z, carry):
        for tile, lanes in enumerate(lane_tiles(width)):
            part = scratch.at[tile]
            part[8:16] = below_ref[z, LOW_BELOW : LOW_BELOW + 8, lanes]
            part[16 : 16 + rows] = high_ref[z, :, lanes]
            part[16 + rows : 24 + rows] = above_ref[z, LOW_ABOVE : LOW_ABOVE + 8, lanes]
            low, high = lift_in_scratch(part, half + 16)
            held[0, z, :, lanes] = low[8 : 8 + half]
            held[1, z, :, lanes] = high[8 : 8 + half]
        return carry

    lax.fori_loop(0, planes, step, 0)
    for k in range(2):
        copies.append(
            pltpu.make_async_copy(
                held.at[k : k + 1], detail_ref.at[2 * k : 2 * k + 1], sems.at[1 + k]
            )
        )
        copies[-1].start()
    for copy in copies:
        copy.wait()
    mark(mark_ref)


def z_high_kernel(x_ref, below_ref, above_ref, whole_ref, after_ref, detail_ref, held, sems):
    del whole_ref, after_ref
    planes, rows, _ = x_ref.shape
    half = rows // 2
    copies = []
    for xb in range(2):

        def body(at):
            here = pl.ds(at.start + xb * half, at.size)
            low, high = lift_rows_of(x_ref, below_ref, above_ref, here)
            for z in range(planes // 2):
                held[2 * xb, z, at, :] = low[z]
                held[2 * xb + 1, z, at, :] = high[z]

        over_rows(half, body)
        copies.append(
            pltpu.make_async_copy(
                held.at[pl.ds(2 * xb, 2)], detail_ref.at[pl.ds(3 + 2 * xb, 2)], sems.at[xb]
            )
        )
        copies[-1].start()
    for copy in copies:
        copy.wait()


def z_middle_kernel(
    bands_ref, below_ref, above_ref, own_ref, far_ref, back_ref,
    detail_ref, deep_ref, coarse_ref, low_ref, high_ref,
):
    planes, rows, _ = bands_ref.shape
    kept = planes // 2
    quarter = detail_ref.shape[2]

    def body(at):
        low, high = lift_planes(
            [bands_ref[z, at, :] for z in range(planes)],
            [below_ref[k, at, :] for k in range(2)],
            [above_ref[k, at, :] for k in range(2)],
        )
        for z in range(kept):
            low_ref[z, at, :] = low[z]
            high_ref[z, at, :] = high[z]

    over_rows(rows, body)
    for z in range(kept):
        for band in range(1, 8):
            source = high_ref if band % 2 else low_ref
            start = quarter * (band // 2)
            detail_ref[band - 1, z] = source[z, start : start + quarter, :]
    height, width = coarse_ref.shape[1:]
    shares = (
        own_ref, below_ref.at[:, rows:, :], above_ref.at[:, rows:, :], far_ref, back_ref
    )
    low, high = (
        functools.reduce(jnp.add, [ref[k] for ref in shares])
        for k in range(2)
    )
    coarse_ref[0] = low[0:height, 0:width]
    for band in range(1, 8):
        value = high if band % 2 else low
        xb, yb = (band // 2) % 2, band // 4
        deep_ref[band - 1, 0] = value[
            xb * height : (xb + 1) * height, yb * width : (yb + 1) * width
        ]


def call(
    kernel, out_shapes, inputs, scratch=(), anywhere=(), aliases=None, open_inputs=(), scalars=(), cost=1
):
    whole = pl.BlockSpec(memory_space=pltpu.VMEM)
    unplaced = pl.BlockSpec(memory_space=pl.ANY)
    small = pl.BlockSpec(memory_space=pltpu.SMEM)
    return pl.pallas_call(
        kernel,
        out_shape=[
            jax.ShapeDtypeStruct(s, jnp.float32)
            if isinstance(s, tuple)
            else jax.ShapeDtypeStruct(s.shape, s.dtype)
            for s in out_shapes
        ],
        in_specs=[
            unplaced if i in open_inputs else small if i in scalars else whole
            for i in range(len(inputs))
        ],
        out_specs=[unplaced if i in anywhere else whole for i in range(len(out_shapes))],
        scratch_shapes=list(scratch),
        input_output_aliases=aliases or {},
        cost_estimate=pl.CostEstimate(flops=cost, bytes_accessed=cost, transcendentals=0),
        compiler_params=pltpu.CompilerParams(vmem_limit_bytes=24 * 2**20),
        name=getattr(kernel, "func", kernel).__name__,
    )(*inputs)


def on_device(velocity):
    planes, rows, width = velocity.shape
    half_width = width // 2
    half = rows // 2
    quarter = half // 2
    tiles = half_width // LANES
    f32 = jnp.float32
    matrix = band_matrix(width)
    w_low = jnp.asarray(three_parts(matrix[:, :half_width]))
    w_high = jnp.asarray(three_parts(matrix[:, half_width:]))
    w_two = jnp.asarray(three_parts(band_matrix(half_width)))
    w_three = jnp.asarray(three_parts(band_matrix(half_width // 2)))

    whole = (planes, rows, half_width)
    rims = (2, rows, half_width)
    up, down, held, weights = call(
        rim_kernel,
        [rims, rims, velocity.shape, w_low],
        [
            pltpu.with_memory_space_constraint(velocity, pltpu.HBM),
            pltpu.with_memory_space_constraint(w_low, pltpu.HBM),
        ],
        [
            pltpu.VMEM((4, rows, width), f32),
            pltpu.SemaphoreType.DMA((PARTS + 1,)),
        ],
        open_inputs=(0, 1),
    )
    low_below, low_above = shifted(up, "gz", 1), shifted(down, "gz", -1)

    edge = (planes, 8, half_width)
    y_low, y_high, up, down = call(
        y_kernel, [whole, whole, edge, edge], [held, weights, w_high]
    )
    below, above = shifted(up, "gx", 1), shifted(down, "gx", -1)
    x_high, up, down, mark_high = call(
        x_high_kernel,
        [whole, rims, rims, MARK],
        [y_high, below, above],
        [pltpu.VMEM((tiles, rows + 32, LANES), f32)],
    )
    high_below, high_above = shifted(up, "gz", 1), shifted(down, "gz", -1)

    kept = (planes // 2, rows, half_width)
    up, down, mark_edge = call(
        z_edge_kernel,
        [
            (planes // 2, LOW_BELOW + 8, half_width),
            (planes // 2, LOW_ABOVE + 8, half_width),
            MARK,
        ],
        [y_low, low_below, low_above, mark_high],
    )
    edge_below, edge_above = shifted(up, "gx", 1), shifted(down, "gx", -1)
    z_low, z_high = call(
        z_lift_kernel, [kept, kept], [y_low, low_below, low_above, mark_edge], cost=GAP
    )
    deep = (rows + 64) // 2
    packed = 4 * quarter
    eighth = quarter // 2
    lanes = half_width // 2
    detail_shape = (7, planes // 2, half, half_width)
    middle = (2, packed + 2 * eighth, lanes)
    share = (2, 2 * eighth, lanes)
    steps = far_steps(planes // 2)
    part, bands, up, down, deep_planes, mark_low = call(
        x_low_kernel,
        [
            (1,) + detail_shape[1:],
            (planes // 2, packed, lanes),
            middle,
            middle,
            (planes // 2, 2 * eighth, lanes),
            MARK,
        ],
        [z_low, edge_below, edge_above, w_two, w_three],
        [
            pltpu.VMEM((tiles, rows + 64, LANES), f32),
            pltpu.VMEM((deep, half_width), f32),
            pltpu.VMEM((planes // 2, tiles, deep, LANES), f32),
            pltpu.VMEM((planes // 2, deep // 2, lanes), f32),
        ],
    )
    detail_one, mark_detail = call(
        x_detail_kernel,
        [detail_shape, MARK],
        [part, z_high, edge_below, edge_above],
        [
            pltpu.VMEM((tiles, rows + 32, LANES), f32),
            pltpu.VMEM((2,) + detail_shape[1:], f32),
            pltpu.SemaphoreType.DMA((3,)),
        ],
        anywhere=(0,),
        cost=GAP_DETAIL,
    )
    below, above = shifted(up, "gz", 1), shifted(down, "gz", -1)
    sent = (sum(count for _, count, _ in steps),) + share[1:]
    keep, give = call(
        far_kernel, [sent, sent], [deep_planes], [pltpu.VMEM((2,) + sent, f32)]
    )
    own, mark_own = call(own_kernel, [share, MARK], [deep_planes], cost=GAP_OWN)
    got = other_core(give)
    both = []
    first = 0
    for distance, count, _ in steps:
        after = mark_own if distance == steps[-1][0] else high_below
        (packed_share,) = call(
            functools.partial(pack_kernel, first), [(2, count) + share[1:]], [keep, got, after]
        )
        both.append(shifted_by_core(packed_share, distance))
        first = first + count
    far, back = call(
        functools.partial(sum_kernel, planes // 2), [share] * 2, [*both, mark_detail]
    )
    back = other_core(back)
    (detail_one,) = call(
        z_high_kernel,
        [detail_shape],
        [x_high, high_below, high_above, detail_one, mark_low],
        [pltpu.VMEM((4,) + detail_shape[1:], f32), pltpu.SemaphoreType.DMA((2,))],
        anywhere=(0,),
        aliases={3: 0},
        open_inputs=(3,),
    )
    last = planes // 4
    detail_two, detail_three, coarse = call(
        z_middle_kernel,
        [
            (7, last, quarter, lanes),
            (7, 1, eighth, lanes // 2),
            (1, eighth, lanes // 2),
        ],
        [bands, below, above, own, far, back],
        [pltpu.VMEM((last, packed, lanes), f32)] * 2,
    )
    return detail_one, detail_two, detail_three, coarse


def solution(mesh):
    placed = (P("gz", "gx", None),)
    return jax.shard_map(
        on_device,
        mesh=mesh,
        in_specs=placed,
        out_specs=(
            P(None, "gz", "gx", None),
            P(None, "gz", "gx", None),
            P(None, "gz", "gx", None),
            P("gz", "gx", None),
        ),
        check_vma=False,
    )
```

```python
import functools

import jax
import jax.numpy as jnp
import numpy as np
from jax import lax
from jax.experimental import pallas as pl
from jax.experimental.pallas import tpu as pltpu
from jax.sharding import PartitionSpec as P

LEVELS = 3
GAP = 1
GAP_OWN = 1
GAP_DETAIL = 1
PLANES = 8
PARTS = 1
MARK = (8, 128)
LANES = 128

LOW_TAPS = (
    0.026748757411,
    -0.016864118443,
    -0.078223266529,
    0.266864118443,
    0.602949018236,
    0.266864118443,
    -0.078223266529,
    -0.016864118443,
    0.026748757411,
)
HIGH_TAPS = (
    0.091271763114,
    -0.057543526229,
    -0.591271763114,
    1.115087052457,
    -0.591271763114,
    -0.057543526229,
    0.091271763114,
)

ALPHA = -1.586134342059924
BETA = -0.052980118572961
GAMMA = 0.882911075530934
DELTA = 0.443506852043971
LOW_SCALE = 0.812893066115961
HIGH_SCALE = 1.230174104914001


def shifted(value, axis, steps):
    count = lax.axis_size(axis)
    pairs = [(source, (source + steps) % count) for source in range(count)]
    return lax.ppermute(value, axis, pairs)


def other_core(value):
    count = lax.axis_size("gx")
    return lax.ppermute(value, "gx", [(source, source ^ 1) for source in range(count)])


def shifted_by_core(value, steps):
    high, wide = lax.axis_size("gz"), lax.axis_size("gx")
    pairs = [
        (z * wide + x, ((z + (-steps if x % 2 else steps)) % high) * wide + x)
        for z in range(high)
        for x in range(wide)
    ]
    return lax.ppermute(value, ("gz", "gx"), pairs)


def band_matrix(length):
    half = length // 2
    matrix = np.zeros((length, length), np.float64)
    for j in range(half):
        for k in range(-4, 5):
            matrix[(2 * j + k) % length, j] += LOW_TAPS[k + 4]
        for k in range(-3, 4):
            matrix[(2 * j + 1 + k) % length, half + j] += HIGH_TAPS[k + 3]
    return matrix


def three_parts(matrix):
    parts = []
    rest = matrix
    for _ in range(3):
        part = rest.astype(np.float32).astype(jnp.bfloat16)
        parts.append(part)
        rest = rest - part.astype(np.float64)
    return np.stack(parts)


def exact_dot(value, parts):
    first = value.astype(jnp.bfloat16)
    rest = value - first.astype(jnp.float32)
    second = rest.astype(jnp.bfloat16)
    third = (rest - second.astype(jnp.float32)).astype(jnp.bfloat16)

    count = value.shape[0]

    def dot(parts_of_value, part):
        rows = jnp.concatenate(parts_of_value, 0)
        result = jnp.dot(rows, part, preferred_element_type=jnp.float32)
        return [result[k * count : (k + 1) * count] for k in range(len(parts_of_value))]

    large, middle, small = dot([first, second, third], parts[0])
    middle_too, small_too = dot([first, second], parts[1])
    (small_last,) = dot([first], parts[2])
    return large + ((middle + middle_too) + (small + small_too + small_last))


def lift_rows(even, odd):
    count = even.shape[0]

    def after(a):
        return pltpu.roll(a, count - 1, 0)

    def before(a):
        return pltpu.roll(a, 1, 0)

    odd = odd + ALPHA * (even + after(even))
    even = even + BETA * (before(odd) + odd)
    odd = odd + GAMMA * (even + after(even))
    even = even + DELTA * (before(odd) + odd)
    return even * LOW_SCALE, odd * HIGH_SCALE


def rim_sums(planes):
    even, odd = planes[0::2], planes[1::2]
    up_odd = odd[-1] + ALPHA * even[-1]
    up_even = even[-1] + BETA * (odd[-2] + ALPHA * (even[-2] + even[-1]))
    down_even = even[0] + BETA * (odd[0] + ALPHA * (even[0] + even[1]))
    return (up_odd, up_even), (even[0], down_even)


def lift_planes(planes, below, above):
    even, odd = planes[0::2], planes[1::2]
    count = len(even)
    first_odd = below[0] + ALPHA * even[0]
    odd = [
        odd[i] + ALPHA * (even[i] + (even[i + 1] if i + 1 < count else above[0]))
        for i in range(count)
    ]
    first_even = below[1] + BETA * first_odd
    even = [
        even[i] + BETA * ((odd[i - 1] if i else first_odd) + odd[i])
        for i in range(count)
    ]
    last_even = above[1] + BETA * odd[-1]
    first_odd = first_odd + GAMMA * (first_even + even[0])
    odd = [
        odd[i] + GAMMA * (even[i] + (even[i + 1] if i + 1 < count else last_even))
        for i in range(count)
    ]
    even = [
        even[i] + DELTA * ((odd[i - 1] if i else first_odd) + odd[i])
        for i in range(count)
    ]
    return [e * LOW_SCALE for e in even], [o * HIGH_SCALE for o in odd]


def double_taps():
    low, high = {}, {}
    for k in range(-4, 5):
        for m in range(-4, 5):
            at = 2 * k + m
            low[at] = low.get(at, 0.0) + LOW_TAPS[k + 4] * LOW_TAPS[m + 4]
    for k in range(-3, 4):
        for m in range(-4, 5):
            at = 2 * (k + 1) + m
            high[at] = high.get(at, 0.0) + HIGH_TAPS[k + 3] * LOW_TAPS[m + 4]
    return low, high


def ring_distances(planes):
    reach = -(-max(double_taps()[0]) // planes)
    return [0] + [sign * step for step in range(1, reach + 1) for sign in (1, -1)]


def deep_share(planes, distance):
    count = len(planes)
    shares = []
    for taps in double_taps():
        terms = [
            planes[z] * taps[z - count * distance]
            for z in range(count)
            if z - count * distance in taps
        ]
        shares.append(functools.reduce(jnp.add, terms) if terms else jnp.zeros_like(planes[0]))
    return shares


def single_plane(planes, distance):
    low, high = (
        [taps.get(z - planes * distance, 0.0) for z in range(planes)] for taps in double_taps()
    )
    if not any(high):
        return 0.0
    if sum(1 for pair in zip(low, high, strict=True) if any(pair)) == 1 and any(low):
        return sum(high) / sum(low)
    return None


def far_steps(planes):
    steps = []
    for distance in range(2, max(ring_distances(planes)) + 1):
        ratios = [single_plane(planes, sign * distance) for sign in (1, -1)]
        steps.append((distance, 2 if None in ratios else 1, ratios))
    return steps


def chunk_of(rows):
    for size in (16, 8):
        if rows % size == 0:
            return size
    return rows


def over_rows(rows, body):
    size = chunk_of(rows)

    def step(i, carry):
        body(pl.ds(pl.multiple_of(i * size, size), size))
        return carry

    lax.fori_loop(0, rows // size, step, 0)


def spread_rims(source, up_ref, down_ref, rows):
    planes = source.shape[0]

    def body(at):
        up, down = rim_sums([source[z, at, :] for z in range(planes)])
        for k in range(2):
            up_ref[k, at, :] = up[k]
            down_ref[k, at, :] = down[k]

    over_rows(rows, body)


def mark(ref):
    ref[...] = jnp.zeros_like(ref)


def rim_kernel(v_ref, w_ref, up_ref, down_ref, held, weights, raw, sems):
    planes, rows, _ = held.shape
    parts = sems.shape[0] - 1
    size = rows // parts
    copies = []
    for part in range(parts):
        at = pl.ds(part * size, size)
        copies.append(pltpu.make_async_copy(v_ref.at[:, at, :], held.at[:, at, :], sems.at[part]))
        copies[-1].start()
    weight_copy = pltpu.make_async_copy(w_ref, weights, sems.at[parts])
    weight_copy.start()
    for part in range(parts):
        copies[part].wait()

        def step(i, carry):
            at = pl.ds(pl.multiple_of(part * size + i * 8, 8), 8)
            up, down = rim_sums([held[z, at, :] for z in range(planes)])
            for k, value in enumerate(up + down):
                raw[k, at, :] = value
            return carry

        lax.fori_loop(0, size // 8, step, 0)
        if part == 0:
            weight_copy.wait()
        at = pl.ds(part * size, size)
        low = exact_dot(raw[:, at, :].reshape(4 * size, -1), weights)
        for k, ref in enumerate((up_ref, up_ref, down_ref, down_ref)):
            ref[k % 2, at, :] = low[k * size : (k + 1) * size]


def y_kernel(v_ref, w_low_ref, w_high_ref, low_ref, high_ref, up_ref, down_ref):
    planes, rows, width = v_ref.shape
    block = PLANES if planes % PLANES == 0 else 1

    def step(i, carry):
        at = pl.ds(i * block, block)
        flat = v_ref[at].reshape(block * rows, width)
        low_ref[at] = exact_dot(flat, w_low_ref).reshape(block, rows, width // 2)
        high = exact_dot(flat, w_high_ref).reshape(block, rows, width // 2)
        high_ref[at] = high
        up_ref[at] = high[:, rows - 8 :]
        down_ref[at] = high[:, :8]
        return carry

    lax.fori_loop(0, planes // block, step, 0)


def lift_in_scratch(scratch, pairs):
    even = scratch[pl.ds(0, pairs, stride=2), :]
    odd = scratch[pl.ds(1, pairs, stride=2), :]
    return lift_rows(even, odd)


def lane_tiles(width):
    size = min(width, LANES)
    return [pl.ds(k, size) for k in range(0, width, size)]


def x_high_kernel(
    y_ref, below_ref, above_ref, x_ref, up_ref, down_ref, mark_ref, scratch
):
    planes, rows, width = y_ref.shape
    half = rows // 2

    def step(z, carry):
        for tile, lanes in enumerate(lane_tiles(width)):
            part = scratch.at[tile]
            part[8:16] = below_ref[z, :, lanes]
            part[16 : 16 + rows] = y_ref[z, :, lanes]
            part[16 + rows : 24 + rows] = above_ref[z, :, lanes]
            low, high = lift_in_scratch(part, half + 16)
            x_ref[z, 0:half, lanes] = low[8 : 8 + half]
            x_ref[z, half:rows, lanes] = high[8 : 8 + half]
        return carry

    scratch[:, 0:8] = jnp.zeros_like(scratch[:, 0:8])
    scratch[:, 24 + rows :] = jnp.zeros_like(scratch[:, 24 + rows :])
    lax.fori_loop(0, planes, step, 0)
    spread_rims(x_ref, up_ref, down_ref, rows)
    mark(mark_ref)


LOW_BELOW, LOW_ABOVE = 32, 24


def lift_rows_of(y_ref, below_ref, above_ref, at):
    return lift_planes(
        [y_ref[z, at, :] for z in range(y_ref.shape[0])],
        [below_ref[k, at, :] for k in range(2)],
        [above_ref[k, at, :] for k in range(2)],
    )


def z_edge_kernel(y_ref, below_ref, above_ref, after_ref, up_ref, down_ref, mark_ref):
    del after_ref
    planes, rows, _ = y_ref.shape
    size = 8
    for start in range(0, LOW_ABOVE, size):
        low, high = lift_rows_of(y_ref, below_ref, above_ref, slice(start, start + size))
        for z in range(planes // 2):
            down_ref[z, start : start + size] = low[z]
            if start == 0:
                down_ref[z, LOW_ABOVE : LOW_ABOVE + size] = high[z]
    for start in range(0, LOW_BELOW, size):
        at = rows - LOW_BELOW + start
        low, high = lift_rows_of(y_ref, below_ref, above_ref, slice(at, at + size))
        for z in range(planes // 2):
            up_ref[z, start : start + size] = low[z]
            if start == LOW_BELOW - size:
                up_ref[z, LOW_BELOW : LOW_BELOW + size] = high[z]
    mark(mark_ref)


def z_lift_kernel(y_ref, below_ref, above_ref, after_ref, low_ref, high_ref):
    del after_ref
    planes, rows, _ = y_ref.shape

    def body(at):
        low, high = lift_rows_of(y_ref, below_ref, above_ref, at)
        for z in range(planes // 2):
            low_ref[z, at, :] = low[z]
            high_ref[z, at, :] = high[z]

    over_rows(rows, body)


def x_low_kernel(
    low_ref, below_ref, above_ref, w_two_ref, w_three_ref,
    part_ref, bands_ref, up_ref, down_ref, deep_planes, mark_ref,
    scratch, approx, split, deep_low, deep_split,
):
    planes, rows, width = low_ref.shape
    half = rows // 2
    deep = (rows + 64) // 2
    quarter = half // 2
    eighth = quarter // 2

    def step(z, carry):
        for tile, lanes in enumerate(lane_tiles(width)):
            part = scratch.at[tile]
            part[0:LOW_BELOW] = below_ref[z, 0:LOW_BELOW, lanes]
            part[LOW_BELOW : LOW_BELOW + rows] = low_ref[z, :, lanes]
            top = LOW_BELOW + rows
            part[top : top + LOW_ABOVE] = above_ref[z, 0:LOW_ABOVE, lanes]
            low, high = lift_in_scratch(part, deep)
            approx[z, :, lanes] = low
            part_ref[0, z, :, lanes] = high[16 : 16 + half]
        return carry

    scratch[:, rows + 32 :] = jnp.zeros_like(scratch[:, rows + 32 :])
    lax.fori_loop(0, planes, step, 0)
    whole = exact_dot(approx[...].reshape(planes * deep, width), w_two_ref)
    for tile in range(split.shape[0]):
        split[tile] = whole[:, tile * LANES : (tile + 1) * LANES]
    span = deep // 2
    for z in range(planes):
        for y in range(2):
            low, high = lift_in_scratch(split.at[y, pl.ds(z * deep, deep)], span)
            start = 2 * y * quarter
            bands_ref[z, start : start + quarter, :] = low[8 : 8 + quarter]
            bands_ref[z, start + quarter : start + 2 * quarter, :] = high[8 : 8 + quarter]
            if y == 0:
                deep_low[z] = low
    deep_split[...] = exact_dot(deep_low[...].reshape(planes * span, -1), w_three_ref)
    for z in range(planes):
        low, high = lift_in_scratch(deep_split.at[pl.ds(z * span, span)], span // 2)
        deep_planes[z, 0:eighth, :] = low[4 : 4 + eighth]
        deep_planes[z, eighth:, :] = high[4 : 4 + eighth]
    packed = bands_ref.shape[1]
    spread_rims(bands_ref, up_ref, down_ref, packed)
    for distance, ref in ((1, up_ref), (-1, down_ref)):
        share = deep_share([deep_planes[z] for z in range(planes)], distance)
        for k in range(2):
            ref[k, packed:, :] = share[k]
    mark(mark_ref)


def own_kernel(deep_ref, own_ref, mark_ref):
    share = deep_share([deep_ref[z] for z in range(deep_ref.shape[0])], 0)
    for k in range(2):
        own_ref[k] = share[k]
    mark(mark_ref)


def far_kernel(deep_ref, keep_ref, give_ref, held):
    planes = [deep_ref[z] for z in range(deep_ref.shape[0])]
    core = lax.rem(lax.axis_index("gx"), 2)
    at = 0
    for distance, count, _ in far_steps(len(planes)):
        for sign, slot in ((1, core), (-1, 1 - core)):
            share = deep_share(planes, sign * distance)
            for k in range(count):
                held[slot, at + k] = share[k]
        at = at + count
    keep_ref[...] = held[0]
    give_ref[...] = held[1]


def pack_kernel(first, keep_ref, got_ref, after_ref, out_ref):
    del after_ref
    for k in range(out_ref.shape[1]):
        out_ref[0, k] = keep_ref[first + k]
        out_ref[1, k] = got_ref[first + k]


def sum_kernel(planes, *refs):
    *far_refs, after_ref, mine_ref, other_ref = refs
    del after_ref
    core = lax.rem(lax.axis_index("gx"), 2)
    for owner, out_ref in enumerate((mine_ref, other_ref)):
        low = jnp.zeros_like(out_ref[0])
        high = jnp.zeros_like(low)
        for ref, (_, count, ratios) in zip(far_refs, far_steps(planes), strict=True):
            part = ref[owner, 0]
            low = low + part
            if count == 1:
                high = high + part * jnp.where(core == 0, *map(jnp.float32, ratios))
            else:
                high = high + ref[owner, 1]
        out_ref[0] = low
        out_ref[1] = high


def x_detail_kernel(
    part_ref, high_ref, below_ref, above_ref, detail_ref, mark_ref, scratch, held, sems
):
    planes, rows, width = high_ref.shape
    half = rows // 2
    copies = [pltpu.make_async_copy(part_ref, detail_ref.at[1:2], sems.at[0])]
    copies[0].start()
    scratch[:, 0:8] = jnp.zeros_like(scratch[:, 0:8])
    scratch[:, rows + 24 :] = jnp.zeros_like(scratch[:, rows + 24 :])

    def step(z, carry):
        for tile, lanes in enumerate(lane_tiles(width)):
            part = scratch.at[tile]
            part[8:16] = below_ref[z, LOW_BELOW : LOW_BELOW + 8, lanes]
            part[16 : 16 + rows] = high_ref[z, :, lanes]
            part[16 + rows : 24 + rows] = above_ref[z, LOW_ABOVE : LOW_ABOVE + 8, lanes]
            low, high = lift_in_scratch(part, half + 16)
            held[0, z, :, lanes] = low[8 : 8 + half]
            held[1, z, :, lanes] = high[8 : 8 + half]
        return carry

    lax.fori_loop(0, planes, step, 0)
    for k in range(2):
        copies.append(
            pltpu.make_async_copy(
                held.at[k : k + 1], detail_ref.at[2 * k : 2 * k + 1], sems.at[1 + k]
            )
        )
        copies[-1].start()
    for copy in copies:
        copy.wait()
    mark(mark_ref)


def z_high_kernel(x_ref, below_ref, above_ref, whole_ref, after_ref, detail_ref, held, sems):
    del whole_ref, after_ref
    planes, rows, _ = x_ref.shape
    half = rows // 2
    copies = []
    for xb in range(2):

        def body(at):
            here = pl.ds(at.start + xb * half, at.size)
            low, high = lift_rows_of(x_ref, below_ref, above_ref, here)
            for z in range(planes // 2):
                held[2 * xb, z, at, :] = low[z]
                held[2 * xb + 1, z, at, :] = high[z]

        over_rows(half, body)
        copies.append(
            pltpu.make_async_copy(
                held.at[pl.ds(2 * xb, 2)], detail_ref.at[pl.ds(3 + 2 * xb, 2)], sems.at[xb]
            )
        )
        copies[-1].start()
    for copy in copies:
        copy.wait()


def z_middle_kernel(
    bands_ref, below_ref, above_ref, own_ref, far_ref, back_ref,
    detail_ref, deep_ref, coarse_ref, low_ref, high_ref,
):
    planes, rows, _ = bands_ref.shape
    kept = planes // 2
    quarter = detail_ref.shape[2]

    def body(at):
        low, high = lift_planes(
            [bands_ref[z, at, :] for z in range(planes)],
            [below_ref[k, at, :] for k in range(2)],
            [above_ref[k, at, :] for k in range(2)],
        )
        for z in range(kept):
            low_ref[z, at, :] = low[z]
            high_ref[z, at, :] = high[z]

    over_rows(rows, body)
    for z in range(kept):
        for band in range(1, 8):
            source = high_ref if band % 2 else low_ref
            start = quarter * (band // 2)
            detail_ref[band - 1, z] = source[z, start : start + quarter, :]
    height, width = coarse_ref.shape[1:]
    shares = (
        own_ref, below_ref.at[:, rows:, :], above_ref.at[:, rows:, :], far_ref, back_ref
    )
    low, high = (
        functools.reduce(jnp.add, [ref[k] for ref in shares])
        for k in range(2)
    )
    coarse_ref[0] = low[0:height, 0:width]
    for band in range(1, 8):
        value = high if band % 2 else low
        xb, yb = (band // 2) % 2, band // 4
        deep_ref[band - 1, 0] = value[
            xb * height : (xb + 1) * height, yb * width : (yb + 1) * width
        ]


def call(
    kernel, out_shapes, inputs, scratch=(), anywhere=(), aliases=None, open_inputs=(), scalars=(), cost=1
):
    whole = pl.BlockSpec(memory_space=pltpu.VMEM)
    unplaced = pl.BlockSpec(memory_space=pl.ANY)
    small = pl.BlockSpec(memory_space=pltpu.SMEM)
    return pl.pallas_call(
        kernel,
        out_shape=[
            jax.ShapeDtypeStruct(s, jnp.float32)
            if isinstance(s, tuple)
            else jax.ShapeDtypeStruct(s.shape, s.dtype)
            for s in out_shapes
        ],
        in_specs=[
            unplaced if i in open_inputs else small if i in scalars else whole
            for i in range(len(inputs))
        ],
        out_specs=[unplaced if i in anywhere else whole for i in range(len(out_shapes))],
        scratch_shapes=list(scratch),
        input_output_aliases=aliases or {},
        cost_estimate=pl.CostEstimate(flops=cost, bytes_accessed=cost, transcendentals=0),
        compiler_params=pltpu.CompilerParams(vmem_limit_bytes=24 * 2**20),
        name=getattr(kernel, "func", kernel).__name__,
    )(*inputs)


def on_device(velocity):
    planes, rows, width = velocity.shape
    half_width = width // 2
    half = rows // 2
    quarter = half // 2
    tiles = half_width // LANES
    f32 = jnp.float32
    matrix = band_matrix(width)
    w_low = jnp.asarray(three_parts(matrix[:, :half_width]))
    w_high = jnp.asarray(three_parts(matrix[:, half_width:]))
    w_two = jnp.asarray(three_parts(band_matrix(half_width)))
    w_three = jnp.asarray(three_parts(band_matrix(half_width // 2)))

    whole = (planes, rows, half_width)
    rims = (2, rows, half_width)
    up, down, held, weights = call(
        rim_kernel,
        [rims, rims, velocity.shape, w_low],
        [
            pltpu.with_memory_space_constraint(velocity, pltpu.HBM),
            pltpu.with_memory_space_constraint(w_low, pltpu.HBM),
        ],
        [
            pltpu.VMEM((4, rows, width), f32),
            pltpu.SemaphoreType.DMA((PARTS + 1,)),
        ],
        open_inputs=(0, 1),
    )
    low_below, low_above = shifted(up, "gz", 1), shifted(down, "gz", -1)

    edge = (planes, 8, half_width)
    y_low, y_high, up, down = call(
        y_kernel, [whole, whole, edge, edge], [held, weights, w_high]
    )
    below, above = shifted(up, "gx", 1), shifted(down, "gx", -1)
    x_high, up, down, mark_high = call(
        x_high_kernel,
        [whole, rims, rims, MARK],
        [y_high, below, above],
        [pltpu.VMEM((tiles, rows + 32, LANES), f32)],
    )
    high_above, high_below = shifted(down, "gz", -1), shifted(up, "gz", 1)

    kept = (planes // 2, rows, half_width)
    up, down, mark_edge = call(
        z_edge_kernel,
        [
            (planes // 2, LOW_BELOW + 8, half_width),
            (planes // 2, LOW_ABOVE + 8, half_width),
            MARK,
        ],
        [y_low, low_below, low_above, mark_high],
    )
    edge_below, edge_above = shifted(up, "gx", 1), shifted(down, "gx", -1)
    z_low, z_high = call(
        z_lift_kernel, [kept, kept], [y_low, low_below, low_above, mark_edge], cost=GAP
    )
    deep = (rows + 64) // 2
    packed = 4 * quarter
    eighth = quarter // 2
    lanes = half_width // 2
    detail_shape = (7, planes // 2, half, half_width)
    middle = (2, packed + 2 * eighth, lanes)
    share = (2, 2 * eighth, lanes)
    steps = far_steps(planes // 2)
    part, bands, up, down, deep_planes, mark_low = call(
        x_low_kernel,
        [
            (1,) + detail_shape[1:],
            (planes // 2, packed, lanes),
            middle,
            middle,
            (planes // 2, 2 * eighth, lanes),
            MARK,
        ],
        [z_low, edge_below, edge_above, w_two, w_three],
        [
            pltpu.VMEM((tiles, rows + 64, LANES), f32),
            pltpu.VMEM((planes // 2, deep, half_width), f32),
            pltpu.VMEM((tiles, planes // 2 * deep, LANES), f32),
            pltpu.VMEM((planes // 2, deep // 2, lanes), f32),
            pltpu.VMEM((planes // 2 * deep // 2, lanes), f32),
        ],
    )
    detail_one, mark_detail = call(
        x_detail_kernel,
        [detail_shape, MARK],
        [part, z_high, edge_below, edge_above],
        [
            pltpu.VMEM((tiles, rows + 32, LANES), f32),
            pltpu.VMEM((2,) + detail_shape[1:], f32),
            pltpu.SemaphoreType.DMA((3,)),
        ],
        anywhere=(0,),
        cost=GAP_DETAIL,
    )
    below, above = shifted(up, "gz", 1), shifted(down, "gz", -1)
    sent = (sum(count for _, count, _ in steps),) + share[1:]
    keep, give = call(
        far_kernel, [sent, sent], [deep_planes], [pltpu.VMEM((2,) + sent, f32)]
    )
    own, mark_own = call(own_kernel, [share, MARK], [deep_planes], cost=GAP_OWN)
    got = other_core(give)
    both = []
    first = 0
    for distance, count, _ in steps:
        after = mark_own if distance == steps[-1][0] else high_above
        (packed_share,) = call(
            functools.partial(pack_kernel, first), [(2, count) + share[1:]], [keep, got, after]
        )
        both.append(shifted_by_core(packed_share, distance))
        first = first + count
    far, back = call(
        functools.partial(sum_kernel, planes // 2), [share] * 2, [*both, mark_detail]
    )
    back = other_core(back)
    (detail_one,) = call(
        z_high_kernel,
        [detail_shape],
        [x_high, high_below, high_above, detail_one, mark_low],
        [pltpu.VMEM((4,) + detail_shape[1:], f32), pltpu.SemaphoreType.DMA((2,))],
        anywhere=(0,),
        aliases={3: 0},
        open_inputs=(3,),
    )
    last = planes // 4
    detail_two, detail_three, coarse = call(
        z_middle_kernel,
        [
            (7, last, quarter, lanes),
            (7, 1, eighth, lanes // 2),
            (1, eighth, lanes // 2),
        ],
        [bands, below, above, own, far, back],
        [pltpu.VMEM((last, packed, lanes), f32)] * 2,
    )
    return detail_one, detail_two, detail_three, coarse


def solution(mesh):
    placed = (P("gz", "gx", None),)
    return jax.shard_map(
        on_device,
        mesh=mesh,
        in_specs=placed,
        out_specs=(
            P(None, "gz", "gx", None),
            P(None, "gz", "gx", None),
            P(None, "gz", "gx", None),
            P("gz", "gx", None),
        ),
        check_vma=False,
    )
```

```python
import functools

import jax
import jax.numpy as jnp
import numpy as np
from jax import lax
from jax.experimental import pallas as pl
from jax.experimental.pallas import tpu as pltpu
from jax.sharding import PartitionSpec as P

LEVELS = 3
GAP = 1
GAP_OWN = 1
GAP_DETAIL = 1
PLANES = 8
PARTS = 1
MARK = (8, 128)
LANES = 128

LOW_TAPS = (
    0.026748757411,
    -0.016864118443,
    -0.078223266529,
    0.266864118443,
    0.602949018236,
    0.266864118443,
    -0.078223266529,
    -0.016864118443,
    0.026748757411,
)
HIGH_TAPS = (
    0.091271763114,
    -0.057543526229,
    -0.591271763114,
    1.115087052457,
    -0.591271763114,
    -0.057543526229,
    0.091271763114,
)

ALPHA = -1.586134342059924
BETA = -0.052980118572961
GAMMA = 0.882911075530934
DELTA = 0.443506852043971
LOW_SCALE = 0.812893066115961
HIGH_SCALE = 1.230174104914001


def shifted(value, axis, steps):
    count = lax.axis_size(axis)
    pairs = [(source, (source + steps) % count) for source in range(count)]
    return lax.ppermute(value, axis, pairs)


def other_core(value):
    count = lax.axis_size("gx")
    return lax.ppermute(value, "gx", [(source, source ^ 1) for source in range(count)])


def shifted_by_core(value, steps):
    high, wide = lax.axis_size("gz"), lax.axis_size("gx")
    pairs = [
        (z * wide + x, ((z + (-steps if x % 2 else steps)) % high) * wide + x)
        for z in range(high)
        for x in range(wide)
    ]
    return lax.ppermute(value, ("gz", "gx"), pairs)


def band_matrix(length):
    half = length // 2
    matrix = np.zeros((length, length), np.float64)
    for j in range(half):
        for k in range(-4, 5):
            matrix[(2 * j + k) % length, j] += LOW_TAPS[k + 4]
        for k in range(-3, 4):
            matrix[(2 * j + 1 + k) % length, half + j] += HIGH_TAPS[k + 3]
    return matrix


def three_parts(matrix):
    parts = []
    rest = matrix
    for _ in range(3):
        part = rest.astype(np.float32).astype(jnp.bfloat16)
        parts.append(part)
        rest = rest - part.astype(np.float64)
    return np.stack(parts)


def exact_dot(value, parts):
    first = value.astype(jnp.bfloat16)
    rest = value - first.astype(jnp.float32)
    second = rest.astype(jnp.bfloat16)
    third = (rest - second.astype(jnp.float32)).astype(jnp.bfloat16)

    count = value.shape[0]

    def dot(parts_of_value, part):
        rows = jnp.concatenate(parts_of_value, 0)
        result = jnp.dot(rows, part, preferred_element_type=jnp.float32)
        return [result[k * count : (k + 1) * count] for k in range(len(parts_of_value))]

    large, middle, small = dot([first, second, third], parts[0])
    middle_too, small_too = dot([first, second], parts[1])
    (small_last,) = dot([first], parts[2])
    return large + ((middle + middle_too) + (small + small_too + small_last))


def lift_rows(even, odd):
    count = even.shape[0]

    def after(a):
        return pltpu.roll(a, count - 1, 0)

    def before(a):
        return pltpu.roll(a, 1, 0)

    odd = odd + ALPHA * (even + after(even))
    even = even + BETA * (before(odd) + odd)
    odd = odd + GAMMA * (even + after(even))
    even = even + DELTA * (before(odd) + odd)
    return even * LOW_SCALE, odd * HIGH_SCALE


def rim_sums(planes):
    even, odd = planes[0::2], planes[1::2]
    up_odd = odd[-1] + ALPHA * even[-1]
    up_even = even[-1] + BETA * (odd[-2] + ALPHA * (even[-2] + even[-1]))
    down_even = even[0] + BETA * (odd[0] + ALPHA * (even[0] + even[1]))
    return (up_odd, up_even), (even[0], down_even)


def lift_planes(planes, below, above):
    even, odd = planes[0::2], planes[1::2]
    count = len(even)
    first_odd = below[0] + ALPHA * even[0]
    odd = [
        odd[i] + ALPHA * (even[i] + (even[i + 1] if i + 1 < count else above[0]))
        for i in range(count)
    ]
    first_even = below[1] + BETA * first_odd
    even = [
        even[i] + BETA * ((odd[i - 1] if i else first_odd) + odd[i])
        for i in range(count)
    ]
    last_even = above[1] + BETA * odd[-1]
    first_odd = first_odd + GAMMA * (first_even + even[0])
    odd = [
        odd[i] + GAMMA * (even[i] + (even[i + 1] if i + 1 < count else last_even))
        for i in range(count)
    ]
    even = [
        even[i] + DELTA * ((odd[i - 1] if i else first_odd) + odd[i])
        for i in range(count)
    ]
    return [e * LOW_SCALE for e in even], [o * HIGH_SCALE for o in odd]


def double_taps():
    low, high = {}, {}
    for k in range(-4, 5):
        for m in range(-4, 5):
            at = 2 * k + m
            low[at] = low.get(at, 0.0) + LOW_TAPS[k + 4] * LOW_TAPS[m + 4]
    for k in range(-3, 4):
        for m in range(-4, 5):
            at = 2 * (k + 1) + m
            high[at] = high.get(at, 0.0) + HIGH_TAPS[k + 3] * LOW_TAPS[m + 4]
    return low, high


def ring_distances(planes):
    reach = -(-max(double_taps()[0]) // planes)
    return [0] + [sign * step for step in range(1, reach + 1) for sign in (1, -1)]


def deep_share(planes, distance):
    count = len(planes)
    shares = []
    for taps in double_taps():
        terms = [
            planes[z] * taps[z - count * distance]
            for z in range(count)
            if z - count * distance in taps
        ]
        shares.append(functools.reduce(jnp.add, terms) if terms else jnp.zeros_like(planes[0]))
    return shares


def single_plane(planes, distance):
    low, high = (
        [taps.get(z - planes * distance, 0.0) for z in range(planes)] for taps in double_taps()
    )
    if not any(high):
        return 0.0
    if sum(1 for pair in zip(low, high, strict=True) if any(pair)) == 1 and any(low):
        return sum(high) / sum(low)
    return None


def far_steps(planes):
    steps = []
    for distance in range(2, max(ring_distances(planes)) + 1):
        ratios = [single_plane(planes, sign * distance) for sign in (1, -1)]
        steps.append((distance, 2 if None in ratios else 1, ratios))
    return steps


def chunk_of(rows):
    for size in (16, 8):
        if rows % size == 0:
            return size
    return rows


def over_rows(rows, body):
    size = chunk_of(rows)

    def step(i, carry):
        body(pl.ds(pl.multiple_of(i * size, size), size))
        return carry

    lax.fori_loop(0, rows // size, step, 0)


def spread_rims(source, up_ref, down_ref, rows):
    planes = source.shape[0]

    def body(at):
        up, down = rim_sums([source[z, at, :] for z in range(planes)])
        for k in range(2):
            up_ref[k, at, :] = up[k]
            down_ref[k, at, :] = down[k]

    over_rows(rows, body)


def mark(ref):
    ref[...] = jnp.zeros_like(ref)


def rim_kernel(v_ref, w_ref, up_ref, down_ref, held, weights, raw, sems):
    planes, rows, _ = held.shape
    parts = sems.shape[0] - 1
    size = rows // parts
    copies = []
    for part in range(parts):
        at = pl.ds(part * size, size)
        copies.append(pltpu.make_async_copy(v_ref.at[:, at, :], held.at[:, at, :], sems.at[part]))
        copies[-1].start()
    weight_copy = pltpu.make_async_copy(w_ref, weights, sems.at[parts])
    weight_copy.start()
    for part in range(parts):
        copies[part].wait()

        def step(i, carry):
            at = pl.ds(pl.multiple_of(part * size + i * 8, 8), 8)
            up, down = rim_sums([held[z, at, :] for z in range(planes)])
            for k, value in enumerate(up + down):
                raw[k, at, :] = value
            return carry

        lax.fori_loop(0, size // 8, step, 0)
        if part == 0:
            weight_copy.wait()
        at = pl.ds(part * size, size)
        low = exact_dot(raw[:, at, :].reshape(4 * size, -1), weights)
        for k, ref in enumerate((up_ref, up_ref, down_ref, down_ref)):
            ref[k % 2, at, :] = low[k * size : (k + 1) * size]


def y_kernel(v_ref, w_low_ref, w_high_ref, low_ref, high_ref, up_ref, down_ref):
    planes, rows, width = v_ref.shape
    block = PLANES if planes % PLANES == 0 else 1

    def step(i, carry):
        at = pl.ds(i * block, block)
        flat = v_ref[at].reshape(block * rows, width)
        low_ref[at] = exact_dot(flat, w_low_ref).reshape(block, rows, width // 2)
        high = exact_dot(flat, w_high_ref).reshape(block, rows, width // 2)
        high_ref[at] = high
        up_ref[at] = high[:, rows - 8 :]
        down_ref[at] = high[:, :8]
        return carry

    lax.fori_loop(0, planes // block, step, 0)


def lift_in_scratch(scratch, pairs, start=0):
    even = scratch[pl.ds(start, pairs, stride=2), :]
    odd = scratch[pl.ds(start + 1, pairs, stride=2), :]
    return lift_rows(even, odd)


def lane_tiles(width):
    size = min(width, LANES)
    return [pl.ds(k, size) for k in range(0, width, size)]


def x_high_kernel(
    y_ref, below_ref, above_ref, x_ref, up_ref, down_ref, mark_ref, scratch
):
    planes, rows, width = y_ref.shape
    half = rows // 2

    def step(z, carry):
        for tile, lanes in enumerate(lane_tiles(width)):
            part = scratch.at[tile]
            part[8:16] = below_ref[z, :, lanes]
            part[16 : 16 + rows] = y_ref[z, :, lanes]
            part[16 + rows : 24 + rows] = above_ref[z, :, lanes]
            low, high = lift_in_scratch(part, half + 16)
            x_ref[z, 0:half, lanes] = low[8 : 8 + half]
            x_ref[z, half:rows, lanes] = high[8 : 8 + half]
        return carry

    scratch[:, 0:8] = jnp.zeros_like(scratch[:, 0:8])
    scratch[:, 24 + rows :] = jnp.zeros_like(scratch[:, 24 + rows :])
    lax.fori_loop(0, planes, step, 0)
    spread_rims(x_ref, up_ref, down_ref, rows)
    mark(mark_ref)


LOW_BELOW, LOW_ABOVE = 32, 24


def lift_rows_of(y_ref, below_ref, above_ref, at):
    return lift_planes(
        [y_ref[z, at, :] for z in range(y_ref.shape[0])],
        [below_ref[k, at, :] for k in range(2)],
        [above_ref[k, at, :] for k in range(2)],
    )


def z_edge_kernel(y_ref, below_ref, above_ref, after_ref, up_ref, down_ref, mark_ref):
    del after_ref
    planes, rows, _ = y_ref.shape
    size = 8
    for start in range(0, LOW_ABOVE, size):
        low, high = lift_rows_of(y_ref, below_ref, above_ref, slice(start, start + size))
        for z in range(planes // 2):
            down_ref[z, start : start + size] = low[z]
            if start == 0:
                down_ref[z, LOW_ABOVE : LOW_ABOVE + size] = high[z]
    for start in range(0, LOW_BELOW, size):
        at = rows - LOW_BELOW + start
        low, high = lift_rows_of(y_ref, below_ref, above_ref, slice(at, at + size))
        for z in range(planes // 2):
            up_ref[z, start : start + size] = low[z]
            if start == LOW_BELOW - size:
                up_ref[z, LOW_BELOW : LOW_BELOW + size] = high[z]
    mark(mark_ref)


def z_lift_kernel(y_ref, below_ref, above_ref, after_ref, low_ref, high_ref):
    del after_ref
    planes, rows, _ = y_ref.shape

    def body(at):
        low, high = lift_rows_of(y_ref, below_ref, above_ref, at)
        for z in range(planes // 2):
            low_ref[z, at, :] = low[z]
            high_ref[z, at, :] = high[z]

    over_rows(rows, body)


def x_low_kernel(
    low_ref, below_ref, above_ref, w_two_ref, w_three_ref,
    part_ref, bands_ref, up_ref, down_ref, deep_planes, mark_ref,
    scratch, approx, split, deep_low, deep_split,
):
    planes, rows, width = low_ref.shape
    half = rows // 2
    deep = (rows + 64) // 2
    quarter = half // 2
    eighth = quarter // 2

    def step(z, carry):
        for tile, lanes in enumerate(lane_tiles(width)):
            part = scratch.at[tile]
            part[0:LOW_BELOW] = below_ref[z, 0:LOW_BELOW, lanes]
            part[LOW_BELOW : LOW_BELOW + rows] = low_ref[z, :, lanes]
            top = LOW_BELOW + rows
            part[top : top + LOW_ABOVE] = above_ref[z, 0:LOW_ABOVE, lanes]
            low, high = lift_in_scratch(part, deep)
            approx[z, :, lanes] = low
            part_ref[0, z, :, lanes] = high[16 : 16 + half]
        return carry

    scratch[:, rows + 32 :] = jnp.zeros_like(scratch[:, rows + 32 :])
    lax.fori_loop(0, planes, step, 0)
    whole = exact_dot(approx[...].reshape(planes * deep, width), w_two_ref)
    for tile in range(split.shape[0]):
        split[tile, 0 : planes * deep] = whole[:, tile * LANES : (tile + 1) * LANES]
    span = deep // 2
    for z in range(planes):
        for y in range(2):
            low, high = lift_in_scratch(split.at[y], span, z * deep)
            start = 2 * y * quarter
            bands_ref[z, start : start + quarter, :] = low[8 : 8 + quarter]
            bands_ref[z, start + quarter : start + 2 * quarter, :] = high[8 : 8 + quarter]
            if y == 0:
                deep_low[z] = low
    deep_split[0 : planes * span] = exact_dot(deep_low[...].reshape(planes * span, -1), w_three_ref)
    for z in range(planes):
        low, high = lift_in_scratch(deep_split, span // 2, z * span)
        deep_planes[z, 0:eighth, :] = low[4 : 4 + eighth]
        deep_planes[z, eighth:, :] = high[4 : 4 + eighth]
    packed = bands_ref.shape[1]
    spread_rims(bands_ref, up_ref, down_ref, packed)
    for distance, ref in ((1, up_ref), (-1, down_ref)):
        share = deep_share([deep_planes[z] for z in range(planes)], distance)
        for k in range(2):
            ref[k, packed:, :] = share[k]
    mark(mark_ref)


def own_kernel(deep_ref, own_ref, mark_ref):
    share = deep_share([deep_ref[z] for z in range(deep_ref.shape[0])], 0)
    for k in range(2):
        own_ref[k] = share[k]
    mark(mark_ref)


def far_kernel(deep_ref, keep_ref, give_ref, held):
    planes = [deep_ref[z] for z in range(deep_ref.shape[0])]
    core = lax.rem(lax.axis_index("gx"), 2)
    at = 0
    for distance, count, _ in far_steps(len(planes)):
        for sign, slot in ((1, core), (-1, 1 - core)):
            share = deep_share(planes, sign * distance)
            for k in range(count):
                held[slot, at + k] = share[k]
        at = at + count
    keep_ref[...] = held[0]
    give_ref[...] = held[1]


def pack_kernel(first, keep_ref, got_ref, after_ref, out_ref):
    del after_ref
    for k in range(out_ref.shape[1]):
        out_ref[0, k] = keep_ref[first + k]
        out_ref[1, k] = got_ref[first + k]


def sum_kernel(planes, *refs):
    *far_refs, after_ref, mine_ref, other_ref = refs
    del after_ref
    core = lax.rem(lax.axis_index("gx"), 2)
    for owner, out_ref in enumerate((mine_ref, other_ref)):
        low = jnp.zeros_like(out_ref[0])
        high = jnp.zeros_like(low)
        for ref, (_, count, ratios) in zip(far_refs, far_steps(planes), strict=True):
            part = ref[owner, 0]
            low = low + part
            if count == 1:
                high = high + part * jnp.where(core == 0, *map(jnp.float32, ratios))
            else:
                high = high + ref[owner, 1]
        out_ref[0] = low
        out_ref[1] = high


def x_detail_kernel(
    part_ref, high_ref, below_ref, above_ref, detail_ref, mark_ref, scratch, held, sems
):
    planes, rows, width = high_ref.shape
    half = rows // 2
    copies = [pltpu.make_async_copy(part_ref, detail_ref.at[1:2], sems.at[0])]
    copies[0].start()
    scratch[:, 0:8] = jnp.zeros_like(scratch[:, 0:8])
    scratch[:, rows + 24 :] = jnp.zeros_like(scratch[:, rows + 24 :])

    def step(z, carry):
        for tile, lanes in enumerate(lane_tiles(width)):
            part = scratch.at[tile]
            part[8:16] = below_ref[z, LOW_BELOW : LOW_BELOW + 8, lanes]
            part[16 : 16 + rows] = high_ref[z, :, lanes]
            part[16 + rows : 24 + rows] = above_ref[z, LOW_ABOVE : LOW_ABOVE + 8, lanes]
            low, high = lift_in_scratch(part, half + 16)
            held[0, z, :, lanes] = low[8 : 8 + half]
            held[1, z, :, lanes] = high[8 : 8 + half]
        return carry

    lax.fori_loop(0, planes, step, 0)
    for k in range(2):
        copies.append(
            pltpu.make_async_copy(
                held.at[k : k + 1], detail_ref.at[2 * k : 2 * k + 1], sems.at[1 + k]
            )
        )
        copies[-1].start()
    for copy in copies:
        copy.wait()
    mark(mark_ref)


def z_high_kernel(x_ref, below_ref, above_ref, whole_ref, after_ref, detail_ref, held, sems):
    del whole_ref, after_ref
    planes, rows, _ = x_ref.shape
    half = rows // 2
    copies = []
    for xb in range(2):

        def body(at):
            here = pl.ds(at.start + xb * half, at.size)
            low, high = lift_rows_of(x_ref, below_ref, above_ref, here)
            for z in range(planes // 2):
                held[2 * xb, z, at, :] = low[z]
                held[2 * xb + 1, z, at, :] = high[z]

        over_rows(half, body)
        copies.append(
            pltpu.make_async_copy(
                held.at[pl.ds(2 * xb, 2)], detail_ref.at[pl.ds(3 + 2 * xb, 2)], sems.at[xb]
            )
        )
        copies[-1].start()
    for copy in copies:
        copy.wait()


def z_middle_kernel(
    bands_ref, below_ref, above_ref, own_ref, far_ref, back_ref,
    detail_ref, deep_ref, coarse_ref, low_ref, high_ref,
):
    planes, rows, _ = bands_ref.shape
    kept = planes // 2
    quarter = detail_ref.shape[2]

    def body(at):
        low, high = lift_planes(
            [bands_ref[z, at, :] for z in range(planes)],
            [below_ref[k, at, :] for k in range(2)],
            [above_ref[k, at, :] for k in range(2)],
        )
        for z in range(kept):
            low_ref[z, at, :] = low[z]
            high_ref[z, at, :] = high[z]

    over_rows(rows, body)
    for z in range(kept):
        for band in range(1, 8):
            source = high_ref if band % 2 else low_ref
            start = quarter * (band // 2)
            detail_ref[band - 1, z] = source[z, start : start + quarter, :]
    height, width = coarse_ref.shape[1:]
    shares = (
        own_ref, below_ref.at[:, rows:, :], above_ref.at[:, rows:, :], far_ref, back_ref
    )
    low, high = (
        functools.reduce(jnp.add, [ref[k] for ref in shares])
        for k in range(2)
    )
    coarse_ref[0] = low[0:height, 0:width]
    for band in range(1, 8):
        value = high if band % 2 else low
        xb, yb = (band // 2) % 2, band // 4
        deep_ref[band - 1, 0] = value[
            xb * height : (xb + 1) * height, yb * width : (yb + 1) * width
        ]


def call(
    kernel, out_shapes, inputs, scratch=(), anywhere=(), aliases=None, open_inputs=(), scalars=(), cost=1
):
    whole = pl.BlockSpec(memory_space=pltpu.VMEM)
    unplaced = pl.BlockSpec(memory_space=pl.ANY)
    small = pl.BlockSpec(memory_space=pltpu.SMEM)
    return pl.pallas_call(
        kernel,
        out_shape=[
            jax.ShapeDtypeStruct(s, jnp.float32)
            if isinstance(s, tuple)
            else jax.ShapeDtypeStruct(s.shape, s.dtype)
            for s in out_shapes
        ],
        in_specs=[
            unplaced if i in open_inputs else small if i in scalars else whole
            for i in range(len(inputs))
        ],
        out_specs=[unplaced if i in anywhere else whole for i in range(len(out_shapes))],
        scratch_shapes=list(scratch),
        input_output_aliases=aliases or {},
        cost_estimate=pl.CostEstimate(flops=cost, bytes_accessed=cost, transcendentals=0),
        compiler_params=pltpu.CompilerParams(vmem_limit_bytes=24 * 2**20),
        name=getattr(kernel, "func", kernel).__name__,
    )(*inputs)


def on_device(velocity):
    planes, rows, width = velocity.shape
    half_width = width // 2
    half = rows // 2
    quarter = half // 2
    tiles = half_width // LANES
    f32 = jnp.float32
    matrix = band_matrix(width)
    w_low = jnp.asarray(three_parts(matrix[:, :half_width]))
    w_high = jnp.asarray(three_parts(matrix[:, half_width:]))
    w_two = jnp.asarray(three_parts(band_matrix(half_width)))
    w_three = jnp.asarray(three_parts(band_matrix(half_width // 2)))

    whole = (planes, rows, half_width)
    rims = (2, rows, half_width)
    up, down, held, weights = call(
        rim_kernel,
        [rims, rims, velocity.shape, w_low],
        [
            pltpu.with_memory_space_constraint(velocity, pltpu.HBM),
            pltpu.with_memory_space_constraint(w_low, pltpu.HBM),
        ],
        [
            pltpu.VMEM((4, rows, width), f32),
            pltpu.SemaphoreType.DMA((PARTS + 1,)),
        ],
        open_inputs=(0, 1),
    )
    low_below, low_above = shifted(up, "gz", 1), shifted(down, "gz", -1)

    edge = (planes, 8, half_width)
    y_low, y_high, up, down = call(
        y_kernel, [whole, whole, edge, edge], [held, weights, w_high]
    )
    below, above = shifted(up, "gx", 1), shifted(down, "gx", -1)
    x_high, up, down, mark_high = call(
        x_high_kernel,
        [whole, rims, rims, MARK],
        [y_high, below, above],
        [pltpu.VMEM((tiles, rows + 40, LANES), f32)],
    )
    high_above, high_below = shifted(down, "gz", -1), shifted(up, "gz", 1)

    kept = (planes // 2, rows, half_width)
    up, down, mark_edge = call(
        z_edge_kernel,
        [
            (planes // 2, LOW_BELOW + 8, half_width),
            (planes // 2, LOW_ABOVE + 8, half_width),
            MARK,
        ],
        [y_low, low_below, low_above, mark_high],
    )
    edge_below, edge_above = shifted(up, "gx", 1), shifted(down, "gx", -1)
    z_low, z_high = call(
        z_lift_kernel, [kept, kept], [y_low, low_below, low_above, mark_edge], cost=GAP
    )
    deep = (rows + 64) // 2
    packed = 4 * quarter
    eighth = quarter // 2
    lanes = half_width // 2
    detail_shape = (7, planes // 2, half, half_width)
    middle = (2, packed + 2 * eighth, lanes)
    share = (2, 2 * eighth, lanes)
    steps = far_steps(planes // 2)
    part, bands, up, down, deep_planes, mark_low = call(
        x_low_kernel,
        [
            (1,) + detail_shape[1:],
            (planes // 2, packed, lanes),
            middle,
            middle,
            (planes // 2, 2 * eighth, lanes),
            MARK,
        ],
        [z_low, edge_below, edge_above, w_two, w_three],
        [
            pltpu.VMEM((tiles, rows + 72, LANES), f32),
            pltpu.VMEM((planes // 2, deep, half_width), f32),
            pltpu.VMEM((tiles, planes // 2 * deep + 8, LANES), f32),
            pltpu.VMEM((planes // 2, deep // 2, lanes), f32),
            pltpu.VMEM((planes // 2 * deep // 2 + 8, lanes), f32),
        ],
    )
    detail_one, mark_detail = call(
        x_detail_kernel,
        [detail_shape, MARK],
        [part, z_high, edge_below, edge_above],
        [
            pltpu.VMEM((tiles, rows + 40, LANES), f32),
            pltpu.VMEM((2,) + detail_shape[1:], f32),
            pltpu.SemaphoreType.DMA((3,)),
        ],
        anywhere=(0,),
        cost=GAP_DETAIL,
    )
    below, above = shifted(up, "gz", 1), shifted(down, "gz", -1)
    sent = (sum(count for _, count, _ in steps),) + share[1:]
    keep, give = call(
        far_kernel, [sent, sent], [deep_planes], [pltpu.VMEM((2,) + sent, f32)]
    )
    own, mark_own = call(own_kernel, [share, MARK], [deep_planes], cost=GAP_OWN)
    got = other_core(give)
    both = []
    first = 0
    for distance, count, _ in steps:
        after = mark_own if distance == steps[-1][0] else high_above
        (packed_share,) = call(
            functools.partial(pack_kernel, first), [(2, count) + share[1:]], [keep, got, after]
        )
        both.append(shifted_by_core(packed_share, distance))
        first = first + count
    far, back = call(
        functools.partial(sum_kernel, planes // 2), [share] * 2, [*both, mark_detail]
    )
    back = other_core(back)
    (detail_one,) = call(
        z_high_kernel,
        [detail_shape],
        [x_high, high_below, high_above, detail_one, mark_low],
        [pltpu.VMEM((4,) + detail_shape[1:], f32), pltpu.SemaphoreType.DMA((2,))],
        anywhere=(0,),
        aliases={3: 0},
        open_inputs=(3,),
    )
    last = planes // 4
    detail_two, detail_three, coarse = call(
        z_middle_kernel,
        [
            (7, last, quarter, lanes),
            (7, 1, eighth, lanes // 2),
            (1, eighth, lanes // 2),
        ],
        [bands, below, above, own, far, back],
        [pltpu.VMEM((last, packed, lanes), f32)] * 2,
    )
    return detail_one, detail_two, detail_three, coarse


def solution(mesh):
    placed = (P("gz", "gx", None),)
    return jax.shard_map(
        on_device,
        mesh=mesh,
        in_specs=placed,
        out_specs=(
            P(None, "gz", "gx", None),
            P(None, "gz", "gx", None),
            P(None, "gz", "gx", None),
            P("gz", "gx", None),
        ),
        check_vma=False,
    )
```

```python
import functools

import jax
import jax.numpy as jnp
import numpy as np
from jax import lax
from jax.experimental import pallas as pl
from jax.experimental.pallas import tpu as pltpu
from jax.sharding import PartitionSpec as P

LEVELS = 3
GAP = 1
GAP_OWN = 1
GAP_DETAIL = 1
PLANES = 8
PARTS = 1
MARK = (8, 128)
LANES = 128

LOW_TAPS = (
    0.026748757411,
    -0.016864118443,
    -0.078223266529,
    0.266864118443,
    0.602949018236,
    0.266864118443,
    -0.078223266529,
    -0.016864118443,
    0.026748757411,
)
HIGH_TAPS = (
    0.091271763114,
    -0.057543526229,
    -0.591271763114,
    1.115087052457,
    -0.591271763114,
    -0.057543526229,
    0.091271763114,
)

ALPHA = -1.586134342059924
BETA = -0.052980118572961
GAMMA = 0.882911075530934
DELTA = 0.443506852043971
LOW_SCALE = 0.812893066115961
HIGH_SCALE = 1.230174104914001


def shifted(value, axis, steps):
    count = lax.axis_size(axis)
    pairs = [(source, (source + steps) % count) for source in range(count)]
    return lax.ppermute(value, axis, pairs)


def other_core(value):
    count = lax.axis_size("gx")
    return lax.ppermute(value, "gx", [(source, source ^ 1) for source in range(count)])


def shifted_by_core(value, steps):
    high, wide = lax.axis_size("gz"), lax.axis_size("gx")
    pairs = [
        (z * wide + x, ((z + (-steps if x % 2 else steps)) % high) * wide + x)
        for z in range(high)
        for x in range(wide)
    ]
    return lax.ppermute(value, ("gz", "gx"), pairs)


def band_matrix(length):
    half = length // 2
    matrix = np.zeros((length, length), np.float64)
    for j in range(half):
        for k in range(-4, 5):
            matrix[(2 * j + k) % length, j] += LOW_TAPS[k + 4]
        for k in range(-3, 4):
            matrix[(2 * j + 1 + k) % length, half + j] += HIGH_TAPS[k + 3]
    return matrix


def three_parts(matrix):
    parts = []
    rest = matrix
    for _ in range(3):
        part = rest.astype(np.float32).astype(jnp.bfloat16)
        parts.append(part)
        rest = rest - part.astype(np.float64)
    return np.stack(parts)


def exact_dot(value, parts):
    first = value.astype(jnp.bfloat16)
    rest = value - first.astype(jnp.float32)
    second = rest.astype(jnp.bfloat16)
    third = (rest - second.astype(jnp.float32)).astype(jnp.bfloat16)

    count = value.shape[0]

    def dot(parts_of_value, part):
        rows = jnp.concatenate(parts_of_value, 0)
        result = jnp.dot(rows, part, preferred_element_type=jnp.float32)
        return [result[k * count : (k + 1) * count] for k in range(len(parts_of_value))]

    large, middle, small = dot([first, second, third], parts[0])
    middle_too, small_too = dot([first, second], parts[1])
    (small_last,) = dot([first], parts[2])
    return large + ((middle + middle_too) + (small + small_too + small_last))


def lift_rows(even, odd):
    count = even.shape[0]

    def after(a):
        return pltpu.roll(a, count - 1, 0)

    def before(a):
        return pltpu.roll(a, 1, 0)

    odd = odd + ALPHA * (even + after(even))
    even = even + BETA * (before(odd) + odd)
    odd = odd + GAMMA * (even + after(even))
    even = even + DELTA * (before(odd) + odd)
    return even * LOW_SCALE, odd * HIGH_SCALE


def rim_sums(planes):
    even, odd = planes[0::2], planes[1::2]
    up_odd = odd[-1] + ALPHA * even[-1]
    up_even = even[-1] + BETA * (odd[-2] + ALPHA * (even[-2] + even[-1]))
    down_even = even[0] + BETA * (odd[0] + ALPHA * (even[0] + even[1]))
    return (up_odd, up_even), (even[0], down_even)


def lift_planes(planes, below, above):
    even, odd = planes[0::2], planes[1::2]
    count = len(even)
    first_odd = below[0] + ALPHA * even[0]
    odd = [
        odd[i] + ALPHA * (even[i] + (even[i + 1] if i + 1 < count else above[0]))
        for i in range(count)
    ]
    first_even = below[1] + BETA * first_odd
    even = [
        even[i] + BETA * ((odd[i - 1] if i else first_odd) + odd[i])
        for i in range(count)
    ]
    last_even = above[1] + BETA * odd[-1]
    first_odd = first_odd + GAMMA * (first_even + even[0])
    odd = [
        odd[i] + GAMMA * (even[i] + (even[i + 1] if i + 1 < count else last_even))
        for i in range(count)
    ]
    even = [
        even[i] + DELTA * ((odd[i - 1] if i else first_odd) + odd[i])
        for i in range(count)
    ]
    return [e * LOW_SCALE for e in even], [o * HIGH_SCALE for o in odd]


def double_taps():
    low, high = {}, {}
    for k in range(-4, 5):
        for m in range(-4, 5):
            at = 2 * k + m
            low[at] = low.get(at, 0.0) + LOW_TAPS[k + 4] * LOW_TAPS[m + 4]
    for k in range(-3, 4):
        for m in range(-4, 5):
            at = 2 * (k + 1) + m
            high[at] = high.get(at, 0.0) + HIGH_TAPS[k + 3] * LOW_TAPS[m + 4]
    return low, high


def ring_distances(planes):
    reach = -(-max(double_taps()[0]) // planes)
    return [0] + [sign * step for step in range(1, reach + 1) for sign in (1, -1)]


def deep_share(planes, distance):
    count = len(planes)
    shares = []
    for taps in double_taps():
        terms = [
            planes[z] * taps[z - count * distance]
            for z in range(count)
            if z - count * distance in taps
        ]
        shares.append(functools.reduce(jnp.add, terms) if terms else jnp.zeros_like(planes[0]))
    return shares


def single_plane(planes, distance):
    low, high = (
        [taps.get(z - planes * distance, 0.0) for z in range(planes)] for taps in double_taps()
    )
    if not any(high):
        return 0.0
    if sum(1 for pair in zip(low, high, strict=True) if any(pair)) == 1 and any(low):
        return sum(high) / sum(low)
    return None


def far_steps(planes):
    steps = []
    for distance in range(2, max(ring_distances(planes)) + 1):
        ratios = [single_plane(planes, sign * distance) for sign in (1, -1)]
        steps.append((distance, 2 if None in ratios else 1, ratios))
    return steps


def chunk_of(rows):
    for size in (16, 8):
        if rows % size == 0:
            return size
    return rows


def over_rows(rows, body):
    size = chunk_of(rows)

    def step(i, carry):
        body(pl.ds(pl.multiple_of(i * size, size), size))
        return carry

    lax.fori_loop(0, rows // size, step, 0)


def spread_rims(source, up_ref, down_ref, rows):
    planes = source.shape[0]

    def body(at):
        up, down = rim_sums([source[z, at, :] for z in range(planes)])
        for k in range(2):
            up_ref[k, at, :] = up[k]
            down_ref[k, at, :] = down[k]

    over_rows(rows, body)


def mark(ref):
    ref[...] = jnp.zeros_like(ref)


def rim_kernel(v_ref, w_ref, up_ref, down_ref, held, weights, raw, sems):
    planes, rows, _ = held.shape
    parts = sems.shape[0] - 1
    size = rows // parts
    copies = []
    for part in range(parts):
        at = pl.ds(part * size, size)
        copies.append(pltpu.make_async_copy(v_ref.at[:, at, :], held.at[:, at, :], sems.at[part]))
        copies[-1].start()
    weight_copy = pltpu.make_async_copy(w_ref, weights, sems.at[parts])
    weight_copy.start()
    for part in range(parts):
        copies[part].wait()

        def step(i, carry):
            at = pl.ds(pl.multiple_of(part * size + i * 8, 8), 8)
            up, down = rim_sums([held[z, at, :] for z in range(planes)])
            for k, value in enumerate(up + down):
                raw[k, at, :] = value
            return carry

        lax.fori_loop(0, size // 8, step, 0)
        if part == 0:
            weight_copy.wait()
        at = pl.ds(part * size, size)
        low = exact_dot(raw[:, at, :].reshape(4 * size, -1), weights)
        for k, ref in enumerate((up_ref, up_ref, down_ref, down_ref)):
            ref[k % 2, at, :] = low[k * size : (k + 1) * size]


def y_kernel(v_ref, w_low_ref, w_high_ref, low_ref, high_ref, up_ref, down_ref):
    planes, rows, width = v_ref.shape
    block = PLANES if planes % PLANES == 0 else 1

    def step(i, carry):
        at = pl.ds(i * block, block)
        flat = v_ref[at].reshape(block * rows, width)
        low_ref[at] = exact_dot(flat, w_low_ref).reshape(block, rows, width // 2)
        high = exact_dot(flat, w_high_ref).reshape(block, rows, width // 2)
        high_ref[at] = high
        up_ref[at] = high[:, rows - 8 :]
        down_ref[at] = high[:, :8]
        return carry

    lax.fori_loop(0, planes // block, step, 0)


def lift_in_scratch(scratch, pairs, start=0):
    even = scratch[pl.ds(start, pairs, stride=2), :]
    odd = scratch[pl.ds(start + 1, pairs, stride=2), :]
    return lift_rows(even, odd)


def lane_tiles(width):
    size = min(width, LANES)
    return [pl.ds(k, size) for k in range(0, width, size)]


def x_high_kernel(
    y_ref, below_ref, above_ref, x_ref, up_ref, down_ref, mark_ref, scratch
):
    planes, rows, width = y_ref.shape
    half = rows // 2

    def step(z, carry):
        for tile, lanes in enumerate(lane_tiles(width)):
            part = scratch.at[tile]
            part[8:16] = below_ref[z, :, lanes]
            part[16 : 16 + rows] = y_ref[z, :, lanes]
            part[16 + rows : 24 + rows] = above_ref[z, :, lanes]
            low, high = lift_in_scratch(part, half + 16)
            x_ref[z, 0:half, lanes] = low[8 : 8 + half]
            x_ref[z, half:rows, lanes] = high[8 : 8 + half]
        return carry

    scratch[:, 0:8] = jnp.zeros_like(scratch[:, 0:8])
    scratch[:, 24 + rows :] = jnp.zeros_like(scratch[:, 24 + rows :])
    lax.fori_loop(0, planes, step, 0)
    spread_rims(x_ref, up_ref, down_ref, rows)
    mark(mark_ref)


LOW_BELOW, LOW_ABOVE = 32, 24


def lift_rows_of(y_ref, below_ref, above_ref, at):
    return lift_planes(
        [y_ref[z, at, :] for z in range(y_ref.shape[0])],
        [below_ref[k, at, :] for k in range(2)],
        [above_ref[k, at, :] for k in range(2)],
    )


def z_edge_kernel(y_ref, below_ref, above_ref, after_ref, up_ref, down_ref, mark_ref):
    del after_ref
    planes, rows, _ = y_ref.shape
    size = 8
    for start in range(0, LOW_ABOVE, size):
        low, high = lift_rows_of(y_ref, below_ref, above_ref, slice(start, start + size))
        for z in range(planes // 2):
            down_ref[z, start : start + size] = low[z]
            if start == 0:
                down_ref[z, LOW_ABOVE : LOW_ABOVE + size] = high[z]
    for start in range(0, LOW_BELOW, size):
        at = rows - LOW_BELOW + start
        low, high = lift_rows_of(y_ref, below_ref, above_ref, slice(at, at + size))
        for z in range(planes // 2):
            up_ref[z, start : start + size] = low[z]
            if start == LOW_BELOW - size:
                up_ref[z, LOW_BELOW : LOW_BELOW + size] = high[z]
    mark(mark_ref)


def z_lift_kernel(y_ref, below_ref, above_ref, after_ref, low_ref, high_ref):
    del after_ref
    planes, rows, _ = y_ref.shape

    def body(at):
        low, high = lift_rows_of(y_ref, below_ref, above_ref, at)
        for z in range(planes // 2):
            low_ref[z, at, :] = low[z]
            high_ref[z, at, :] = high[z]

    over_rows(rows, body)


def x_low_kernel(
    low_ref, below_ref, above_ref, w_two_ref, w_three_ref,
    part_ref, bands_ref, up_ref, down_ref, deep_planes, mark_ref,
    scratch, approx, split, deep_low, deep_split, sums,
):
    planes, rows, width = low_ref.shape
    half = rows // 2
    deep = (rows + 64) // 2
    quarter = half // 2
    eighth = quarter // 2

    def step(z, carry):
        for tile, lanes in enumerate(lane_tiles(width)):
            part = scratch.at[tile]
            part[0:LOW_BELOW] = below_ref[z, 0:LOW_BELOW, lanes]
            part[LOW_BELOW : LOW_BELOW + rows] = low_ref[z, :, lanes]
            top = LOW_BELOW + rows
            part[top : top + LOW_ABOVE] = above_ref[z, 0:LOW_ABOVE, lanes]
            low, high = lift_in_scratch(part, deep)
            approx[z, :, lanes] = low
            part_ref[0, z, :, lanes] = high[16 : 16 + half]
        return carry

    scratch[:, rows + 32 :] = jnp.zeros_like(scratch[:, rows + 32 :])
    lax.fori_loop(0, planes, step, 0)
    whole = exact_dot(approx[...].reshape(planes * deep, width), w_two_ref)
    for tile in range(split.shape[0]):
        split[tile, 0 : planes * deep] = whole[:, tile * LANES : (tile + 1) * LANES]
    span = deep // 2
    for z in range(planes):
        for y in range(2):
            low, high = lift_in_scratch(split.at[y], span, z * deep)
            start = 2 * y * quarter
            bands_ref[z, start : start + quarter, :] = low[8 : 8 + quarter]
            bands_ref[z, start + quarter : start + 2 * quarter, :] = high[8 : 8 + quarter]
            if y == 0:
                deep_low[z] = low
    deep_split[0 : planes * span] = exact_dot(deep_low[...].reshape(planes * span, -1), w_three_ref)
    for z in range(planes):
        low, high = lift_in_scratch(deep_split, span // 2, z * span)
        deep_planes[z, 0:eighth, :] = low[4 : 4 + eighth]
        deep_planes[z, eighth:, :] = high[4 : 4 + eighth]
    packed = bands_ref.shape[1]
    spread_rims(bands_ref, sums, down_ref, packed)
    up_ref[0:packed] = sums[0]
    up_ref[packed : 2 * packed - quarter] = sums[1, quarter:, :]
    planes_held = [deep_planes[z] for z in range(planes)]
    up_share, down_share = (deep_share(planes_held, distance) for distance in (1, -1))
    for k in range(2):
        start = 2 * packed - quarter + 2 * eighth * k
        up_ref[start : start + 2 * eighth] = up_share[k]
        down_ref[k, packed:, :] = down_share[k]
    mark(mark_ref)


def own_kernel(deep_ref, own_ref, mark_ref):
    share = deep_share([deep_ref[z] for z in range(deep_ref.shape[0])], 0)
    for k in range(2):
        own_ref[k] = share[k]
    mark(mark_ref)


def far_kernel(deep_ref, keep_ref, give_ref, held):
    planes = [deep_ref[z] for z in range(deep_ref.shape[0])]
    core = lax.rem(lax.axis_index("gx"), 2)
    at = 0
    for distance, count, _ in far_steps(len(planes)):
        for sign, slot in ((1, core), (-1, 1 - core)):
            share = deep_share(planes, sign * distance)
            for k in range(count):
                held[slot, at + k] = share[k]
        at = at + count
    keep_ref[...] = held[0]
    give_ref[...] = held[1]


def pack_kernel(first, keep_ref, got_ref, after_ref, out_ref):
    del after_ref
    for k in range(out_ref.shape[1]):
        out_ref[0, k] = keep_ref[first + k]
        out_ref[1, k] = got_ref[first + k]


def sum_kernel(planes, *refs):
    *far_refs, after_ref, mine_ref, other_ref = refs
    del after_ref
    core = lax.rem(lax.axis_index("gx"), 2)
    for owner, out_ref in enumerate((mine_ref, other_ref)):
        low = jnp.zeros_like(out_ref[0])
        high = jnp.zeros_like(low)
        for ref, (_, count, ratios) in zip(far_refs, far_steps(planes), strict=True):
            part = ref[owner, 0]
            low = low + part
            if count == 1:
                high = high + part * jnp.where(core == 0, *map(jnp.float32, ratios))
            else:
                high = high + ref[owner, 1]
        out_ref[0] = low
        out_ref[1] = high


def x_detail_kernel(
    part_ref, high_ref, below_ref, above_ref, detail_ref, mark_ref, scratch, held, sems
):
    planes, rows, width = high_ref.shape
    half = rows // 2
    copies = [pltpu.make_async_copy(part_ref, detail_ref.at[1:2], sems.at[0])]
    copies[0].start()
    scratch[:, 0:8] = jnp.zeros_like(scratch[:, 0:8])
    scratch[:, rows + 24 :] = jnp.zeros_like(scratch[:, rows + 24 :])

    def step(z, carry):
        for tile, lanes in enumerate(lane_tiles(width)):
            part = scratch.at[tile]
            part[8:16] = below_ref[z, LOW_BELOW : LOW_BELOW + 8, lanes]
            part[16 : 16 + rows] = high_ref[z, :, lanes]
            part[16 + rows : 24 + rows] = above_ref[z, LOW_ABOVE : LOW_ABOVE + 8, lanes]
            low, high = lift_in_scratch(part, half + 16)
            held[0, z, :, lanes] = low[8 : 8 + half]
            held[1, z, :, lanes] = high[8 : 8 + half]
        return carry

    lax.fori_loop(0, planes, step, 0)
    for k in range(2):
        copies.append(
            pltpu.make_async_copy(
                held.at[k : k + 1], detail_ref.at[2 * k : 2 * k + 1], sems.at[1 + k]
            )
        )
        copies[-1].start()
    for copy in copies:
        copy.wait()
    mark(mark_ref)


def z_high_kernel(x_ref, below_ref, above_ref, whole_ref, after_ref, detail_ref, held, sems):
    del whole_ref, after_ref
    planes, rows, _ = x_ref.shape
    half = rows // 2
    copies = []
    for xb in range(2):

        def body(at):
            here = pl.ds(at.start + xb * half, at.size)
            low, high = lift_rows_of(x_ref, below_ref, above_ref, here)
            for z in range(planes // 2):
                held[2 * xb, z, at, :] = low[z]
                held[2 * xb + 1, z, at, :] = high[z]

        over_rows(half, body)
        copies.append(
            pltpu.make_async_copy(
                held.at[pl.ds(2 * xb, 2)], detail_ref.at[pl.ds(3 + 2 * xb, 2)], sems.at[xb]
            )
        )
        copies[-1].start()
    for copy in copies:
        copy.wait()


def z_middle_kernel(
    bands_ref, below_ref, above_ref, own_ref, far_ref, back_ref,
    detail_ref, deep_ref, coarse_ref, low_ref, high_ref,
):
    planes, rows, _ = bands_ref.shape
    kept = planes // 2
    quarter = detail_ref.shape[2]

    def body(at):
        low, high = lift_planes(
            [bands_ref[z, at, :] for z in range(planes)],
            [below_ref[at, :], below_ref[pl.ds(at.start + rows - quarter, at.size), :]],
            [above_ref[k, at, :] for k in range(2)],
        )
        for z in range(kept):
            low_ref[z, at, :] = low[z]
            high_ref[z, at, :] = high[z]

    over_rows(rows, body)
    for z in range(kept):
        for band in range(1, 8):
            source = high_ref if band % 2 else low_ref
            start = quarter * (band // 2)
            detail_ref[band - 1, z] = source[z, start : start + quarter, :]
    height, width = coarse_ref.shape[1:]
    first = 2 * rows - quarter
    shares = (
        own_ref, above_ref.at[:, rows:, :], far_ref, back_ref,
    )
    low, high = (
        functools.reduce(
            jnp.add,
            [ref[k] for ref in shares]
            + [below_ref[first + 2 * height * k : first + 2 * height * (k + 1), :]],
        )
        for k in range(2)
    )
    coarse_ref[0] = low[0:height, 0:width]
    for band in range(1, 8):
        value = high if band % 2 else low
        xb, yb = (band // 2) % 2, band // 4
        deep_ref[band - 1, 0] = value[
            xb * height : (xb + 1) * height, yb * width : (yb + 1) * width
        ]


def call(
    kernel, out_shapes, inputs, scratch=(), anywhere=(), aliases=None, open_inputs=(), scalars=(), cost=1
):
    whole = pl.BlockSpec(memory_space=pltpu.VMEM)
    unplaced = pl.BlockSpec(memory_space=pl.ANY)
    small = pl.BlockSpec(memory_space=pltpu.SMEM)
    return pl.pallas_call(
        kernel,
        out_shape=[
            jax.ShapeDtypeStruct(s, jnp.float32)
            if isinstance(s, tuple)
            else jax.ShapeDtypeStruct(s.shape, s.dtype)
            for s in out_shapes
        ],
        in_specs=[
            unplaced if i in open_inputs else small if i in scalars else whole
            for i in range(len(inputs))
        ],
        out_specs=[unplaced if i in anywhere else whole for i in range(len(out_shapes))],
        scratch_shapes=list(scratch),
        input_output_aliases=aliases or {},
        cost_estimate=pl.CostEstimate(flops=cost, bytes_accessed=cost, transcendentals=0),
        compiler_params=pltpu.CompilerParams(vmem_limit_bytes=24 * 2**20),
        name=getattr(kernel, "func", kernel).__name__,
    )(*inputs)


def on_device(velocity):
    planes, rows, width = velocity.shape
    half_width = width // 2
    half = rows // 2
    quarter = half // 2
    tiles = half_width // LANES
    f32 = jnp.float32
    matrix = band_matrix(width)
    w_low = jnp.asarray(three_parts(matrix[:, :half_width]))
    w_high = jnp.asarray(three_parts(matrix[:, half_width:]))
    w_two = jnp.asarray(three_parts(band_matrix(half_width)))
    w_three = jnp.asarray(three_parts(band_matrix(half_width // 2)))

    whole = (planes, rows, half_width)
    rims = (2, rows, half_width)
    up, down, held, weights = call(
        rim_kernel,
        [rims, rims, velocity.shape, w_low],
        [
            pltpu.with_memory_space_constraint(velocity, pltpu.HBM),
            pltpu.with_memory_space_constraint(w_low, pltpu.HBM),
        ],
        [
            pltpu.VMEM((4, rows, width), f32),
            pltpu.SemaphoreType.DMA((PARTS + 1,)),
        ],
        open_inputs=(0, 1),
    )
    low_below, low_above = shifted(up, "gz", 1), shifted(down, "gz", -1)

    edge = (planes, 8, half_width)
    y_low, y_high, up, down = call(
        y_kernel, [whole, whole, edge, edge], [held, weights, w_high]
    )
    below, above = shifted(up, "gx", 1), shifted(down, "gx", -1)
    x_high, up, down, mark_high = call(
        x_high_kernel,
        [whole, rims, rims, MARK],
        [y_high, below, above],
        [pltpu.VMEM((tiles, rows + 40, LANES), f32)],
    )
    high_above, high_below = shifted(down, "gz", -1), shifted(up, "gz", 1)

    kept = (planes // 2, rows, half_width)
    up, down, mark_edge = call(
        z_edge_kernel,
        [
            (planes // 2, LOW_BELOW + 8, half_width),
            (planes // 2, LOW_ABOVE + 8, half_width),
            MARK,
        ],
        [y_low, low_below, low_above, mark_high],
    )
    edge_below, edge_above = shifted(up, "gx", 1), shifted(down, "gx", -1)
    z_low, z_high = call(
        z_lift_kernel, [kept, kept], [y_low, low_below, low_above, mark_edge], cost=GAP
    )
    deep = (rows + 64) // 2
    packed = 4 * quarter
    eighth = quarter // 2
    lanes = half_width // 2
    detail_shape = (7, planes // 2, half, half_width)
    middle = (2, packed + 2 * eighth, lanes)
    share = (2, 2 * eighth, lanes)
    steps = far_steps(planes // 2)
    part, bands, up, down, deep_planes, mark_low = call(
        x_low_kernel,
        [
            (1,) + detail_shape[1:],
            (planes // 2, packed, lanes),
            (2 * packed - quarter + 4 * eighth, lanes),
            middle,
            (planes // 2, 2 * eighth, lanes),
            MARK,
        ],
        [z_low, edge_below, edge_above, w_two, w_three],
        [
            pltpu.VMEM((tiles, rows + 72, LANES), f32),
            pltpu.VMEM((planes // 2, deep, half_width), f32),
            pltpu.VMEM((tiles, planes // 2 * deep + 8, LANES), f32),
            pltpu.VMEM((planes // 2, deep // 2, lanes), f32),
            pltpu.VMEM((planes // 2 * deep // 2 + 8, lanes), f32),
            pltpu.VMEM((2, packed, lanes), f32),
        ],
    )
    detail_one, mark_detail = call(
        x_detail_kernel,
        [detail_shape, MARK],
        [part, z_high, edge_below, edge_above],
        [
            pltpu.VMEM((tiles, rows + 40, LANES), f32),
            pltpu.VMEM((2,) + detail_shape[1:], f32),
            pltpu.SemaphoreType.DMA((3,)),
        ],
        anywhere=(0,),
        cost=GAP_DETAIL,
    )
    below, above = shifted(up, "gz", 1), shifted(down, "gz", -1)
    sent = (sum(count for _, count, _ in steps),) + share[1:]
    keep, give = call(
        far_kernel, [sent, sent], [deep_planes], [pltpu.VMEM((2,) + sent, f32)]
    )
    own, mark_own = call(own_kernel, [share, MARK], [deep_planes], cost=GAP_OWN)
    got = other_core(give)
    both = []
    first = 0
    for distance, count, _ in steps:
        after = mark_own if distance == steps[-1][0] else high_above
        (packed_share,) = call(
            functools.partial(pack_kernel, first), [(2, count) + share[1:]], [keep, got, after]
        )
        both.append(shifted_by_core(packed_share, distance))
        first = first + count
    far, back = call(
        functools.partial(sum_kernel, planes // 2), [share] * 2, [*both, mark_detail]
    )
    back = other_core(back)
    (detail_one,) = call(
        z_high_kernel,
        [detail_shape],
        [x_high, high_below, high_above, detail_one, mark_low],
        [pltpu.VMEM((4,) + detail_shape[1:], f32), pltpu.SemaphoreType.DMA((2,))],
        anywhere=(0,),
        aliases={3: 0},
        open_inputs=(3,),
    )
    last = planes // 4
    detail_two, detail_three, coarse = call(
        z_middle_kernel,
        [
            (7, last, quarter, lanes),
            (7, 1, eighth, lanes // 2),
            (1, eighth, lanes // 2),
        ],
        [bands, below, above, own, far, back],
        [pltpu.VMEM((last, packed, lanes), f32)] * 2,
    )
    return detail_one, detail_two, detail_three, coarse


def solution(mesh):
    placed = (P("gz", "gx", None),)
    return jax.shard_map(
        on_device,
        mesh=mesh,
        in_specs=placed,
        out_specs=(
            P(None, "gz", "gx", None),
            P(None, "gz", "gx", None),
            P(None, "gz", "gx", None),
            P("gz", "gx", None),
        ),
        check_vma=False,
    )
```

```python
import functools

import jax
import jax.numpy as jnp
import numpy as np
from jax import lax
from jax.experimental import pallas as pl
from jax.experimental.pallas import tpu as pltpu
from jax.sharding import PartitionSpec as P

LEVELS = 3
GAP = 1
GAP_OWN = 1
GAP_DETAIL = 1
PLANES = 8
PARTS = 1
MARK = (8, 128)
LANES = 128

LOW_TAPS = (
    0.026748757411,
    -0.016864118443,
    -0.078223266529,
    0.266864118443,
    0.602949018236,
    0.266864118443,
    -0.078223266529,
    -0.016864118443,
    0.026748757411,
)
HIGH_TAPS = (
    0.091271763114,
    -0.057543526229,
    -0.591271763114,
    1.115087052457,
    -0.591271763114,
    -0.057543526229,
    0.091271763114,
)

ALPHA = -1.586134342059924
BETA = -0.052980118572961
GAMMA = 0.882911075530934
DELTA = 0.443506852043971
LOW_SCALE = 0.812893066115961
HIGH_SCALE = 1.230174104914001


def shifted(value, axis, steps):
    count = lax.axis_size(axis)
    pairs = [(source, (source + steps) % count) for source in range(count)]
    return lax.ppermute(value, axis, pairs)


def other_core(value):
    count = lax.axis_size("gx")
    return lax.ppermute(value, "gx", [(source, source ^ 1) for source in range(count)])


def shifted_by_core(value, steps):
    high, wide = lax.axis_size("gz"), lax.axis_size("gx")
    pairs = [
        (z * wide + x, ((z + (-steps if x % 2 else steps)) % high) * wide + x)
        for z in range(high)
        for x in range(wide)
    ]
    return lax.ppermute(value, ("gz", "gx"), pairs)


def band_matrix(length):
    half = length // 2
    matrix = np.zeros((length, length), np.float64)
    for j in range(half):
        for k in range(-4, 5):
            matrix[(2 * j + k) % length, j] += LOW_TAPS[k + 4]
        for k in range(-3, 4):
            matrix[(2 * j + 1 + k) % length, half + j] += HIGH_TAPS[k + 3]
    return matrix


def three_parts(matrix):
    parts = []
    rest = matrix
    for _ in range(3):
        part = rest.astype(np.float32).astype(jnp.bfloat16)
        parts.append(part)
        rest = rest - part.astype(np.float64)
    return np.stack(parts)


def exact_dot(value, parts):
    first = value.astype(jnp.bfloat16)
    rest = value - first.astype(jnp.float32)
    second = rest.astype(jnp.bfloat16)
    third = (rest - second.astype(jnp.float32)).astype(jnp.bfloat16)

    count = value.shape[0]

    def dot(parts_of_value, part):
        rows = jnp.concatenate(parts_of_value, 0)
        result = jnp.dot(rows, part, preferred_element_type=jnp.float32)
        return [result[k * count : (k + 1) * count] for k in range(len(parts_of_value))]

    large, middle, small = dot([first, second, third], parts[0])
    middle_too, small_too = dot([first, second], parts[1])
    (small_last,) = dot([first], parts[2])
    return large + ((middle + middle_too) + (small + small_too + small_last))


def lift_rows(even, odd):
    count = even.shape[0]

    def after(a):
        return pltpu.roll(a, count - 1, 0)

    def before(a):
        return pltpu.roll(a, 1, 0)

    odd = odd + ALPHA * (even + after(even))
    even = even + BETA * (before(odd) + odd)
    odd = odd + GAMMA * (even + after(even))
    even = even + DELTA * (before(odd) + odd)
    return even * LOW_SCALE, odd * HIGH_SCALE


def rim_sums(planes):
    even, odd = planes[0::2], planes[1::2]
    up_odd = odd[-1] + ALPHA * even[-1]
    up_even = even[-1] + BETA * (odd[-2] + ALPHA * (even[-2] + even[-1]))
    down_even = even[0] + BETA * (odd[0] + ALPHA * (even[0] + even[1]))
    return (up_odd, up_even), (even[0], down_even)


def lift_planes(planes, below, above):
    even, odd = planes[0::2], planes[1::2]
    count = len(even)
    first_odd = below[0] + ALPHA * even[0]
    odd = [
        odd[i] + ALPHA * (even[i] + (even[i + 1] if i + 1 < count else above[0]))
        for i in range(count)
    ]
    first_even = below[1] + BETA * first_odd
    even = [
        even[i] + BETA * ((odd[i - 1] if i else first_odd) + odd[i])
        for i in range(count)
    ]
    last_even = above[1] + BETA * odd[-1]
    first_odd = first_odd + GAMMA * (first_even + even[0])
    odd = [
        odd[i] + GAMMA * (even[i] + (even[i + 1] if i + 1 < count else last_even))
        for i in range(count)
    ]
    even = [
        even[i] + DELTA * ((odd[i - 1] if i else first_odd) + odd[i])
        for i in range(count)
    ]
    return [e * LOW_SCALE for e in even], [o * HIGH_SCALE for o in odd]


def double_taps():
    low, high = {}, {}
    for k in range(-4, 5):
        for m in range(-4, 5):
            at = 2 * k + m
            low[at] = low.get(at, 0.0) + LOW_TAPS[k + 4] * LOW_TAPS[m + 4]
    for k in range(-3, 4):
        for m in range(-4, 5):
            at = 2 * (k + 1) + m
            high[at] = high.get(at, 0.0) + HIGH_TAPS[k + 3] * LOW_TAPS[m + 4]
    return low, high


def ring_distances(planes):
    reach = -(-max(double_taps()[0]) // planes)
    return [0] + [sign * step for step in range(1, reach + 1) for sign in (1, -1)]


def deep_share(planes, distance):
    count = len(planes)
    shares = []
    for taps in double_taps():
        terms = [
            planes[z] * taps[z - count * distance]
            for z in range(count)
            if z - count * distance in taps
        ]
        shares.append(functools.reduce(jnp.add, terms) if terms else jnp.zeros_like(planes[0]))
    return shares


def single_plane(planes, distance):
    low, high = (
        [taps.get(z - planes * distance, 0.0) for z in range(planes)] for taps in double_taps()
    )
    if not any(high):
        return 0.0
    if sum(1 for pair in zip(low, high, strict=True) if any(pair)) == 1 and any(low):
        return sum(high) / sum(low)
    return None


def far_steps(planes):
    steps = []
    for distance in range(2, max(ring_distances(planes)) + 1):
        ratios = [single_plane(planes, sign * distance) for sign in (1, -1)]
        steps.append((distance, 2 if None in ratios else 1, ratios))
    return steps


def chunk_of(rows):
    for size in (16, 8):
        if rows % size == 0:
            return size
    return rows


def over_rows(rows, body):
    size = chunk_of(rows)

    def step(i, carry):
        body(pl.ds(pl.multiple_of(i * size, size), size))
        return carry

    lax.fori_loop(0, rows // size, step, 0)


def spread_rims(source, up_ref, down_ref, rows):
    planes = source.shape[0]

    def body(at):
        up, down = rim_sums([source[z, at, :] for z in range(planes)])
        for k in range(2):
            up_ref[k, at, :] = up[k]
            down_ref[k, at, :] = down[k]

    over_rows(rows, body)


def mark(ref):
    ref[...] = jnp.zeros_like(ref)


def rim_kernel(v_ref, w_ref, up_ref, down_ref, held, weights, raw, sems):
    planes, rows, _ = held.shape
    parts = sems.shape[0] - 1
    size = rows // parts
    copies = []
    for part in range(parts):
        at = pl.ds(part * size, size)
        copies.append(pltpu.make_async_copy(v_ref.at[:, at, :], held.at[:, at, :], sems.at[part]))
        copies[-1].start()
    weight_copy = pltpu.make_async_copy(w_ref, weights, sems.at[parts])
    weight_copy.start()
    for part in range(parts):
        copies[part].wait()

        def step(i, carry):
            at = pl.ds(pl.multiple_of(part * size + i * 8, 8), 8)
            up, down = rim_sums([held[z, at, :] for z in range(planes)])
            for k, value in enumerate(up + down):
                raw[k, at, :] = value
            return carry

        lax.fori_loop(0, size // 8, step, 0)
        if part == 0:
            weight_copy.wait()
        at = pl.ds(part * size, size)
        low = exact_dot(raw[:, at, :].reshape(4 * size, -1), weights)
        for k, ref in enumerate((up_ref, up_ref, down_ref, down_ref)):
            ref[k % 2, at, :] = low[k * size : (k + 1) * size]


def y_kernel(v_ref, w_low_ref, w_high_ref, low_ref, high_ref, up_ref, down_ref):
    planes, rows, width = v_ref.shape
    block = PLANES if planes % PLANES == 0 else 1

    def step(i, carry):
        at = pl.ds(i * block, block)
        flat = v_ref[at].reshape(block * rows, width)
        low_ref[at] = exact_dot(flat, w_low_ref).reshape(block, rows, width // 2)
        high = exact_dot(flat, w_high_ref).reshape(block, rows, width // 2)
        high_ref[at] = high
        up_ref[at] = high[:, rows - 8 :]
        down_ref[at] = high[:, :8]
        return carry

    lax.fori_loop(0, planes // block, step, 0)


def lift_in_scratch(scratch, pairs, start=0):
    even = scratch[pl.ds(start, pairs, stride=2), :]
    odd = scratch[pl.ds(start + 1, pairs, stride=2), :]
    return lift_rows(even, odd)


def lane_tiles(width):
    size = min(width, LANES)
    return [pl.ds(k, size) for k in range(0, width, size)]


def x_high_kernel(
    y_ref, below_ref, above_ref, x_ref, up_ref, down_ref, mark_ref, scratch
):
    planes, rows, width = y_ref.shape
    half = rows // 2

    def step(z, carry):
        for tile, lanes in enumerate(lane_tiles(width)):
            part = scratch.at[tile]
            part[8:16] = below_ref[z, :, lanes]
            part[16 : 16 + rows] = y_ref[z, :, lanes]
            part[16 + rows : 24 + rows] = above_ref[z, :, lanes]
            low, high = lift_in_scratch(part, half + 16)
            x_ref[z, 0:half, lanes] = low[8 : 8 + half]
            x_ref[z, half:rows, lanes] = high[8 : 8 + half]
        return carry

    scratch[:, 0:8] = jnp.zeros_like(scratch[:, 0:8])
    scratch[:, 24 + rows :] = jnp.zeros_like(scratch[:, 24 + rows :])
    lax.fori_loop(0, planes, step, 0)
    spread_rims(x_ref, up_ref, down_ref, rows)
    mark(mark_ref)


LOW_BELOW, LOW_ABOVE = 32, 24


def lift_rows_of(y_ref, below_ref, above_ref, at):
    return lift_planes(
        [y_ref[z, at, :] for z in range(y_ref.shape[0])],
        [below_ref[k, at, :] for k in range(2)],
        [above_ref[k, at, :] for k in range(2)],
    )


def z_edge_kernel(y_ref, below_ref, above_ref, after_ref, up_ref, down_ref, mark_ref):
    del after_ref
    planes, rows, _ = y_ref.shape
    size = 8
    for start in range(0, LOW_ABOVE, size):
        low, high = lift_rows_of(y_ref, below_ref, above_ref, slice(start, start + size))
        for z in range(planes // 2):
            down_ref[z, start : start + size] = low[z]
            if start == 0:
                down_ref[z, LOW_ABOVE : LOW_ABOVE + size] = high[z]
    for start in range(0, LOW_BELOW, size):
        at = rows - LOW_BELOW + start
        low, high = lift_rows_of(y_ref, below_ref, above_ref, slice(at, at + size))
        for z in range(planes // 2):
            up_ref[z, start : start + size] = low[z]
            if start == LOW_BELOW - size:
                up_ref[z, LOW_BELOW : LOW_BELOW + size] = high[z]
    mark(mark_ref)


def z_lift_kernel(y_ref, below_ref, above_ref, after_ref, low_ref, high_ref):
    del after_ref
    planes, rows, _ = y_ref.shape

    def body(at):
        low, high = lift_rows_of(y_ref, below_ref, above_ref, at)
        for z in range(planes // 2):
            low_ref[z, at, :] = low[z]
            high_ref[z, at, :] = high[z]

    over_rows(rows, body)


def x_low_kernel(
    low_ref, below_ref, above_ref, w_two_ref, w_three_ref,
    part_ref, bands_ref, up_ref, down_ref, deep_planes, mark_ref,
    scratch, approx, split, deep_low, deep_split,
):
    planes, rows, width = low_ref.shape
    half = rows // 2
    deep = (rows + 64) // 2
    quarter = half // 2
    eighth = quarter // 2

    def step(z, carry):
        for tile, lanes in enumerate(lane_tiles(width)):
            part = scratch.at[tile]
            part[0:LOW_BELOW] = below_ref[z, 0:LOW_BELOW, lanes]
            part[LOW_BELOW : LOW_BELOW + rows] = low_ref[z, :, lanes]
            top = LOW_BELOW + rows
            part[top : top + LOW_ABOVE] = above_ref[z, 0:LOW_ABOVE, lanes]
            low, high = lift_in_scratch(part, deep)
            approx[z, :, lanes] = low
            part_ref[0, z, :, lanes] = high[16 : 16 + half]
        return carry

    scratch[:, rows + 32 :] = jnp.zeros_like(scratch[:, rows + 32 :])
    lax.fori_loop(0, planes, step, 0)
    whole = exact_dot(approx[...].reshape(planes * deep, width), w_two_ref)
    for tile in range(split.shape[0]):
        split[tile, 0 : planes * deep] = whole[:, tile * LANES : (tile + 1) * LANES]
    span = deep // 2
    for z in range(planes):
        for y in range(2):
            low, high = lift_in_scratch(split.at[y], span, z * deep)
            start = 2 * y * quarter
            bands_ref[z, start : start + quarter, :] = low[8 : 8 + quarter]
            bands_ref[z, start + quarter : start + 2 * quarter, :] = high[8 : 8 + quarter]
            if y == 0:
                deep_low[z] = low
    deep_split[0 : planes * span] = exact_dot(deep_low[...].reshape(planes * span, -1), w_three_ref)
    for z in range(planes):
        low, high = lift_in_scratch(deep_split, span // 2, z * span)
        deep_planes[z, 0:eighth, :] = low[4 : 4 + eighth]
        deep_planes[z, eighth:, :] = high[4 : 4 + eighth]
    packed = bands_ref.shape[1]
    spread_rims(bands_ref, up_ref, down_ref, packed)
    for distance, ref in ((1, up_ref), (-1, down_ref)):
        share = deep_share([deep_planes[z] for z in range(planes)], distance)
        for k in range(2):
            ref[k, packed:, :] = share[k]
    mark(mark_ref)


def own_kernel(deep_ref, own_ref, mark_ref):
    share = deep_share([deep_ref[z] for z in range(deep_ref.shape[0])], 0)
    for k in range(2):
        own_ref[k] = share[k]
    mark(mark_ref)


def far_kernel(deep_ref, keep_ref, give_ref, held):
    planes = [deep_ref[z] for z in range(deep_ref.shape[0])]
    core = lax.rem(lax.axis_index("gx"), 2)
    at = 0
    for distance, count, _ in far_steps(len(planes)):
        for sign, slot in ((1, core), (-1, 1 - core)):
            share = deep_share(planes, sign * distance)
            for k in range(count):
                held[slot, at + k] = share[k]
        at = at + count
    keep_ref[...] = held[0]
    give_ref[...] = held[1]


def pack_kernel(first, keep_ref, got_ref, after_ref, out_ref):
    del after_ref
    for k in range(out_ref.shape[1]):
        out_ref[0, k] = keep_ref[first + k]
        out_ref[1, k] = got_ref[first + k]


def sum_kernel(planes, *refs):
    *far_refs, after_ref, mine_ref, other_ref = refs
    del after_ref
    core = lax.rem(lax.axis_index("gx"), 2)
    for owner, out_ref in enumerate((mine_ref, other_ref)):
        low = jnp.zeros_like(out_ref[0])
        high = jnp.zeros_like(low)
        for ref, (_, count, ratios) in zip(far_refs, far_steps(planes), strict=True):
            part = ref[owner, 0]
            low = low + part
            if count == 1:
                high = high + part * jnp.where(core == 0, *map(jnp.float32, ratios))
            else:
                high = high + ref[owner, 1]
        out_ref[0] = low
        out_ref[1] = high


def x_detail_kernel(
    part_ref, high_ref, below_ref, above_ref, detail_ref, mark_ref, scratch, held, sems
):
    planes, rows, width = high_ref.shape
    half = rows // 2
    copies = [pltpu.make_async_copy(part_ref, detail_ref.at[1:2], sems.at[0])]
    copies[0].start()
    scratch[:, 0:8] = jnp.zeros_like(scratch[:, 0:8])
    scratch[:, rows + 24 :] = jnp.zeros_like(scratch[:, rows + 24 :])

    def step(z, carry):
        for tile, lanes in enumerate(lane_tiles(width)):
            part = scratch.at[tile]
            part[8:16] = below_ref[z, LOW_BELOW : LOW_BELOW + 8, lanes]
            part[16 : 16 + rows] = high_ref[z, :, lanes]
            part[16 + rows : 24 + rows] = above_ref[z, LOW_ABOVE : LOW_ABOVE + 8, lanes]
            low, high = lift_in_scratch(part, half + 16)
            held[0, z, :, lanes] = low[8 : 8 + half]
            held[1, z, :, lanes] = high[8 : 8 + half]
        return carry

    lax.fori_loop(0, planes, step, 0)
    for k in range(2):
        copies.append(
            pltpu.make_async_copy(
                held.at[k : k + 1], detail_ref.at[2 * k : 2 * k + 1], sems.at[1 + k]
            )
        )
        copies[-1].start()
    for copy in copies:
        copy.wait()
    mark(mark_ref)


def z_high_kernel(x_ref, below_ref, above_ref, whole_ref, after_ref, detail_ref, held, sems):
    del whole_ref, after_ref
    planes, rows, _ = x_ref.shape
    half = rows // 2
    copies = []
    for xb in range(2):

        def body(at):
            here = pl.ds(at.start + xb * half, at.size)
            low, high = lift_rows_of(x_ref, below_ref, above_ref, here)
            for z in range(planes // 2):
                held[2 * xb, z, at, :] = low[z]
                held[2 * xb + 1, z, at, :] = high[z]

        over_rows(half, body)
        copies.append(
            pltpu.make_async_copy(
                held.at[pl.ds(2 * xb, 2)], detail_ref.at[pl.ds(3 + 2 * xb, 2)], sems.at[xb]
            )
        )
        copies[-1].start()
    for copy in copies:
        copy.wait()


def z_middle_kernel(
    bands_ref, below_ref, above_ref, own_ref, far_ref, back_ref,
    detail_ref, deep_ref, coarse_ref, low_ref, high_ref,
):
    planes, rows, _ = bands_ref.shape
    kept = planes // 2
    quarter = detail_ref.shape[2]

    def body(at):
        low, high = lift_planes(
            [bands_ref[z, at, :] for z in range(planes)],
            [below_ref[k, at, :] for k in range(2)],
            [above_ref[k, at, :] for k in range(2)],
        )
        for z in range(kept):
            low_ref[z, at, :] = low[z]
            high_ref[z, at, :] = high[z]

    over_rows(rows, body)
    for z in range(kept):
        for band in range(1, 8):
            source = high_ref if band % 2 else low_ref
            start = quarter * (band // 2)
            detail_ref[band - 1, z] = source[z, start : start + quarter, :]
    height, width = coarse_ref.shape[1:]
    shares = (
        own_ref, below_ref.at[:, rows:, :], above_ref.at[:, rows:, :], far_ref, back_ref
    )
    low, high = (
        functools.reduce(jnp.add, [ref[k] for ref in shares])
        for k in range(2)
    )
    coarse_ref[0] = low[0:height, 0:width]
    for band in range(1, 8):
        value = high if band % 2 else low
        xb, yb = (band // 2) % 2, band // 4
        deep_ref[band - 1, 0] = value[
            xb * height : (xb + 1) * height, yb * width : (yb + 1) * width
        ]


def call(
    kernel, out_shapes, inputs, scratch=(), anywhere=(), aliases=None, open_inputs=(), scalars=(), cost=1
):
    whole = pl.BlockSpec(memory_space=pltpu.VMEM)
    unplaced = pl.BlockSpec(memory_space=pl.ANY)
    small = pl.BlockSpec(memory_space=pltpu.SMEM)
    return pl.pallas_call(
        kernel,
        out_shape=[
            jax.ShapeDtypeStruct(s, jnp.float32)
            if isinstance(s, tuple)
            else jax.ShapeDtypeStruct(s.shape, s.dtype)
            for s in out_shapes
        ],
        in_specs=[
            unplaced if i in open_inputs else small if i in scalars else whole
            for i in range(len(inputs))
        ],
        out_specs=[unplaced if i in anywhere else whole for i in range(len(out_shapes))],
        scratch_shapes=list(scratch),
        input_output_aliases=aliases or {},
        cost_estimate=pl.CostEstimate(flops=cost, bytes_accessed=cost, transcendentals=0),
        compiler_params=pltpu.CompilerParams(vmem_limit_bytes=24 * 2**20),
        name=getattr(kernel, "func", kernel).__name__,
    )(*inputs)


def on_device(velocity):
    planes, rows, width = velocity.shape
    half_width = width // 2
    half = rows // 2
    quarter = half // 2
    tiles = half_width // LANES
    f32 = jnp.float32
    matrix = band_matrix(width)
    w_low = jnp.asarray(three_parts(matrix[:, :half_width]))
    w_high = jnp.asarray(three_parts(matrix[:, half_width:]))
    w_two = jnp.asarray(three_parts(band_matrix(half_width)))
    w_three = jnp.asarray(three_parts(band_matrix(half_width // 2)))

    whole = (planes, rows, half_width)
    rims = (2, rows, half_width)
    up, down, held, weights = call(
        rim_kernel,
        [rims, rims, velocity.shape, w_low],
        [
            pltpu.with_memory_space_constraint(velocity, pltpu.HBM),
            pltpu.with_memory_space_constraint(w_low, pltpu.HBM),
        ],
        [
            pltpu.VMEM((4, rows, width), f32),
            pltpu.SemaphoreType.DMA((PARTS + 1,)),
        ],
        open_inputs=(0, 1),
    )
    low_above, low_below = shifted(down, "gz", -1), shifted(up, "gz", 1)

    edge = (planes, 8, half_width)
    y_low, y_high, up, down = call(
        y_kernel, [whole, whole, edge, edge], [held, weights, w_high]
    )
    below, above = shifted(up, "gx", 1), shifted(down, "gx", -1)
    x_high, up, down, mark_high = call(
        x_high_kernel,
        [whole, rims, rims, MARK],
        [y_high, below, above],
        [pltpu.VMEM((tiles, rows + 40, LANES), f32)],
    )
    high_above, high_below = shifted(down, "gz", -1), shifted(up, "gz", 1)

    kept = (planes // 2, rows, half_width)
    up, down, mark_edge = call(
        z_edge_kernel,
        [
            (planes // 2, LOW_BELOW + 8, half_width),
            (planes // 2, LOW_ABOVE + 8, half_width),
            MARK,
        ],
        [y_low, low_below, low_above, mark_high],
    )
    edge_below, edge_above = shifted(up, "gx", 1), shifted(down, "gx", -1)
    z_low, z_high = call(
        z_lift_kernel, [kept, kept], [y_low, low_below, low_above, mark_edge], cost=GAP
    )
    deep = (rows + 64) // 2
    packed = 4 * quarter
    eighth = quarter // 2
    lanes = half_width // 2
    detail_shape = (7, planes // 2, half, half_width)
    middle = (2, packed + 2 * eighth, lanes)
    share = (2, 2 * eighth, lanes)
    steps = far_steps(planes // 2)
    part, bands, up, down, deep_planes, mark_low = call(
        x_low_kernel,
        [
            (1,) + detail_shape[1:],
            (planes // 2, packed, lanes),
            middle,
            middle,
            (planes // 2, 2 * eighth, lanes),
            MARK,
        ],
        [z_low, edge_below, edge_above, w_two, w_three],
        [
            pltpu.VMEM((tiles, rows + 72, LANES), f32),
            pltpu.VMEM((planes // 2, deep, half_width), f32),
            pltpu.VMEM((tiles, planes // 2 * deep + 8, LANES), f32),
            pltpu.VMEM((planes // 2, deep // 2, lanes), f32),
            pltpu.VMEM((planes // 2 * deep // 2 + 8, lanes), f32),
        ],
    )
    detail_one, mark_detail = call(
        x_detail_kernel,
        [detail_shape, MARK],
        [part, z_high, edge_below, edge_above],
        [
            pltpu.VMEM((tiles, rows + 40, LANES), f32),
            pltpu.VMEM((2,) + detail_shape[1:], f32),
            pltpu.SemaphoreType.DMA((3,)),
        ],
        anywhere=(0,),
        cost=GAP_DETAIL,
    )
    above, below = shifted(down, "gz", -1), shifted(up, "gz", 1)
    sent = (sum(count for _, count, _ in steps),) + share[1:]
    keep, give = call(
        far_kernel, [sent, sent], [deep_planes], [pltpu.VMEM((2,) + sent, f32)]
    )
    own, mark_own = call(own_kernel, [share, MARK], [deep_planes], cost=GAP_OWN)
    got = other_core(give)
    both = []
    first = 0
    for distance, count, _ in steps:
        after = mark_own if distance == steps[-1][0] else high_above
        (packed_share,) = call(
            functools.partial(pack_kernel, first), [(2, count) + share[1:]], [keep, got, after]
        )
        both.append(shifted_by_core(packed_share, distance))
        first = first + count
    far, back = call(
        functools.partial(sum_kernel, planes // 2), [share] * 2, [*both, mark_detail]
    )
    back = other_core(back)
    (detail_one,) = call(
        z_high_kernel,
        [detail_shape],
        [x_high, high_below, high_above, detail_one, mark_low],
        [pltpu.VMEM((4,) + detail_shape[1:], f32), pltpu.SemaphoreType.DMA((2,))],
        anywhere=(0,),
        aliases={3: 0},
        open_inputs=(3,),
    )
    last = planes // 4
    detail_two, detail_three, coarse = call(
        z_middle_kernel,
        [
            (7, last, quarter, lanes),
            (7, 1, eighth, lanes // 2),
            (1, eighth, lanes // 2),
        ],
        [bands, below, above, own, far, back],
        [pltpu.VMEM((last, packed, lanes), f32)] * 2,
    )
    return detail_one, detail_two, detail_three, coarse


def solution(mesh):
    placed = (P("gz", "gx", None),)
    return jax.shard_map(
        on_device,
        mesh=mesh,
        in_specs=placed,
        out_specs=(
            P(None, "gz", "gx", None),
            P(None, "gz", "gx", None),
            P(None, "gz", "gx", None),
            P("gz", "gx", None),
        ),
        check_vma=False,
    )
```
